32 devices in a mesh: dp: 8 (over z, y), ctx: 4 (over x, core).
Axes of the slice: x: 2, y: 2, z: 4, core: 2. Of those that a mesh axis runs over, the one named last changes fastest.
Arguments:
- tokens: bfloat16 [2, 4096, 1088], P(None, ('dp', 'ctx')), may hold values from -6 to 6
- cotangent: bfloat16 [2, 4096, 1088], P(None, ('dp', 'ctx')), may hold values from -6 to 6
- w_attn: bfloat16 [1088, 4352], P(None, ('dp', 'ctx'))
- w_up: bfloat16 [1088, 4352], P(None, ('dp', 'ctx')), may hold values from -0.1875 to 0.1875
- w_down: bfloat16 [4352, 1088], P(('dp', 'ctx')), may hold values from -0.09375 to 0.09375
- vectors: bfloat16 [13056], P(('dp', 'ctx'))
- segments: int32 [2, 8, 512], P(None, 'dp'), may hold values from 0 to 511, as said below
Outputs:
- mixed: bfloat16 [2, 4096, 1088], P(None, ('dp', 'ctx'))
- input_grad: bfloat16 [2, 4096, 1088], P(None, ('dp', 'ctx'))
- attn_grad: float32 [1088, 4352], P(None, ('dp', 'ctx'))
- up_grad: float32 [1088, 4352], P(None, ('dp', 'ctx'))
- down_grad: float32 [4352, 1088], P(('dp', 'ctx'))
- vector_grad: float32 [13056], P(('dp', 'ctx'))
The draws below stay inside these ranges and needn't reach their ends.
Inputs may be any that keep to these rules, and one draw needn't show every extreme that they name: `segments`: entries never fall along a group's rows; each equals the row where its sequence starts (the first row of a group starts one; a sequence may be a single row). In every group and micro-batch one sequence has rows on the first and the last of the group's ctx devices.
All inputs are finite; a program needn't handle non-finite values.
Results may differ from the reference program's by a relative error of at most 0.014.
Values may be sent and summed in bfloat16 or wider, within the bound.
No kernel may reach another device: no remote copies, remote signals or barrier semaphores. Data moves between devices by JAX's collectives and lax.ppermute only.
A program may use at most 256 MiB of HBM per device.

```python
import jax
import jax.numpy as jnp
from jax import lax

HEADS = 17
HEAD_DIM = 64
D = 1088
FF = 4352
ROWS_DEV = 128
MICRO = 2
GROUP_ROWS = 512
TOKENS_MB = 4096
N_DP = 8


OUT_GAIN = 4.0


def draw_w_attn(key, part):
    key = jax.random.fold_in(key, 5)
    columns = jnp.arange(4 * D)
    col_scale = jnp.where(columns < 3 * D, 1.0, OUT_GAIN) * D ** (-0.5)
    base = jnp.clip(jax.random.normal(key, (D, 4 * D), jnp.float32), -4.0, 4.0)
    return (base * col_scale[None, :]).astype(jnp.bfloat16)


def draw_vectors(key, part):
    key = jax.random.fold_in(key, 7)
    key_gain, key_bias = jax.random.split(key)
    total = 8 * D + FF
    places = jnp.arange(total)
    is_gain = (places < D) | (places >= 5 * D) & (places < 6 * D)
    gains = jax.random.uniform(key_gain, (total,), jnp.float32, 0.7, 1.3)
    biases = jnp.clip(0.3 * jax.random.normal(key_bias, (total,), jnp.float32), -1.2, 1.2)
    return jnp.where(is_gain, gains, biases).astype(jnp.bfloat16)


def draw_segments(key, part):
    key = jax.random.fold_in(key, 11)
    key_len, key_start, key_pick, key_break = jax.random.split(key, 4)
    groups = MICRO * N_DP
    least = max(GROUP_ROWS - 2 * ROWS_DEV + 2, GROUP_ROWS // 2)
    long_len = jax.random.randint(key_len, (groups,), least, GROUP_ROWS + 1, dtype=jnp.int32)
    start_lo = jnp.maximum(0, GROUP_ROWS - ROWS_DEV - long_len + 1)
    start_hi = jnp.minimum(ROWS_DEV - 1, GROUP_ROWS - long_len)
    long_start = jax.random.randint(key_start, (groups,), start_lo, start_hi + 1, dtype=jnp.int32)
    chosen = jax.random.randint(key_pick, (), 0, groups, dtype=jnp.int32)
    group_ids = jnp.arange(groups, dtype=jnp.int32)
    picked = group_ids == chosen
    closing = group_ids == (chosen + 1) % groups
    long_len = jnp.where(picked, GROUP_ROWS, long_len)
    long_start = jnp.where(picked, 0, long_start)
    long_end = long_start + long_len
    breaks = jax.random.randint(key_break, (groups, GROUP_ROWS), 0, max(4, ROWS_DEV // 4), dtype=jnp.int32) == 0
    positions = jnp.arange(GROUP_ROWS, dtype=jnp.int32)[None, :]
    outside = (positions < long_start[:, None]) | (positions > long_end[:, None])
    last_row = (positions == GROUP_ROWS - 1) & closing[:, None]
    flagged = (positions == 0) | (positions == long_start[:, None]) | (positions == long_end[:, None]) | breaks & outside | last_row
    starts = lax.cummax(jnp.where(flagged, positions, 0), axis=1)
    return starts.reshape(MICRO, N_DP, GROUP_ROWS).astype(jnp.int32)


def block_levels(key, dims, shards, low, top_value):
    def one(axis_at, parts):
        steps = jax.random.uniform(jax.random.fold_in(jax.random.fold_in(key, 6), axis_at), (parts,), jnp.float32, low / len(shards), top_value / len(shards))
        return jnp.repeat(jnp.exp(steps), dims[axis_at] // parts).reshape((-1,) + (1,) * (len(dims) - axis_at - 1))

    factor_of = one(*shards[0])
    for cut in shards[1:]:
        factor_of = factor_of * one(*cut)
    return factor_of


def bell_draw(key, dims, scale, most, cuts=(), kind=jnp.bfloat16):
    array = scale * jax.random.normal(key, dims, jnp.float32)
    if cuts:
        array = array * block_levels(key, dims, cuts, -0.22, 0.18)
    return jnp.clip(array, -most, most).astype(kind)


def setup_inputs(seed: int = 0) -> dict:
    keys = jax.random.split(jax.random.key(seed), 8)
    tokens = bell_draw(keys[0], (MICRO, TOKENS_MB, D), 1.0, 6.0, ((1, 32),))
    cotangent = bell_draw(keys[1], (MICRO, TOKENS_MB, D), 1.0, 6.0, ((1, 32),))
    w_attn = draw_w_attn(jax.random.fold_in(keys[7], 71), 0)
    w_up = bell_draw(keys[3], (D, FF), D ** -0.5, 0.1875, ((1, 32),))
    w_down = bell_draw(keys[4], (FF, D), FF ** -0.5, 0.09375, ((0, 32),))
    vectors = draw_vectors(jax.random.fold_in(keys[7], 71), 0)
    segments = draw_segments(jax.random.fold_in(keys[7], 71), 0)
    return dict(tokens=tokens, cotangent=cotangent, w_attn=w_attn, w_up=w_up, w_down=w_down, vectors=vectors, segments=segments)


HIGHEST = lax.Precision.HIGHEST
NEG_FILL = -1e+30

@jax.custom_vjp
def low(v):
    return lax.optimization_barrier(v.astype(jnp.bfloat16)).astype(jnp.float32)

@jax.custom_vjp
def low_back(v):
    return v

def low_keep(v):
    return (low(v), None)

def low_pass(kept, grad):
    return (grad,)

def back_keep(v):
    return (v, None)

def back_low(kept, grad):
    return (low(grad),)
low.defvjp(low_keep, low_pass)
low_back.defvjp(back_keep, back_low)

def layer_norm(values, gain_vec, bias_vec):
    row_mean = lax.optimization_barrier(jnp.mean(values, axis=-1, keepdims=True))
    centred = values - row_mean
    variance = lax.optimization_barrier(jnp.mean(centred * centred, axis=-1, keepdims=True))
    return centred * lax.rsqrt(variance + 1e-05) * gain_vec + bias_vec

def group_attention(packed):
    queries, key_rows, value_rows, starts = packed
    scores = jnp.einsum('qhd,khd->hqk', queries, key_rows, precision=HIGHEST) * HEAD_DIM ** (-0.5)
    scores = low_back(scores)
    positions = jnp.arange(GROUP_ROWS)
    allowed = (positions[None, :] <= positions[:, None]) & (starts[None, :] == starts[:, None])
    scores = jnp.where(allowed[None], scores, NEG_FILL)
    row_top = lax.optimization_barrier(jnp.max(scores, axis=-1, keepdims=True))
    weights = jnp.where(allowed[None], jnp.exp(scores - row_top), 0.0)
    probs = low(weights / lax.optimization_barrier(jnp.sum(weights, axis=-1, keepdims=True)))
    return jnp.einsum('hqk,khd->qhd', probs, value_rows, precision=HIGHEST)

def forward(tokens, w_attn, w_up, w_down, vectors, segments):
    pieces = [vectors[member * D:(member + 1) * D] for member in range(8)]
    gain_one, bias_one, q_bias, v_bias, out_bias, gain_two, bias_two, down_bias = pieces
    up_bias = vectors[8 * D:]
    flat = tokens.reshape(MICRO * N_DP * GROUP_ROWS, D)
    normed_one = low(layer_norm(flat, gain_one, bias_one))
    qkv_bias = jnp.concatenate([q_bias, jnp.zeros_like(q_bias), v_bias])
    projected = jnp.dot(normed_one, w_attn[:, :3 * D], precision=HIGHEST) + qkv_bias
    projected = low_back(low(projected))
    grouped = projected.reshape(MICRO * N_DP, GROUP_ROWS, 3, HEADS, HEAD_DIM)
    attended = lax.map(jax.checkpoint(group_attention), (grouped[:, :, 0], grouped[:, :, 1], grouped[:, :, 2], segments.reshape(MICRO * N_DP, GROUP_ROWS)))
    heads_out = low_back(low(attended.reshape(MICRO * N_DP * GROUP_ROWS, D)))
    branch = low_back(jnp.dot(heads_out, w_attn[:, 3 * D:].T, precision=HIGHEST) + out_bias)
    middle = flat + branch
    normed_two = low(layer_norm(middle, gain_two, bias_two))
    hidden_pre = low_back(jnp.dot(normed_two, w_up, precision=HIGHEST) + up_bias)
    active = low(jax.nn.gelu(hidden_pre, approximate=True))
    feed = low_back(jnp.dot(active, w_down, precision=HIGHEST) + down_bias)
    return (middle + feed).reshape(tokens.shape)

def reference(tokens, cotangent, w_attn, w_up, w_down, vectors, segments):

    def wrapped(x_val, attn_val, up_val, down_val, vec_val):
        return forward(x_val, attn_val, up_val, down_val, vec_val, segments)
    result, pull_back = jax.vjp(wrapped, tokens.astype(jnp.float32), w_attn.astype(jnp.float32), w_up.astype(jnp.float32), w_down.astype(jnp.float32), vectors.astype(jnp.float32))
    gradients = pull_back(cotangent.astype(jnp.float32))
    return (result.astype(jnp.bfloat16), gradients[0].astype(jnp.bfloat16), gradients[1], gradients[2], gradients[3], gradients[4])
```

```python
import jax
import jax.numpy as jnp
from jax import lax
from jax.sharding import PartitionSpec as P

HEAD_DIM = 64
HALO = 32
NEG_FILL = -1e30
EPSILON = 1e-05
BF = jnp.bfloat16
F32 = jnp.float32
BOTH = ("dp", "ctx")
CORE_PAIRS = [(0, 1), (1, 0), (2, 3), (3, 2)]
CHIP_PAIRS = [(0, 2), (2, 0), (1, 3), (3, 1)]
BLOCKS = (0, 2, 1, 3)
SIDE_PAIRS = [(p, p ^ 1) for p in range(8)]


def shift_pairs(step):
    return [(z * 2 + y, ((z + step) % 4) * 2 + y) for z in range(4) for y in range(2)]


def dot(left, right, left_dim, right_dim):
    return lax.dot_general(
        left, right, (((left_dim,), (right_dim,)), ((), ())), preferred_element_type=F32
    )


def norm_stats(values):
    centred = values - jnp.mean(values, axis=-1, keepdims=True)
    scale = lax.rsqrt(jnp.mean(centred * centred, axis=-1, keepdims=True) + EPSILON)
    return centred * scale, scale


def norm_pull(grad, hat, scale, gain):
    grad_hat = grad * gain
    along = jnp.mean(grad_hat * hat, axis=-1, keepdims=True)
    return scale * (grad_hat - jnp.mean(grad_hat, axis=-1, keepdims=True) - hat * along)


def row_gather(mine):
    across = lax.ppermute(mine, "ctx", CHIP_PAIRS)
    pair = jnp.concatenate([mine, across], axis=1)
    return jnp.concatenate([pair, lax.ppermute(pair, "ctx", CORE_PAIRS)], axis=1)


def row_scatter(partial):
    half = partial.shape[1] // 2
    rows = half // 2
    arrived = lax.ppermute(partial[:, half:].astype(BF), "ctx", CORE_PAIRS)
    other = partial[:, rows:half].astype(F32) + arrived[:, rows:].astype(F32)
    across = lax.ppermute(other.astype(BF), "ctx", CHIP_PAIRS)
    return partial[:, :rows].astype(F32) + arrived[:, :rows].astype(F32) + across.astype(F32)


def block_gather(block):
    near = [block] + [lax.ppermute(block, "dp", shift_pairs(k)) for k in (1, 2, 3)]
    return [b for own in near for b in (own, lax.ppermute(own, "dp", SIDE_PAIRS))]


def block_scatter(blocks):
    total = None
    for k in range(4):
        arrived = lax.ppermute(blocks[2 * k + 1], "dp", SIDE_PAIRS)
        both = blocks[2 * k].astype(F32) + arrived.astype(F32)
        if k:
            back = [(b, a) for a, b in shift_pairs(k)]
            both = lax.ppermute(both.astype(BF), "dp", back).astype(F32)
        total = both if total is None else total + both
    return total


def dp_order(z, y):
    return [((z - k) % 4) * 2 + (y ^ s) for k in range(4) for s in range(2)]


def pick(stacked, index):
    return lax.dynamic_index_in_dim(stacked, index, axis=0, keepdims=False)


def reorder(table, order):
    hot = (order[:, None] == jnp.arange(table.shape[0])[None, :]).astype(F32)
    return jnp.sum(hot[:, :, None] * table[None], axis=1)


def reorder_back(table, order):
    hot = (order[:, None] == jnp.arange(table.shape[0])[None, :]).astype(F32)
    return jnp.sum(hot[:, :, None] * table[:, None, :], axis=0)


def ctx_table(mine, ctx):
    across = lax.ppermute(mine[None], "ctx", CHIP_PAIRS)
    pair = jnp.concatenate([mine[None], across], axis=0)
    table = jnp.concatenate([pair, lax.ppermute(pair, "ctx", CORE_PAIRS)], axis=0)
    return reorder_back(table.astype(F32), jnp.stack([ctx ^ j for j in BLOCKS]))


class Aligned:
    def __init__(self, w_attn):
        self.dp = lax.axis_index("dp")
        self.ctx = lax.axis_index("ctx")
        self.z, self.y = self.dp // 2, self.dp % 2
        self.order = jnp.stack(dp_order(self.z, self.y))
        self.width = w_attn.shape[1]
        self.odd = self.y == 1
        self.last = self.ctx == 3

    def attn_weights(self, w_attn, vectors):
        turned = w_attn.T
        width, model = turned.shape
        pairs = []
        for p in range(8):
            for c in range(4):
                to = (c - 1) % 4 if p % 2 else (c + 1) % 4
                pairs.append((p * 4 + c, p * 4 + to))
        edge = jnp.where(self.odd, turned[:HALO], turned[width - HALO :])
        halo = lax.ppermute(edge, BOTH, pairs)
        none = jnp.zeros_like(halo)
        wide = jnp.concatenate(
            [jnp.where(self.odd, none, halo), turned, jnp.where(self.odd, halo, none)], axis=0
        )
        odd = self.y
        body = lax.dynamic_slice_in_dim(wide, HALO - 8 * self.ctx + HALO * odd, 128, axis=0)
        extra = lax.dynamic_slice_in_dim(wide, width + HALO * odd, HALO, axis=0)
        extra = jnp.where(self.last, extra, jnp.zeros_like(extra))
        table = ctx_table(vectors, self.ctx).astype(BF).reshape(-1)
        lines = jnp.pad(table, (0, 2 * model - table.shape[0])).reshape(2, model)
        lines = jnp.pad(lines, ((0, 14), (0, 0)))
        block = jnp.concatenate([body, extra, lines], axis=0)
        got = jnp.stack(block_gather(block)).reshape(8, 176, model)
        regions, vecs = [], []
        for region in range(4):
            k = (self.z - region) % 4
            first, second = [pick(got, k * 2 + (self.y ^ side)) for side in range(2)]
            regions.append(
                jnp.concatenate(
                    [first[:128], second[:128], first[128:160], second[128:160]], axis=0
                )
            )
            vecs += [first[160:162].reshape(-1), second[160:162].reshape(-1)]
        whole = jnp.concatenate([v[: 4 * vectors.shape[0]] for v in vecs])
        return regions, whole.astype(F32)

    def attn_owned(self, parts):
        sides = []
        for part in parts:
            first = jnp.concatenate([part[:128], part[256:288]], axis=0)
            second = jnp.concatenate([part[128:256], part[288:320]], axis=0)
            sides.append((first, second))
        summed = []
        for first, second in sides:
            away = jnp.where(self.odd, first, second).astype(BF)
            keep = jnp.where(self.odd, second, first).astype(F32)
            summed.append(keep + lax.ppermute(away, "dp", SIDE_PAIRS).astype(F32))
        own = pick(jnp.stack(summed), self.z)
        table = jnp.stack([s.astype(BF) for s in summed])
        for k in (1, 2, 3):
            back = [(b, a) for a, b in shift_pairs(k)]
            own = own + lax.ppermute(pick(table, (self.z - k) % 4), "dp", back).astype(F32)
        pairs = []
        for p in range(8):
            for c in range(4):
                to = (c + 1) % 4 if p % 2 else (c - 1) % 4
                pairs.append((p * 4 + c, p * 4 + to))
        body, extra = own[:128], own[128:]
        tail = jnp.where(self.last, extra, body[128 - HALO :])
        edge = jnp.where(self.odd, tail, body[:HALO])
        halo = lax.ppermute(edge, BOTH, pairs)
        halo = jnp.where(self.last & (self.y == 0), extra, halo)
        wide = jnp.where(
            self.odd,
            jnp.concatenate([halo, body], axis=0),
            jnp.concatenate([body, halo], axis=0),
        )
        start = jnp.where(self.odd, 8 * self.ctx, 8 * self.ctx)
        return lax.dynamic_slice_in_dim(wide, start, self.width, axis=0)

    def mlp_weights(self, w_up, w_down):
        width = self.width
        blocks = block_gather(jnp.concatenate([w_up.T, w_down], axis=0))
        return (
            jnp.concatenate([b[:width] for b in blocks], axis=0),
            jnp.concatenate([b[width:] for b in blocks], axis=0),
        )

    def mlp_owned(self, up_part, down_part):
        width = self.width
        blocks = [
            jnp.concatenate(
                [up_part[i * width : (i + 1) * width], down_part[i * width : (i + 1) * width]],
                axis=0,
            )
            for i in range(8)
        ]
        owned = block_scatter(blocks)
        return owned[:width], owned[width:]

    def vector_owned(self, part):
        each = part.shape[0] // 32
        table = part.reshape(8, 4, each).transpose(1, 0, 2)
        table = jnp.stack([pick(table, self.ctx ^ j) for j in BLOCKS])
        mine = table[:2] + lax.ppermute(table[2:], "ctx", CORE_PAIRS)
        mine = mine[0] + lax.ppermute(mine[1], "ctx", CHIP_PAIRS)
        sides = mine.reshape(4, 2, each).transpose(1, 0, 2)
        mine = pick(sides, self.y) + lax.ppermute(pick(sides, 1 - self.y), "dp", SIDE_PAIRS)
        total = pick(mine, self.z)
        for k in (1, 2, 3):
            back = [(b, a) for a, b in shift_pairs(k)]
            total = total + lax.ppermute(pick(mine, (self.z - k) % 4)[None], "dp", back)[0]
        return total


class Plain:
    def __init__(self, w_attn):
        self.ctx = lax.axis_index("ctx")
        self.order = jnp.arange(lax.axis_size("dp"))
        self.width = w_attn.shape[1]
        self.last = self.ctx == lax.axis_size("ctx") - 1

    def attn_weights(self, w_attn, vectors):
        model = w_attn.shape[0]
        whole = lax.all_gather(w_attn.T, BOTH, axis=0, tiled=True)
        regions = [
            head_rows(whole[r * model : (r + 1) * model], self.ctx, self.last) for r in range(4)
        ]
        return regions, lax.all_gather(vectors, BOTH, axis=0, tiled=True).astype(F32)

    def attn_owned(self, parts):
        whole = jnp.concatenate([head_rows_back(p, self.ctx, self.last) for p in parts], axis=0)
        return lax.psum_scatter(whole.astype(BF), BOTH, scatter_dimension=0, tiled=True).astype(F32)

    def mlp_weights(self, w_up, w_down):
        return (
            lax.all_gather(w_up.T, "dp", axis=0, tiled=True),
            lax.all_gather(w_down, "dp", axis=0, tiled=True),
        )

    def mlp_owned(self, up_part, down_part):
        return tuple(
            lax.psum_scatter(p.astype(BF), "dp", scatter_dimension=0, tiled=True).astype(F32)
            for p in (up_part, down_part)
        )

    def vector_owned(self, part):
        return lax.psum_scatter(part, BOTH, scatter_dimension=0, tiled=True)


def head_rows(table, ctx, last):
    middle = 8 * HEAD_DIM
    first = lax.dynamic_slice_in_dim(table, 128 * ctx, 128, axis=0)
    second = lax.dynamic_slice_in_dim(table, middle + HEAD_DIM + 128 * ctx, 128, axis=0)
    mid = table[middle : middle + HEAD_DIM]
    return jnp.concatenate([first, second, jnp.where(last, mid, jnp.zeros_like(mid))], axis=0)


def head_rows_back(mine, ctx, last):
    middle = 8 * HEAD_DIM
    table = jnp.zeros((2 * middle + HEAD_DIM,) + mine.shape[1:], mine.dtype)
    table = lax.dynamic_update_slice_in_dim(table, mine[:128], 128 * ctx, axis=0)
    table = lax.dynamic_update_slice_in_dim(
        table, mine[128:256], middle + HEAD_DIM + 128 * ctx, axis=0
    )
    mid = jnp.where(last, mine[256:], jnp.zeros_like(mine[256:]))
    return lax.dynamic_update_slice_in_dim(table, mid, middle, axis=0)


def gelu_parts(hidden):
    factor = 0.7978845608028654
    square = hidden * hidden
    bent = jnp.tanh(factor * hidden * (1.0 + 0.044715 * square))
    active = 0.5 * hidden * (1.0 + bent)
    slope = 0.5 * (1.0 + bent) + 0.5 * hidden * (1.0 - bent * bent) * factor * (
        1.0 + 3 * 0.044715 * square
    )
    return active, slope


def split_heads(flat):
    return flat.reshape(flat.shape[:-1] + (flat.shape[-1] // HEAD_DIM, HEAD_DIM))


def masked_scores(queries, keys, allowed):
    scores = jnp.einsum("mqhd,mkhd->mhqk", queries, keys, preferred_element_type=F32)
    return jnp.where(allowed[:, None], scores * HEAD_DIM ** (-0.5), NEG_FILL)


def attend(queries, keys, values, allowed):
    scores = masked_scores(queries, keys, allowed)
    top = jnp.max(scores, axis=-1, keepdims=True)
    weights = jnp.exp(scores - top)
    total = jnp.sum(weights, axis=-1, keepdims=True)
    probs = (weights / total).astype(BF)
    heads = jnp.einsum("mhqk,mkhd->mqhd", probs, values, preferred_element_type=F32)
    return heads, top + jnp.log(total)


def attend_pull(queries, keys, values, allowed, log_total, heads, grad):
    scale = HEAD_DIM ** (-0.5)
    probs = jnp.exp(masked_scores(queries, keys, allowed) - log_total)
    delta = jnp.einsum("mqhd,mqhd->mhq", grad.astype(F32), heads)
    grad_probs = jnp.einsum("mqhd,mkhd->mhqk", grad, values, preferred_element_type=F32)
    grad_scores = (probs * (grad_probs - delta[..., None])).astype(BF)
    dq = scale * jnp.einsum("mhqk,mkhd->mqhd", grad_scores, keys, preferred_element_type=F32)
    dk = scale * jnp.einsum("mhqk,mqhd->mkhd", grad_scores, queries, preferred_element_type=F32)
    dv = jnp.einsum("mhqk,mqhd->mkhd", probs.astype(BF), grad, preferred_element_type=F32)
    return dq, dk, dv


def shards(tokens, cotangent, w_attn, w_up, w_down, vectors, segments):
    micro, rows, model = tokens.shape
    ctx = lax.axis_index("ctx")
    group = rows * 4
    flat = micro * group
    n_dp = lax.axis_size("dp")
    fits = n_dp == 8 and lax.axis_size("ctx") == 4 and w_attn.shape == (1088, 136)
    plan = (Aligned if fits else Plain)(w_attn)

    regions, vec = plan.attn_weights(w_attn, vectors)
    pieces = [vec[i * model : (i + 1) * model] for i in range(8)]
    gain_one, bias_one, q_bias, v_bias, out_bias, gain_two, bias_two, down_bias = pieces
    up_bias = vec[8 * model :].reshape(n_dp, 4, plan.width)
    up_bias = reorder(pick(up_bias.transpose(1, 0, 2), ctx), plan.order).reshape(-1)
    w_qkv = jnp.concatenate(regions[:3], axis=0)
    w_out = regions[3]
    own_width = w_out.shape[0]

    all_tokens = row_gather(tokens).reshape(flat, model)
    all_grads = row_gather(cotangent).reshape(flat, model)
    up, down = plan.mlp_weights(w_up, w_down)

    ranks = [ctx ^ j for j in BLOCKS]
    starts = segments[:, 0].reshape(micro, 4, rows).transpose(1, 0, 2)
    starts = jnp.concatenate([pick(starts, r) for r in ranks], axis=1)
    places = jnp.concatenate([r * rows + jnp.arange(rows) for r in ranks])
    allowed = (places[None, None, :] <= places[None, :, None]) & (
        starts[:, None, :] == starts[:, :, None]
    )

    hat_all, _ = norm_stats(all_tokens.astype(F32))
    normed_one = (hat_all * gain_one + bias_one).astype(BF)
    own_q = head_rows(q_bias[:, None], ctx, plan.last)[:, 0]
    own_v = head_rows(v_bias[:, None], ctx, plan.last)[:, 0]
    qkv_bias = jnp.concatenate([own_q, jnp.zeros_like(own_q), own_v])
    projected = (dot(normed_one, w_qkv, 1, 1) + qkv_bias).astype(BF)
    grouped = projected.reshape(micro, group, 3 * own_width)
    queries, keys, values = [
        split_heads(grouped[..., i * own_width : (i + 1) * own_width]) for i in range(3)
    ]
    heads, log_total = attend(queries, keys, values, allowed)
    heads_out = heads.reshape(flat, own_width).astype(BF)
    branch = dot(heads_out, w_out, 1, 0).reshape(micro, group, model)
    tokens32 = tokens.astype(F32)
    middle = tokens32 + row_scatter(branch) + out_bias

    hat_two, scale_two = norm_stats(middle)
    normed_two = row_gather((hat_two * gain_two + bias_two).astype(BF)).reshape(flat, model)
    hidden = dot(normed_two, up, 1, 1) + up_bias
    active, slope = gelu_parts(hidden)
    active = active.astype(BF)
    grad_hidden = (dot(all_grads, down, 1, 1) * slope).astype(BF)
    back_two = row_scatter(dot(grad_hidden, up, 1, 0).reshape(micro, group, model))
    feed = row_scatter(dot(active, down, 1, 0).reshape(micro, group, model))
    mixed = (middle + feed + down_bias).astype(BF)
    down_part = dot(active, all_grads, 0, 0).astype(BF)
    up_part = dot(grad_hidden, normed_two, 0, 0).astype(BF)
    up_owned, down_owned = plan.mlp_owned(up_part, down_part)
    up_bias_part = jnp.sum(grad_hidden.astype(F32), axis=0)

    grad_out = cotangent.astype(F32)
    grad_middle = grad_out + norm_pull(back_two, hat_two, scale_two, gain_two)
    own_branch = grad_middle.astype(BF)
    grad_branch = row_gather(own_branch).reshape(flat, model)
    out_part = dot(heads_out, grad_branch, 0, 0).astype(BF)
    grad_heads = dot(grad_branch, w_out, 1, 1).astype(BF).reshape(micro, group, own_width)
    pulled = attend_pull(
        queries, keys, values, allowed, log_total, heads, split_heads(grad_heads)
    )
    grad_qkv = jnp.concatenate([g.reshape(flat, own_width) for g in pulled], axis=1).astype(BF)
    back_one = row_scatter(dot(grad_qkv, w_qkv, 1, 0).reshape(micro, group, model))
    qkv_part = dot(grad_qkv, normed_one, 0, 0).astype(BF)
    attn_owned = plan.attn_owned(
        [qkv_part[i * own_width : (i + 1) * own_width] for i in range(3)] + [out_part]
    )
    qkv_bias_part = jnp.sum(grad_qkv.astype(F32), axis=0)

    hat_one, scale_one = norm_stats(tokens32)
    input_grad = (grad_middle + norm_pull(back_one, hat_one, scale_one, gain_one)).astype(BF)

    def row_sum(values):
        return jnp.sum(values, axis=(0, 1))

    def own_bias(part):
        return head_rows_back(part[:, None], ctx, plan.last)[:, 0]

    up_rows = reorder_back(up_bias_part.reshape(n_dp, plan.width), plan.order)
    mine = (jnp.arange(4) == ctx).astype(F32)
    vector_part = jnp.concatenate(
        [
            row_sum(back_one * hat_one),
            row_sum(back_one),
            own_bias(qkv_bias_part[:own_width]),
            own_bias(qkv_bias_part[2 * own_width :]),
            row_sum(own_branch.astype(F32)),
            row_sum(back_two * hat_two),
            row_sum(back_two),
            row_sum(grad_out),
            (up_rows[:, None, :] * mine[None, :, None]).reshape(-1),
        ]
    )
    vector_owned = plan.vector_owned(vector_part)
    return (mixed, input_grad, attn_owned.T, up_owned.T, down_owned, vector_owned)


def solution(mesh):
    return jax.shard_map(
        shards,
        mesh=mesh,
        in_specs=(
            P(None, BOTH, None),
            P(None, BOTH, None),
            P(None, BOTH),
            P(None, BOTH),
            P(BOTH, None),
            P(BOTH),
            P(None, "dp", None),
        ),
        out_specs=(
            P(None, BOTH, None),
            P(None, BOTH, None),
            P(None, BOTH),
            P(None, BOTH),
            P(BOTH, None),
            P(BOTH),
        ),
        check_vma=False,
    )
```

```python
import jax
import jax.numpy as jnp
from jax import lax
from jax.experimental import pallas as pl
from jax.experimental.pallas import tpu as pltpu
from jax.sharding import PartitionSpec as P

HEAD_DIM = 64
HALO = 32
NEG_FILL = -1e30
EPSILON = 1e-05
BF = jnp.bfloat16
F32 = jnp.float32
BOTH = ("dp", "ctx")
CORE_PAIRS = [(0, 1), (1, 0), (2, 3), (3, 2)]
CHIP_PAIRS = [(0, 2), (2, 0), (1, 3), (3, 1)]
BLOCKS = (0, 2, 1, 3)
SIDE_PAIRS = [(p, p ^ 1) for p in range(8)]


def shift_pairs(step):
    return [(z * 2 + y, ((z + step) % 4) * 2 + y) for z in range(4) for y in range(2)]


def dot(left, right, left_dim, right_dim):
    return lax.dot_general(
        left, right, (((left_dim,), (right_dim,)), ((), ())), preferred_element_type=F32
    )


def after(value, *others):
    return lax.optimization_barrier((value,) + others)[0]


def norm_stats(values):
    centred = values - jnp.mean(values, axis=-1, keepdims=True)
    scale = lax.rsqrt(jnp.mean(centred * centred, axis=-1, keepdims=True) + EPSILON)
    return centred * scale, scale


def norm_pull(grad, hat, scale, gain):
    grad_hat = grad * gain
    along = jnp.mean(grad_hat * hat, axis=-1, keepdims=True)
    return scale * (grad_hat - jnp.mean(grad_hat, axis=-1, keepdims=True) - hat * along)


def row_gather(mine):
    across = lax.ppermute(mine, "ctx", CHIP_PAIRS)
    pair = jnp.concatenate([mine, across], axis=1)
    return jnp.concatenate([pair, lax.ppermute(pair, "ctx", CORE_PAIRS)], axis=1)


def row_scatter(keep, send):
    rows = keep.shape[1] // 2
    arrived = lax.ppermute(send, "ctx", CORE_PAIRS)
    other = keep[:, rows:] + arrived[:, rows:].astype(F32)
    across = lax.ppermute(other.astype(BF), "ctx", CHIP_PAIRS)
    return keep[:, :rows] + arrived[:, :rows].astype(F32) + across.astype(F32)


def block_gather(block):
    near = [block] + [lax.ppermute(block, "dp", shift_pairs(k)) for k in (1, 2, 3)]
    return [b for own in near for b in (own, lax.ppermute(own, "dp", SIDE_PAIRS))]


def block_scatter(blocks):
    total = None
    for k in range(4):
        arrived = lax.ppermute(blocks[2 * k + 1], "dp", SIDE_PAIRS)
        both = blocks[2 * k].astype(F32) + arrived.astype(F32)
        if k:
            back = [(b, a) for a, b in shift_pairs(k)]
            both = lax.ppermute(both.astype(BF), "dp", back).astype(F32)
        total = both if total is None else total + both
    return total


def dp_order(z, y):
    return [((z - k) % 4) * 2 + (y ^ s) for k in range(4) for s in range(2)]


def pick(stacked, index):
    return lax.dynamic_index_in_dim(stacked, index, axis=0, keepdims=False)


def reorder(table, order):
    hot = (order[:, None] == jnp.arange(table.shape[0])[None, :]).astype(F32)
    return jnp.sum(hot[:, :, None] * table[None], axis=1)


def reorder_back(table, order):
    hot = (order[:, None] == jnp.arange(table.shape[0])[None, :]).astype(F32)
    return jnp.sum(hot[:, :, None] * table[:, None, :], axis=0)


def ctx_table(mine, ctx):
    across = lax.ppermute(mine[None], "ctx", CHIP_PAIRS)
    pair = jnp.concatenate([mine[None], across], axis=0)
    table = jnp.concatenate([pair, lax.ppermute(pair, "ctx", CORE_PAIRS)], axis=0)
    return reorder_back(table.astype(F32), jnp.stack([ctx ^ j for j in BLOCKS]))


class Aligned:
    def __init__(self, w_attn):
        self.dp = lax.axis_index("dp")
        self.ctx = lax.axis_index("ctx")
        self.z, self.y = self.dp // 2, self.dp % 2
        self.order = jnp.stack(dp_order(self.z, self.y))
        self.width = w_attn.shape[1]
        self.odd = self.y == 1
        self.last = self.ctx == 3

    def attn_weights(self, w_attn, vectors):
        turned = w_attn.T
        width, model = turned.shape
        pairs = []
        for p in range(8):
            for c in range(4):
                to = (c - 1) % 4 if p % 2 else (c + 1) % 4
                pairs.append((p * 4 + c, p * 4 + to))
        edge = jnp.where(self.odd, turned[:HALO], turned[width - HALO :])
        halo = lax.ppermute(edge, BOTH, pairs)
        none = jnp.zeros_like(halo)
        wide = jnp.concatenate(
            [jnp.where(self.odd, none, halo), turned, jnp.where(self.odd, halo, none)], axis=0
        )
        odd = self.y
        body = lax.dynamic_slice_in_dim(wide, HALO - 8 * self.ctx + HALO * odd, 128, axis=0)
        extra = lax.dynamic_slice_in_dim(wide, width + HALO * odd, HALO, axis=0)
        extra = jnp.where(self.last, extra, jnp.zeros_like(extra))
        table = ctx_table(vectors, self.ctx).astype(BF).reshape(-1)
        lines = jnp.pad(table, (0, 2 * model - table.shape[0])).reshape(2, model)
        lines = jnp.pad(lines, ((0, 14), (0, 0)))
        block = jnp.concatenate([body, extra, lines], axis=0)
        blocks = block_gather(block)
        self.near = blocks[2::2]
        got = jnp.stack(blocks)
        regions, vecs = [], []
        for region in range(4):
            k = (self.z - region) % 4
            first, second = [pick(got, k * 2 + (self.y ^ side)) for side in range(2)]
            regions.append(
                jnp.concatenate(
                    [first[:128], second[:128], first[128:160], second[128:160]], axis=0
                )
            )
            vecs += [first[160:162].reshape(-1), second[160:162].reshape(-1)]
        whole = jnp.concatenate([v[: 4 * vectors.shape[0]] for v in vecs])
        return regions, whole.astype(F32)

    def attn_owned(self, parts):
        sides = []
        for part in parts:
            first = jnp.concatenate([part[:128], part[256:288]], axis=0)
            second = jnp.concatenate([part[128:256], part[288:320]], axis=0)
            sides.append((first, second))
        summed = []
        for first, second in sides:
            away = jnp.where(self.odd, first, second).astype(BF)
            keep = jnp.where(self.odd, second, first).astype(F32)
            summed.append(keep + lax.ppermute(away, "dp", SIDE_PAIRS).astype(F32))
        own = pick(jnp.stack(summed), self.z)
        table = jnp.stack([s.astype(BF) for s in summed])
        for k in (1, 2, 3):
            back = [(b, a) for a, b in shift_pairs(k)]
            own = own + lax.ppermute(pick(table, (self.z - k) % 4), "dp", back).astype(F32)
        pairs = []
        for p in range(8):
            for c in range(4):
                to = (c + 1) % 4 if p % 2 else (c - 1) % 4
                pairs.append((p * 4 + c, p * 4 + to))
        body, extra = own[:128], own[128:]
        tail = jnp.where(self.last, extra, body[128 - HALO :])
        edge = jnp.where(self.odd, tail, body[:HALO])
        halo = lax.ppermute(edge, BOTH, pairs)
        halo = jnp.where(self.last & (self.y == 0), extra, halo)
        wide = jnp.where(
            self.odd,
            jnp.concatenate([halo, body], axis=0),
            jnp.concatenate([body, halo], axis=0),
        )
        start = jnp.where(self.odd, 8 * self.ctx, 8 * self.ctx)
        return lax.dynamic_slice_in_dim(wide, start, self.width, axis=0)

    def mlp_weights(self, w_up, w_down):
        width = self.width
        block = after(jnp.concatenate([w_up.T, w_down], axis=0), *self.near)
        blocks = block_gather(block)
        return (
            jnp.concatenate([b[:width] for b in blocks], axis=0),
            jnp.concatenate([b[width:] for b in blocks], axis=0),
        )

    def mlp_owned(self, up_part, down_part):
        width = self.width
        blocks = [
            jnp.concatenate(
                [up_part[i * width : (i + 1) * width], down_part[i * width : (i + 1) * width]],
                axis=0,
            )
            for i in range(8)
        ]
        owned = block_scatter(blocks)
        return owned[:width], owned[width:]

    def vector_owned(self, part):
        each = part.shape[0] // 32
        table = part.reshape(8, 4, each).transpose(1, 0, 2)
        table = jnp.stack([pick(table, self.ctx ^ j) for j in BLOCKS])
        mine = table[:2] + lax.ppermute(table[2:], "ctx", CORE_PAIRS)
        mine = mine[0] + lax.ppermute(mine[1], "ctx", CHIP_PAIRS)
        sides = mine.reshape(4, 2, each).transpose(1, 0, 2)
        mine = pick(sides, self.y) + lax.ppermute(pick(sides, 1 - self.y), "dp", SIDE_PAIRS)
        total = pick(mine, self.z)
        for k in (1, 2, 3):
            back = [(b, a) for a, b in shift_pairs(k)]
            total = total + lax.ppermute(pick(mine, (self.z - k) % 4)[None], "dp", back)[0]
        return total


class Plain:
    def __init__(self, w_attn):
        self.ctx = lax.axis_index("ctx")
        self.order = jnp.arange(lax.axis_size("dp"))
        self.width = w_attn.shape[1]
        self.last = self.ctx == lax.axis_size("ctx") - 1

    def attn_weights(self, w_attn, vectors):
        model = w_attn.shape[0]
        whole = lax.all_gather(w_attn.T, BOTH, axis=0, tiled=True)
        regions = [
            head_rows(whole[r * model : (r + 1) * model], self.ctx, self.last) for r in range(4)
        ]
        return regions, lax.all_gather(vectors, BOTH, axis=0, tiled=True).astype(F32)

    def attn_owned(self, parts):
        whole = jnp.concatenate([head_rows_back(p, self.ctx, self.last) for p in parts], axis=0)
        return lax.psum_scatter(whole.astype(BF), BOTH, scatter_dimension=0, tiled=True).astype(F32)

    def mlp_weights(self, w_up, w_down):
        return (
            lax.all_gather(w_up.T, "dp", axis=0, tiled=True),
            lax.all_gather(w_down, "dp", axis=0, tiled=True),
        )

    def mlp_owned(self, up_part, down_part):
        return tuple(
            lax.psum_scatter(p.astype(BF), "dp", scatter_dimension=0, tiled=True).astype(F32)
            for p in (up_part, down_part)
        )

    def vector_owned(self, part):
        return lax.psum_scatter(part, BOTH, scatter_dimension=0, tiled=True)


def head_rows(table, ctx, last):
    middle = 8 * HEAD_DIM
    first = lax.dynamic_slice_in_dim(table, 128 * ctx, 128, axis=0)
    second = lax.dynamic_slice_in_dim(table, middle + HEAD_DIM + 128 * ctx, 128, axis=0)
    mid = table[middle : middle + HEAD_DIM]
    return jnp.concatenate([first, second, jnp.where(last, mid, jnp.zeros_like(mid))], axis=0)


def head_rows_back(mine, ctx, last):
    middle = 8 * HEAD_DIM
    table = jnp.zeros((2 * middle + HEAD_DIM,) + mine.shape[1:], mine.dtype)
    table = lax.dynamic_update_slice_in_dim(table, mine[:128], 128 * ctx, axis=0)
    table = lax.dynamic_update_slice_in_dim(
        table, mine[128:256], middle + HEAD_DIM + 128 * ctx, axis=0
    )
    mid = jnp.where(last, mine[256:], jnp.zeros_like(mine[256:]))
    return lax.dynamic_update_slice_in_dim(table, mid, middle, axis=0)


def gelu_parts(hidden):
    factor = 0.7978845608028654
    square = hidden * hidden
    bent = jnp.tanh(factor * hidden * (1.0 + 0.044715 * square))
    active = 0.5 * hidden * (1.0 + bent)
    slope = 0.5 * (1.0 + bent) + 0.5 * hidden * (1.0 - bent * bent) * factor * (
        1.0 + 3 * 0.044715 * square
    )
    return active, slope


def full(shape):
    return pl.BlockSpec(shape, lambda *_: (0,) * len(shape))


def per(shape, step=1):
    return pl.BlockSpec((1,) + shape, lambda i: (i // step,) + (0,) * len(shape))


def params(mib):
    return pltpu.CompilerParams(vmem_limit_bytes=mib * 1024 * 1024)


def attend_kernel(
    x_ref, gain_ref, bias_ref, w_qkv_ref, qkv_bias_ref, w_out_ref, col_ref, row_ref,
    normed_ref, qkv_ref, probs_ref, heads_ref, keep_ref, send_ref, mask_ref,
):
    count = probs_ref.shape[1]
    width = count * HEAD_DIM
    half = keep_ref.shape[1]
    hat, _ = norm_stats(x_ref[0].astype(F32))
    normed = (hat * gain_ref[...] + bias_ref[...]).astype(BF)
    normed_ref[0] = normed
    qkv_ref[0] = (dot(normed, w_qkv_ref[...], 1, 1) + qkv_bias_ref[...]).astype(BF)
    col, row = col_ref[0], row_ref[0]
    allowed = (row[1:2, :] <= col[:, 1:2]) & (row[0:1, :] == col[:, 0:1])
    mask_ref[...] = jnp.where(allowed, 0.0, NEG_FILL)
    for head in range(count):
        lanes = slice(head * HEAD_DIM, (head + 1) * HEAD_DIM)
        queries = qkv_ref[0, :, lanes] * jnp.asarray(HEAD_DIM ** (-0.5), BF)
        keys = qkv_ref[0, :, width + head * HEAD_DIM : width + (head + 1) * HEAD_DIM]
        values = qkv_ref[0, :, 2 * width + head * HEAD_DIM : 2 * width + (head + 1) * HEAD_DIM]
        scores = dot(queries, keys, 1, 1) + mask_ref[...]
        weights = jnp.exp(scores - jnp.max(scores, axis=1, keepdims=True))
        probs = (weights * (1.0 / jnp.sum(weights, axis=1, keepdims=True))).astype(BF)
        probs_ref[0, head] = probs
        heads_ref[0, :, lanes] = dot(probs, values, 1, 0).astype(BF)
    branch = dot(heads_ref[0], w_out_ref[...], 1, 0)
    keep_ref[0] = branch[:half]
    send_ref[0] = branch[half:].astype(BF)


def attend(x, gain, bias, w_qkv, qkv_bias, w_out, col, row):
    micro, rows, model = x.shape
    width = w_out.shape[0]
    count = width // HEAD_DIM
    half = rows // 2
    shape = jax.ShapeDtypeStruct
    return pl.pallas_call(
        attend_kernel,
        grid=(micro,),
        in_specs=[
            per((rows, model)), full((1, model)), full((1, model)), full(w_qkv.shape),
            full(qkv_bias.shape), full(w_out.shape), per(col.shape[1:]), per(row.shape[1:]),
        ],
        out_specs=[
            per((rows, model)), per((rows, 3 * width)), per((count, rows, rows)),
            per((rows, width)), per((half, model)), per((half, model)),
        ],
        out_shape=[
            shape((micro, rows, model), BF), shape((micro, rows, 3 * width), BF),
            shape((micro, count, rows, rows), BF), shape((micro, rows, width), BF),
            shape((micro, half, model), F32), shape((micro, half, model), BF),
        ],
        scratch_shapes=[pltpu.VMEM((rows, rows), F32)],
        compiler_params=params(56),
        cost_estimate=pl.CostEstimate(
            flops=2 * micro * rows * model * 4 * width,
            bytes_accessed=12 * micro * rows * model,
            transcendentals=micro * count * rows * rows,
        ),
        name="attend",
    )(x, gain, bias, w_qkv, qkv_bias, w_out, col, row)


def attend_pull_kernel(
    grad_ref, w_out_ref, w_qkv_ref, qkv_ref, probs_ref, heads_ref,
    grad_qkv_ref, keep_ref, send_ref,
):
    count = probs_ref.shape[1]
    width = count * HEAD_DIM
    half = keep_ref.shape[1]
    scale = HEAD_DIM ** (-0.5)
    grad_heads = dot(grad_ref[0], w_out_ref[...], 1, 1).astype(BF)
    for head in range(count):
        lanes = [slice(i * width + head * HEAD_DIM, i * width + (head + 1) * HEAD_DIM) for i in range(3)]
        queries, keys, values = [qkv_ref[0, :, part] for part in lanes]
        probs = probs_ref[0, head]
        grad = grad_heads[:, lanes[0]]
        delta = jnp.sum(
            grad.astype(F32) * heads_ref[0, :, lanes[0]].astype(F32), axis=1, keepdims=True
        )
        grad_scores = (probs.astype(F32) * (dot(grad, values, 1, 1) - delta)).astype(BF)
        grad_qkv_ref[0, :, lanes[0]] = (scale * dot(grad_scores, keys, 1, 0)).astype(BF)
        grad_qkv_ref[0, :, lanes[1]] = (scale * dot(grad_scores, queries, 0, 0)).astype(BF)
        grad_qkv_ref[0, :, lanes[2]] = dot(probs, grad, 0, 0).astype(BF)
    back = dot(grad_qkv_ref[0], w_qkv_ref[...], 1, 0)
    keep_ref[0] = back[:half]
    send_ref[0] = back[half:].astype(BF)


def attend_pull(grad, w_out, w_qkv, qkv, probs, heads):
    micro, rows, model = grad.shape
    width = w_out.shape[0]
    count = width // HEAD_DIM
    half = rows // 2
    shape = jax.ShapeDtypeStruct
    return pl.pallas_call(
        attend_pull_kernel,
        grid=(micro,),
        in_specs=[
            per((rows, model)), full(w_out.shape), full(w_qkv.shape), per((rows, 3 * width)),
            per((count, rows, rows)), per((rows, width)),
        ],
        out_specs=[per((rows, 3 * width)), per((half, model)), per((half, model))],
        out_shape=[
            shape((micro, rows, 3 * width), BF),
            shape((micro, half, model), F32), shape((micro, half, model), BF),
        ],
        compiler_params=params(56),
        cost_estimate=pl.CostEstimate(
            flops=2 * micro * rows * model * 6 * width,
            bytes_accessed=12 * micro * rows * model,
            transcendentals=0,
        ),
        name="attend_pull",
    )(grad, w_out, w_qkv, qkv, probs, heads)


def feed_kernel(
    x_ref, grad_ref, up_ref, down_ref, bias_ref,
    active_ref, grad_hidden_ref, feed_keep_ref, feed_send_ref, back_keep_ref, back_send_ref, sum_ref,
):
    step = pl.program_id(0)
    active, slope = gelu_parts(dot(x_ref[0], up_ref[...], 1, 1) + bias_ref[...])
    active = active.astype(BF)
    active_ref[0] = active
    grad_hidden = (dot(grad_ref[0], down_ref[...], 1, 1) * slope).astype(BF)
    grad_hidden_ref[0] = grad_hidden
    sums = jnp.sum(grad_hidden.astype(F32), axis=0, keepdims=True)
    back = dot(grad_hidden, up_ref[...], 1, 0)
    feed = dot(active, down_ref[...], 1, 0)

    @pl.when(step == 0)
    def _():
        sum_ref[...] = sums

    @pl.when(step > 0)
    def _():
        sum_ref[...] += sums

    @pl.when(step % 2 == 0)
    def _():
        feed_keep_ref[0] = feed
        back_keep_ref[0] = back

    @pl.when(step % 2 == 1)
    def _():
        feed_send_ref[0] = feed.astype(BF)
        back_send_ref[0] = back.astype(BF)


def feed_forward(x, grad, up, down, bias):
    steps, half, model = x.shape
    hidden = up.shape[0]
    shape = jax.ShapeDtypeStruct
    kept = shape((steps // 2, half, model), F32)
    sent = shape((steps // 2, half, model), BF)
    return pl.pallas_call(
        feed_kernel,
        grid=(steps,),
        in_specs=[
            per((half, model)), per((half, model)), full(up.shape), full(down.shape),
            full(bias.shape),
        ],
        out_specs=[per((half, hidden))] * 2 + [per((half, model), 2)] * 4 + [full((1, hidden))],
        out_shape=[shape((steps, half, hidden), BF)] * 2
        + [kept, sent, kept, sent, shape((1, hidden), F32)],
        compiler_params=params(56),
        cost_estimate=pl.CostEstimate(
            flops=8 * steps * half * model * hidden,
            bytes_accessed=16 * steps * half * model,
            transcendentals=steps * half * hidden,
        ),
        name="feed_forward",
    )(x, grad, up, down, bias)


def shards(tokens, cotangent, w_attn, w_up, w_down, vectors, segments):
    micro, rows, model = tokens.shape
    ctx = lax.axis_index("ctx")
    group = rows * 4
    flat = micro * group
    n_dp = lax.axis_size("dp")
    fits = n_dp == 8 and lax.axis_size("ctx") == 4 and w_attn.shape == (1088, 136)
    plan = (Aligned if fits else Plain)(w_attn)

    regions, vec = plan.attn_weights(w_attn, vectors)
    pieces = [vec[i * model : (i + 1) * model] for i in range(8)]
    gain_one, bias_one, q_bias, v_bias, out_bias, gain_two, bias_two, down_bias = pieces
    up_bias = vec[8 * model :].reshape(n_dp, 4, plan.width)
    up_bias = reorder(pick(up_bias.transpose(1, 0, 2), ctx), plan.order).reshape(-1)
    w_qkv = jnp.concatenate(regions[:3], axis=0)
    w_out = regions[3]
    own_width = w_out.shape[0]

    all_tokens = row_gather(tokens)
    all_grads = row_gather(after(cotangent, all_tokens))
    up, down = plan.mlp_weights(w_up, w_down)

    ranks = [ctx ^ j for j in BLOCKS]
    starts = segments[:, 0].reshape(micro, 4, rows).transpose(1, 0, 2)
    starts = jnp.concatenate([pick(starts, r) for r in ranks], axis=1)
    places = jnp.concatenate([r * rows + jnp.arange(rows, dtype=jnp.int32) for r in ranks])
    places = jnp.broadcast_to(places[None], starts.shape)
    row_info = jnp.stack([starts, places] + [places] * 6, axis=1)
    col_info = row_info.transpose(0, 2, 1)

    own_q = head_rows(q_bias[:, None], ctx, plan.last)[:, 0]
    own_v = head_rows(v_bias[:, None], ctx, plan.last)[:, 0]
    qkv_bias = jnp.concatenate([own_q, jnp.zeros_like(own_q), own_v])
    normed_one, qkv, probs, heads, keep, send = attend(
        all_tokens, gain_one[None], bias_one[None], w_qkv, qkv_bias[None], w_out, col_info, row_info
    )
    tokens32 = tokens.astype(F32)
    middle = tokens32 + row_scatter(keep, send) + out_bias

    hat_two, scale_two = norm_stats(middle)
    normed_two = row_gather((hat_two * gain_two + bias_two).astype(BF))
    halves = (2 * micro, group // 2, model)
    active, grad_hidden, feed_keep, feed_send, back_keep, back_send, up_bias_part = feed_forward(
        normed_two.reshape(halves), all_grads.reshape(halves), up, down, up_bias[None]
    )
    back_two = row_scatter(back_keep, back_send)
    feed = row_scatter(feed_keep, feed_send)
    mixed = (middle + feed + down_bias).astype(BF)

    def rows_of(values):
        return values.reshape(flat, values.shape[-1])

    down_part = dot(rows_of(active), rows_of(all_grads), 0, 0).astype(BF)
    up_part = dot(rows_of(grad_hidden), rows_of(normed_two), 0, 0).astype(BF)
    up_owned, down_owned = plan.mlp_owned(up_part, down_part)

    grad_out = cotangent.astype(F32)
    grad_middle = grad_out + norm_pull(back_two, hat_two, scale_two, gain_two)
    own_branch = grad_middle.astype(BF)
    grad_branch = row_gather(own_branch)
    out_part = dot(rows_of(heads), rows_of(grad_branch), 0, 0).astype(BF)
    grad_qkv, keep, send = attend_pull(grad_branch, w_out, w_qkv, qkv, probs, heads)
    back_one = row_scatter(keep, send)
    grad_qkv = rows_of(grad_qkv)
    qkv_part = dot(grad_qkv, rows_of(normed_one), 0, 0).astype(BF)
    attn_owned = plan.attn_owned(
        [qkv_part[i * own_width : (i + 1) * own_width] for i in range(3)] + [out_part]
    )
    qkv_bias_part = jnp.sum(grad_qkv.astype(F32), axis=0)

    hat_one, scale_one = norm_stats(tokens32)
    input_grad = (grad_middle + norm_pull(back_one, hat_one, scale_one, gain_one)).astype(BF)

    def row_sum(values):
        return jnp.sum(values, axis=(0, 1))

    def own_bias(part):
        return head_rows_back(part[:, None], ctx, plan.last)[:, 0]

    up_rows = reorder_back(up_bias_part.reshape(n_dp, plan.width), plan.order)
    mine = (jnp.arange(4) == ctx).astype(F32)
    vector_part = jnp.concatenate(
        [
            row_sum(back_one * hat_one),
            row_sum(back_one),
            own_bias(qkv_bias_part[:own_width]),
            own_bias(qkv_bias_part[2 * own_width :]),
            row_sum(own_branch.astype(F32)),
            row_sum(back_two * hat_two),
            row_sum(back_two),
            row_sum(grad_out),
            (up_rows[:, None, :] * mine[None, :, None]).reshape(-1),
        ]
    )
    vector_owned = plan.vector_owned(vector_part)
    return (mixed, input_grad, attn_owned.T, up_owned.T, down_owned, vector_owned)


def solution(mesh):
    return jax.shard_map(
        shards,
        mesh=mesh,
        in_specs=(
            P(None, BOTH, None),
            P(None, BOTH, None),
            P(None, BOTH),
            P(None, BOTH),
            P(BOTH, None),
            P(BOTH),
            P(None, "dp", None),
        ),
        out_specs=(
            P(None, BOTH, None),
            P(None, BOTH, None),
            P(None, BOTH),
            P(None, BOTH),
            P(BOTH, None),
            P(BOTH),
        ),
        check_vma=False,
    )
```

```python
import jax
import jax.numpy as jnp
from jax import lax
from jax.experimental import pallas as pl
from jax.experimental.layout import Layout, with_layout_constraint
from jax.experimental.pallas import tpu as pltpu
from jax.sharding import PartitionSpec as P

HEAD_DIM = 64
HALO = 32
BODY = 128
NEG_FILL = -1e30
EPSILON = 1e-05
BF = jnp.bfloat16
F32 = jnp.float32
BOTH = ("dp", "ctx")
CORE_PAIRS = [(0, 1), (1, 0), (2, 3), (3, 2)]
CHIP_PAIRS = [(0, 2), (2, 0), (1, 3), (3, 1)]
BLOCKS = (0, 2, 1, 3)
SIDE_PAIRS = [(p, p ^ 1) for p in range(8)]


def shift_pairs(step):
    return [(z * 2 + y, ((z + step) % 4) * 2 + y) for z in range(4) for y in range(2)]


def dot(left, right, left_dim, right_dim):
    return lax.dot_general(
        left, right, (((left_dim,), (right_dim,)), ((), ())), preferred_element_type=F32
    )


def after(value, *others):
    return lax.optimization_barrier((value,) + others)[0]


def norm_stats(values):
    centred = values - jnp.mean(values, axis=-1, keepdims=True)
    scale = lax.rsqrt(jnp.mean(centred * centred, axis=-1, keepdims=True) + EPSILON)
    return centred * scale, scale


def norm_pull(grad, hat, scale, gain):
    grad_hat = grad * gain
    along = jnp.mean(grad_hat * hat, axis=-1, keepdims=True)
    return scale * (grad_hat - jnp.mean(grad_hat, axis=-1, keepdims=True) - hat * along)


def row_major(value):
    return with_layout_constraint(value, Layout(tuple(range(value.ndim))))


def send(value, axes, pairs):
    return row_major(lax.ppermute(row_major(value), axes, pairs))


def norm_stats(values):
    centred = values - jnp.mean(values, axis=-1, keepdims=True)
    scale = lax.rsqrt(jnp.mean(centred * centred, axis=-1, keepdims=True) + EPSILON)
    return centred * scale, scale


def norm_pull(grad, hat, scale, gain):
    grad_hat = grad * gain
    along = jnp.mean(grad_hat * hat, axis=-1, keepdims=True)
    return scale * (grad_hat - jnp.mean(grad_hat, axis=-1, keepdims=True) - hat * along)


def row_major(value):
    return with_layout_constraint(value, Layout(tuple(range(value.ndim))))


def send(value, axes, pairs):
    return row_major(lax.ppermute(row_major(value), axes, pairs))


def after(value, *others):
    return lax.optimization_barrier((value,) + others)[0]


def row_gather(mine):
    across = send(mine, "ctx", CHIP_PAIRS)
    return [mine, across, send(mine, "ctx", CORE_PAIRS), send(across, "ctx", CORE_PAIRS)]


def core_sum(keep, other, away):
    rows = keep.shape[1]
    arrived = send(away, "ctx", CORE_PAIRS)
    return keep, arrived, (other + arrived[:, rows:].astype(F32)).astype(BF)


def chip_sum(keep, arrived, away):
    return keep, arrived, send(away, "ctx", CHIP_PAIRS)


def near_gather(block):
    first, third, second = [send(block, "dp", shift_pairs(k)) for k in (1, 3, 2)]
    return [block, first, second, third]


def side_gather(near):
    return [send(own, "dp", SIDE_PAIRS) for own in near]


def shifted_sum(parts):
    total = parts[0]
    for k in (2, 3, 1):
        back = [(b, a) for a, b in shift_pairs(k)]
        total = total + send(parts[k].astype(BF), "dp", back).astype(F32)
    return total


def dp_order(z, y):
    return [((z - k) % 4) * 2 + (y ^ s) for k in range(4) for s in range(2)]


def pick(stacked, index):
    return lax.dynamic_index_in_dim(stacked, index, axis=0, keepdims=False)


def reorder(table, order):
    hot = (order[:, None] == jnp.arange(table.shape[0])[None, :]).astype(F32)
    return jnp.sum(hot[:, :, None] * table[None], axis=1)


def reorder_back(table, order):
    hot = (order[:, None] == jnp.arange(table.shape[0])[None, :]).astype(F32)
    return jnp.sum(hot[:, :, None] * table[:, None, :], axis=0)


def ctx_table(mine, ctx):
    across = lax.ppermute(mine[None], "ctx", CHIP_PAIRS)
    pair = jnp.concatenate([mine[None], across], axis=0)
    table = jnp.concatenate([pair, lax.ppermute(pair, "ctx", CORE_PAIRS)], axis=0)
    return reorder_back(table.astype(F32), jnp.stack([ctx ^ j for j in BLOCKS]))


class Aligned:
    def __init__(self, w_attn):
        dp = lax.axis_index("dp")
        self.ctx = lax.axis_index("ctx")
        self.z, self.y = dp // 2, dp % 2
        self.order = jnp.stack(dp_order(self.z, self.y))
        self.width = w_attn.shape[1]
        self.odd = self.y == 1
        self.last = self.ctx == 3

    def halo(self, edge, back):
        pairs = []
        for p in range(8):
            for c in range(4):
                to = (c - 1) % 4 if (p % 2 == 1) != back else (c + 1) % 4
                pairs.append((p * 4 + c, p * 4 + to))
        return lax.ppermute(edge, BOTH, pairs)

    def attn_weights(self, w_attn, vectors):
        turned = row_major(w_attn.T)
        width, model = turned.shape
        table = ctx_table(vectors, self.ctx).astype(BF).reshape(-1)
        halo = self.halo(jnp.where(self.odd, turned[:HALO], turned[width - HALO :]), False)
        none = jnp.zeros_like(halo)
        wide = jnp.concatenate(
            [jnp.where(self.odd, none, halo), turned, jnp.where(self.odd, halo, none)], axis=0
        )
        body = lax.dynamic_slice_in_dim(wide, HALO - 8 * self.ctx + HALO * self.y, BODY, axis=0)
        extra = lax.dynamic_slice_in_dim(wide, width + HALO * self.y, HALO, axis=0)
        extra = jnp.where(self.last, extra, jnp.zeros_like(extra))
        lines = jnp.pad(table, (0, 2 * model - table.shape[0])).reshape(2, model)
        block = jnp.concatenate([body, extra, jnp.pad(lines, ((0, 14), (0, 0)))], axis=0)
        self.started = block
        near = near_gather(block)
        side = side_gather(near)
        self.arrived = near[1:] + side[:2]
        rows = jnp.stack([b[BODY + HALO : BODY + HALO + 2] for pair in zip(near, side) for b in pair])
        rows = reorder_back(rows.reshape(8, 2 * model).astype(F32), self.order)
        return near, side, rows[:, : table.shape[0]].reshape(-1)

    def attn_owned(self, keeps, sends):
        arrived = side_gather(sends)
        own = shifted_sum([k.astype(F32) + a.astype(F32) for k, a in zip(keeps, arrived)])
        body, extra = own[:BODY], own[BODY:]
        tail = jnp.where(self.last, extra, body[BODY - HALO :])
        halo = self.halo(jnp.where(self.odd, tail, body[:HALO]), True)
        halo = jnp.where(self.last & (self.y == 0), extra, halo)
        wide = jnp.where(
            self.odd,
            jnp.concatenate([halo, body], axis=0),
            jnp.concatenate([body, halo], axis=0),
        )
        return lax.dynamic_slice_in_dim(wide, 8 * self.ctx, self.width, axis=0)

    def mlp_weights(self, w_up, w_down):
        block = jnp.concatenate([w_up.T, w_down], axis=0)
        near = near_gather(after(block, *self.arrived))
        near[0] = block
        side = side_gather(near)
        return [b for pair in zip(near, side) for b in pair]

    def mlp_owned(self, blocks, first, second):
        arrived = side_gather(blocks[1::2])
        parts = []
        for k, gate in ((0, second), (1, second), (2, first), (3, first)):
            own, other = blocks[2 * k], after(arrived[k], gate)
            parts.append(own.astype(F32) + other.astype(F32))
        total = shifted_sum(parts)
        return total[: self.width], total[self.width :]

    def vector_owned(self, part):
        each = part.shape[0] // 32
        table = part.reshape(8, 4, each).transpose(1, 0, 2)
        table = jnp.stack([pick(table, self.ctx ^ j) for j in BLOCKS])
        mine = table[:2] + lax.ppermute(table[2:], "ctx", CORE_PAIRS)
        mine = mine[0] + lax.ppermute(mine[1], "ctx", CHIP_PAIRS)
        sides = mine.reshape(4, 2, each).transpose(1, 0, 2)
        mine = pick(sides, self.y) + lax.ppermute(pick(sides, 1 - self.y), "dp", SIDE_PAIRS)
        total = pick(mine, self.z)
        for k in (1, 2, 3):
            back = [(b, a) for a, b in shift_pairs(k)]
            total = total + lax.ppermute(pick(mine, (self.z - k) % 4)[None], "dp", back)[0]
        return total


class Plain:
    def __init__(self, w_attn):
        self.ctx = lax.axis_index("ctx")
        self.started = w_attn
        self.z = self.y = jnp.zeros((), jnp.int32)
        self.order = jnp.arange(lax.axis_size("dp"))
        self.width = w_attn.shape[1]
        self.last = self.ctx == lax.axis_size("ctx") - 1

    def attn_weights(self, w_attn, vectors):
        model = w_attn.shape[0]
        whole = lax.all_gather(w_attn.T, BOTH, axis=0, tiled=True)
        near, side = [], []
        for k in range(4):
            region = -k % 4
            rows = head_rows(whole[region * model : (region + 1) * model], self.ctx, self.last)
            extra = rows[2 * BODY :]
            pad = jnp.zeros((16, model), rows.dtype)
            near.append(jnp.concatenate([rows[:BODY], extra[:HALO], pad], axis=0))
            side.append(jnp.concatenate([rows[BODY : 2 * BODY], extra[HALO:], pad], axis=0))
        return near, side, lax.all_gather(vectors, BOTH, axis=0, tiled=True).astype(F32)

    def attn_owned(self, keeps, sends):
        parts = []
        for region in range(4):
            keep, other = keeps[-region % 4], sends[-region % 4]
            rows = [keep[:BODY], other[:BODY], keep[BODY:], other[BODY:]]
            parts.append(head_rows_back(jnp.concatenate(rows, axis=0), self.ctx, self.last))
        whole = jnp.concatenate(parts, axis=0)
        return lax.psum_scatter(whole, BOTH, scatter_dimension=0, tiled=True).astype(F32)

    def mlp_weights(self, w_up, w_down):
        up = lax.all_gather(w_up.T, "dp", axis=0, tiled=True)
        down = lax.all_gather(w_down, "dp", axis=0, tiled=True)
        each = up.shape[0] // 8
        return [
            jnp.concatenate([w[i * each : (i + 1) * each] for w in (up, down)], axis=0)
            for i in range(8)
        ]

    def mlp_owned(self, blocks, first, second):
        each = blocks[0].shape[0] // 2
        halves = [[b[:each] for b in blocks], [b[each:] for b in blocks]]
        return tuple(
            lax.psum_scatter(
                jnp.concatenate(h, axis=0), "dp", scatter_dimension=0, tiled=True
            ).astype(F32)
            for h in halves
        )

    def vector_owned(self, part):
        return lax.psum_scatter(part, BOTH, scatter_dimension=0, tiled=True)


def head_rows(table, ctx, last):
    middle = 8 * HEAD_DIM
    first = lax.dynamic_slice_in_dim(table, 128 * ctx, 128, axis=0)
    second = lax.dynamic_slice_in_dim(table, middle + HEAD_DIM + 128 * ctx, 128, axis=0)
    mid = table[middle : middle + HEAD_DIM]
    return jnp.concatenate([first, second, jnp.where(last, mid, jnp.zeros_like(mid))], axis=0)


def head_rows_back(mine, ctx, last):
    middle = 8 * HEAD_DIM
    table = jnp.zeros((2 * middle + HEAD_DIM,) + mine.shape[1:], mine.dtype)
    table = lax.dynamic_update_slice_in_dim(table, mine[:128], 128 * ctx, axis=0)
    table = lax.dynamic_update_slice_in_dim(
        table, mine[128:256], middle + HEAD_DIM + 128 * ctx, axis=0
    )
    mid = jnp.where(last, mine[256:], jnp.zeros_like(mine[256:]))
    return lax.dynamic_update_slice_in_dim(table, mid, middle, axis=0)


def gelu_parts(hidden):
    factor = 0.7978845608028654
    square = hidden * hidden
    bent = jnp.tanh(factor * hidden * (1.0 + 0.044715 * square))
    active = 0.5 * hidden * (1.0 + bent)
    slope = 0.5 * (1.0 + bent) + 0.5 * hidden * (1.0 - bent * bent) * factor * (
        1.0 + 3 * 0.044715 * square
    )
    return active, slope


def full(shape):
    return pl.BlockSpec(shape, lambda *_: (0,) * len(shape))


def per(shape, step=1):
    return pl.BlockSpec((1,) + shape, lambda i: (i // step,) + (0,) * len(shape))


def params(mib):
    return pltpu.CompilerParams(vmem_limit_bytes=mib * 1024 * 1024)


def whole(array):
    return full(array.shape)


SCALARS = pl.BlockSpec(memory_space=pltpu.SMEM)


def shape_of(dtype, *dims):
    return jax.ShapeDtypeStruct(dims, dtype)


def head_places(shape, axis, ctx):
    own = lax.broadcasted_iota(jnp.int32, shape, axis)
    middle = 8 * HEAD_DIM
    shift = jnp.where(own < BODY, BODY * ctx, middle + HEAD_DIM - BODY + BODY * ctx)
    shift = jnp.where(own < 2 * BODY, shift, middle - 2 * BODY)
    return jnp.where((own < 2 * BODY) | (ctx == 3), own + shift, -1)


def write_halves(values, rows, keep_ref, other_ref, send_ref):
    keep_ref[0] = values[:rows]
    other_ref[0] = values[rows : 2 * rows]
    send_ref[0] = values[2 * rows :].astype(BF)


def attend_kernel(
    place_ref, x0, x1, x2, x3, vec_ref, n0, n1, n2, n3, s0, s1, s2, s3, col_ref, row_ref,
    normed_ref, qkv_ref, probs_ref, heads_ref, weight_ref, keep_ref, other_ref, send_ref,
    mask_ref, bias_ref,
):
    count = probs_ref.shape[1]
    width = count * HEAD_DIM
    model = vec_ref.shape[1]
    rows = x0.shape[1]

    @pl.when(pl.program_id(0) == 0)
    def _():
        z, y, ctx = place_ref[0], place_ref[1], place_ref[2]
        for k, pair in enumerate(((n0, s0), (n1, s1), (n2, s2), (n3, s3))):
            region = lax.rem(z + 4 - k, 4) * width
            for block_ref, half in zip(pair, (y, 1 - y)):
                to = pl.multiple_of(region + BODY * half, HEAD_DIM)
                weight_ref[pl.ds(to, BODY), :] = block_ref[:BODY, :]
                to = pl.multiple_of(region + 2 * BODY + HALO * half, HALO)
                weight_ref[pl.ds(to, HALO), :] = block_ref[BODY : BODY + HALO, :]
        own = head_places((model, width), 1, ctx)
        hot = (lax.broadcasted_iota(jnp.int32, (model, width), 0) == own).astype(F32).astype(BF)
        bias_ref[...] = dot(vec_ref[...].astype(BF), hot, 1, 0)

    gain, bias = vec_ref[0:1, :], vec_ref[1:2, :]
    for i, x_ref in enumerate((x0, x1, x2, x3)):
        hat, _ = norm_stats(x_ref[0].astype(F32))
        normed_ref[0, i * rows : (i + 1) * rows, :] = (hat * gain + bias).astype(BF)
    normed = normed_ref[0]
    for i, line in ((0, 2), (1, None), (2, 3)):
        part = dot(normed, weight_ref[i * width : (i + 1) * width, :], 1, 1)
        if line is not None:
            part = part + bias_ref[line : line + 1, :]
        qkv_ref[0, :, i * width : (i + 1) * width] = part.astype(BF)
    col, row = col_ref[0], row_ref[0]
    allowed = (row[1:2, :] <= col[:, 1:2]) & (row[0:1, :] == col[:, 0:1])
    mask_ref[...] = jnp.where(allowed, 0.0, NEG_FILL)
    for head in range(count):
        lanes = [slice(i * width + head * HEAD_DIM, i * width + (head + 1) * HEAD_DIM) for i in range(3)]
        queries, keys, values = [qkv_ref[0, :, part] for part in lanes]
        queries = queries * jnp.asarray(HEAD_DIM ** (-0.5), BF)
        scores = dot(queries, keys, 1, 1) + mask_ref[...]
        weights = jnp.exp(scores - jnp.max(scores, axis=1, keepdims=True))
        probs = (weights * (1.0 / jnp.sum(weights, axis=1, keepdims=True))).astype(BF)
        probs_ref[0, head] = probs
        heads_ref[0, :, lanes[0]] = dot(probs, values, 1, 0).astype(BF)
    branch = dot(heads_ref[0], weight_ref[3 * width :, :], 1, 0)
    write_halves(branch, rows, keep_ref, other_ref, send_ref)


def attend(place, blocks, vec, near, side, col, row):
    micro, rows, model = blocks[0].shape
    group = 4 * rows
    width = 2 * (BODY + HALO)
    count = width // HEAD_DIM
    return pl.pallas_call(
        attend_kernel,
        grid=(micro,),
        in_specs=[SCALARS] + [per((rows, model))] * 4 + [whole(vec)]
        + [whole(b) for b in near + side] + [per(col.shape[1:]), per(row.shape[1:])],
        out_specs=[
            per((group, model)), per((group, 3 * width)), per((count, group, group)),
            per((group, width)), full((4 * width, model)),
            per((rows, model)), per((rows, model)), per((2 * rows, model)),
        ],
        out_shape=[
            shape_of(BF, micro, group, model), shape_of(BF, micro, group, 3 * width),
            shape_of(BF, micro, count, group, group), shape_of(BF, micro, group, width),
            shape_of(BF, 4 * width, model), shape_of(F32, micro, rows, model),
            shape_of(F32, micro, rows, model), shape_of(BF, micro, 2 * rows, model),
        ],
        scratch_shapes=[pltpu.VMEM((group, group), F32), pltpu.VMEM((8, width), F32)],
        compiler_params=params(56),
        cost_estimate=pl.CostEstimate(
            flops=2 * micro * group * model * 4 * width,
            bytes_accessed=12 * micro * group * model,
            transcendentals=micro * count * group * group,
        ),
        name="attend",
    )(place, *blocks, vec, *near, *side, col, row)


def middle_kernel(x_ref, keep_ref, arrived_ref, across_ref, vec_ref, middle_ref, normed_ref):
    rows = x_ref.shape[1]
    branch = keep_ref[0] + arrived_ref[0, :rows, :].astype(F32) + across_ref[0].astype(F32)
    middle = x_ref[0].astype(F32) + branch + vec_ref[4:5, :]
    middle_ref[0] = middle
    hat, _ = norm_stats(middle)
    normed_ref[0] = (hat * vec_ref[5:6, :] + vec_ref[6:7, :]).astype(BF)


def middle_rows(x, keep, arrived, across, vec):
    micro, rows, model = x.shape
    one = per((rows, model))
    return pl.pallas_call(
        middle_kernel,
        grid=(micro,),
        in_specs=[one, one, per((2 * rows, model)), one, whole(vec)],
        out_specs=[one, one],
        out_shape=[shape_of(F32, micro, rows, model), shape_of(BF, micro, rows, model)],
        name="middle_rows",
    )(x, keep, arrived, across, vec)


def feed_kernel(
    x0, x1, x2, x3, g0, g1, g2, g3, b0, b1, b2, b3, b4, b5, b6, b7, bias_ref,
    x_ref, grad_ref, active_ref, grad_hidden_ref,
    feed_keep, feed_other, feed_send, back_keep, back_other, back_send, sum_ref,
    up_ref, down_ref,
):
    rows = x0.shape[1]
    each = b0.shape[0] // 2

    @pl.when(pl.program_id(0) == 0)
    def _():
        for i, block_ref in enumerate((b0, b1, b2, b3, b4, b5, b6, b7)):
            up_ref[i * each : (i + 1) * each, :] = block_ref[:each, :]
            down_ref[i * each : (i + 1) * each, :] = block_ref[each:, :]
        sum_ref[...] = jnp.zeros_like(sum_ref)

    for i, (a, b) in enumerate(((x0, g0), (x1, g1), (x2, g2), (x3, g3))):
        x_ref[0, i * rows : (i + 1) * rows, :] = a[0]
        grad_ref[0, i * rows : (i + 1) * rows, :] = b[0]
    active, slope = gelu_parts(dot(x_ref[0], up_ref[...], 1, 1) + bias_ref[...])
    active_ref[0] = active.astype(BF)
    grad_hidden = (dot(grad_ref[0], down_ref[...], 1, 1) * slope).astype(BF)
    grad_hidden_ref[0] = grad_hidden
    sum_ref[...] += jnp.sum(grad_hidden.astype(F32), axis=0, keepdims=True)
    write_halves(dot(grad_hidden, up_ref[...], 1, 0), rows, back_keep, back_other, back_send)
    write_halves(dot(active_ref[0], down_ref[...], 1, 0), rows, feed_keep, feed_other, feed_send)


def feed_forward(x, grads, blocks, bias):
    micro, rows, model = x[0].shape
    group = 4 * rows
    hidden = 4 * blocks[0].shape[0]
    one, two, big = per((rows, model)), per((2 * rows, model)), per((group, model))
    wide = per((group, hidden))
    halves = [
        shape_of(F32, micro, rows, model), shape_of(F32, micro, rows, model),
        shape_of(BF, micro, 2 * rows, model),
    ]
    return pl.pallas_call(
        feed_kernel,
        grid=(micro,),
        in_specs=[one] * 8 + [whole(b) for b in blocks] + [whole(bias)],
        out_specs=[big, big, wide, wide] + [one, one, two] * 2 + [full((1, hidden))],
        out_shape=[shape_of(BF, micro, group, model)] * 2
        + [shape_of(BF, micro, group, hidden)] * 2 + halves * 2 + [shape_of(F32, 1, hidden)],
        scratch_shapes=[pltpu.VMEM((hidden, model), BF)] * 2,
        compiler_params=params(60),
        cost_estimate=pl.CostEstimate(
            flops=8 * micro * group * model * hidden,
            bytes_accessed=16 * micro * group * model,
            transcendentals=micro * group * hidden,
        ),
        name="feed_forward",
    )(*x, *grads, *blocks, bias)


def feed_grads_kernel(active_ref, grad_ref, grad_hidden_ref, x_ref, *rest):
    outs, total_ref = rest[:8], rest[8]
    each = outs[0].shape[0] // 2
    step = pl.program_id(0)
    hidden = active_ref.shape[1]
    cut = hidden // 256 * 128
    for left_ref, right_ref, part in ((grad_hidden_ref, x_ref, 0), (active_ref, grad_ref, 1)):

        @pl.when(step == part)
        def _():
            total_ref[:cut, :] = dot(left_ref[:, :cut], right_ref[...], 0, 0)
            total_ref[cut:, :] = dot(left_ref[:, cut:], right_ref[...], 0, 0)
            for i, out_ref in enumerate(outs):
                rows = total_ref[i * each : (i + 1) * each, :].astype(BF)
                out_ref[part * each : (part + 1) * each, :] = rows


def feed_grads(active, grad, grad_hidden, x):
    rows, hidden = active.shape
    model = grad.shape[1]
    block = (hidden // 4, model)
    return pl.pallas_call(
        feed_grads_kernel,
        grid=(2,),
        in_specs=[whole(a) for a in (active, grad, grad_hidden, x)],
        out_specs=[full(block)] * 8,
        out_shape=[shape_of(BF, *block)] * 8,
        scratch_shapes=[pltpu.VMEM((hidden, model), F32)],
        compiler_params=params(56),
        cost_estimate=pl.CostEstimate(
            flops=4 * rows * model * hidden, bytes_accessed=12 * rows * model, transcendentals=0
        ),
        name="feed_grads",
    )(active, grad, grad_hidden, x)


def middle_pull_kernel(
    out_ref, middle_ref, keep_ref, arrived_ref, across_ref, vec_ref, grad_ref, branch_ref, sum_ref
):
    rows = out_ref.shape[1]
    back = keep_ref[0] + arrived_ref[0, :rows, :].astype(F32) + across_ref[0].astype(F32)
    hat, scale = norm_stats(middle_ref[0])
    out = out_ref[0].astype(F32)
    grad = out + norm_pull(back, hat, scale, vec_ref[5:6, :])
    grad_ref[0] = grad
    branch = grad.astype(BF)
    branch_ref[0] = branch

    @pl.when(pl.program_id(0) == 0)
    def _():
        sum_ref[...] = jnp.zeros_like(sum_ref)

    for i, terms in enumerate((branch.astype(F32), back * hat, back, out)):
        sum_ref[i : i + 1, :] += jnp.sum(terms, axis=0, keepdims=True)


def middle_pull(out, middle, keep, arrived, across, vec):
    micro, rows, model = out.shape
    one = per((rows, model))
    return pl.pallas_call(
        middle_pull_kernel,
        grid=(micro,),
        in_specs=[one, one, one, per((2 * rows, model)), one, whole(vec)],
        out_specs=[one, one, full((4, model))],
        out_shape=[
            shape_of(F32, micro, rows, model), shape_of(BF, micro, rows, model),
            shape_of(F32, 4, model),
        ],
        name="middle_pull",
    )(out, middle, keep, arrived, across, vec)


def attend_pull_kernel(
    place_ref, g0, g1, g2, g3, weight_ref, qkv_ref, probs_ref, heads_ref, normed_ref,
    keep_ref, other_ref, send_ref, k0, k1, k2, k3, s0, s1, s2, s3, bias_ref,
    grad_ref, grad_qkv_ref, total_ref, sum_ref,
):
    count = probs_ref.shape[1]
    width = count * HEAD_DIM
    rows = g0.shape[1]
    model = g0.shape[2]
    scale = HEAD_DIM ** (-0.5)
    step = pl.program_id(0)
    for i, block_ref in enumerate((g0, g1, g2, g3)):
        grad_ref[i * rows : (i + 1) * rows, :] = block_ref[0]
    grad_heads = dot(grad_ref[...], weight_ref[3 * width :, :], 1, 1).astype(BF)
    for head in range(count):
        lanes = [slice(i * width + head * HEAD_DIM, i * width + (head + 1) * HEAD_DIM) for i in range(3)]
        queries, keys, values = [qkv_ref[0, :, part] for part in lanes]
        probs = probs_ref[0, head]
        grad = grad_heads[:, lanes[0]]
        delta = jnp.sum(
            grad.astype(F32) * heads_ref[0, :, lanes[0]].astype(F32), axis=1, keepdims=True
        )
        grad_scores = (probs.astype(F32) * (dot(grad, values, 1, 1) - delta)).astype(BF)
        grad_qkv_ref[:, lanes[0]] = (scale * dot(grad_scores, keys, 1, 0)).astype(BF)
        grad_qkv_ref[:, lanes[1]] = (scale * dot(grad_scores, queries, 0, 0)).astype(BF)
        grad_qkv_ref[:, lanes[2]] = dot(probs, grad, 0, 0).astype(BF)
    write_halves(dot(grad_qkv_ref[...], weight_ref[: 3 * width, :], 1, 0), rows, keep_ref, other_ref, send_ref)
    qkv_part = dot(grad_qkv_ref[...], normed_ref[0], 0, 0)
    out_part = dot(heads_ref[0], grad_ref[...], 0, 0)
    sums = jnp.sum(grad_qkv_ref[...].astype(F32), axis=0, keepdims=True)

    @pl.when(step == 0)
    def _():
        total_ref[: 3 * width, :] = qkv_part
        total_ref[3 * width :, :] = out_part
        sum_ref[...] = jnp.broadcast_to(sums, sum_ref.shape)

    @pl.when(step > 0)
    def _():
        total_ref[: 3 * width, :] += qkv_part
        total_ref[3 * width :, :] += out_part
        sum_ref[...] += sums

    @pl.when(step == pl.num_programs(0) - 1)
    def _():
        z, y, ctx = place_ref[0], place_ref[1], place_ref[2]
        for k, pair in enumerate(((k0, s0), (k1, s1), (k2, s2), (k3, s3))):
            region = lax.rem(z + 4 - k, 4) * width
            for out_ref, half in zip(pair, (y, 1 - y)):
                start = pl.multiple_of(region + BODY * half, HEAD_DIM)
                out_ref[:BODY, :] = total_ref[pl.ds(start, BODY), :].astype(BF)
                start = pl.multiple_of(region + 2 * BODY + HALO * half, HALO)
                out_ref[BODY:, :] = total_ref[pl.ds(start, HALO), :].astype(BF)
        own = head_places((width, model), 0, ctx)
        hot = (lax.broadcasted_iota(jnp.int32, (width, model), 1) == own).astype(F32)
        for i, part in enumerate((0, 2)):
            line = lax.dot_general(
                sum_ref[:, part * width : (part + 1) * width],
                hot,
                (((1,), (0,)), ((), ())),
                preferred_element_type=F32,
                precision=lax.Precision.HIGHEST,
            )
            bias_ref[i : i + 1, :] = line[0:1]


def attend_pull(place, grads, weight, qkv, probs, heads, normed):
    micro, rows, model = grads[0].shape
    group = 4 * rows
    width = heads.shape[2]
    count = width // HEAD_DIM
    block = (BODY + HALO, model)
    one = per((rows, model))
    return pl.pallas_call(
        attend_pull_kernel,
        grid=(micro,),
        in_specs=[SCALARS] + [one] * 4 + [
            whole(weight), per((group, 3 * width)), per((count, group, group)),
            per((group, width)), per((group, model)),
        ],
        out_specs=[one, one, per((2 * rows, model))] + [full(block)] * 8 + [full((2, model))],
        out_shape=[
            shape_of(F32, micro, rows, model), shape_of(F32, micro, rows, model),
            shape_of(BF, micro, 2 * rows, model),
        ] + [shape_of(BF, *block)] * 8 + [shape_of(F32, 2, model)],
        scratch_shapes=[
            pltpu.VMEM((group, model), BF), pltpu.VMEM((group, 3 * width), BF),
            pltpu.VMEM((4 * width, model), F32), pltpu.VMEM((8, 3 * width), F32),
        ],
        compiler_params=params(60),
        cost_estimate=pl.CostEstimate(
            flops=2 * micro * group * model * 10 * width,
            bytes_accessed=12 * micro * group * model,
            transcendentals=0,
        ),
        name="attend_pull",
    )(place, *grads, weight, qkv, probs, heads, normed)


def input_pull_kernel(
    x_ref, grad_ref, keep_ref, arrived_ref, across_ref, vec_ref, out_ref, sum_ref
):
    rows = x_ref.shape[1]
    back = keep_ref[0] + arrived_ref[0, :rows, :].astype(F32) + across_ref[0].astype(F32)
    hat, scale = norm_stats(x_ref[0].astype(F32))
    out_ref[0] = (grad_ref[0] + norm_pull(back, hat, scale, vec_ref[0:1, :])).astype(BF)

    @pl.when(pl.program_id(0) == 0)
    def _():
        sum_ref[...] = jnp.zeros_like(sum_ref)

    for i, terms in enumerate((back * hat, back)):
        sum_ref[i : i + 1, :] += jnp.sum(terms, axis=0, keepdims=True)


def input_pull(x, grad, keep, arrived, across, vec):
    micro, rows, model = x.shape
    one = per((rows, model))
    return pl.pallas_call(
        input_pull_kernel,
        grid=(micro,),
        in_specs=[one, one, one, per((2 * rows, model)), one, whole(vec)],
        out_specs=[one, full((2, model))],
        out_shape=[shape_of(BF, micro, rows, model), shape_of(F32, 2, model)],
        name="input_pull",
    )(x, grad, keep, arrived, across, vec)


def mixed_kernel(middle_ref, keep_ref, arrived_ref, across_ref, vec_ref, out_ref):
    rows = middle_ref.shape[1]
    feed = keep_ref[0] + arrived_ref[0, :rows, :].astype(F32) + across_ref[0].astype(F32)
    out_ref[0] = (middle_ref[0] + feed + vec_ref[7:8, :]).astype(BF)


def mixed_rows(middle, keep, arrived, across, vec):
    micro, rows, model = middle.shape
    one = per((rows, model))
    return pl.pallas_call(
        mixed_kernel,
        grid=(micro,),
        in_specs=[one, one, per((2 * rows, model)), one, whole(vec)],
        out_specs=one,
        out_shape=shape_of(BF, micro, rows, model),
        name="mixed_rows",
    )(middle, keep, arrived, across, vec)


def shards(tokens, cotangent, w_attn, w_up, w_down, vectors, segments):
    micro, rows, model = tokens.shape
    ctx = lax.axis_index("ctx")
    n_dp = lax.axis_size("dp")
    fits = n_dp == 8 and lax.axis_size("ctx") == 4 and w_attn.shape == (1088, 136)
    plan = (Aligned if fits else Plain)(w_attn)
    place = jnp.stack([plan.z, plan.y, ctx]).astype(jnp.int32)

    tokens, cotangent = row_major(tokens), row_major(cotangent)
    near, side, vec = plan.attn_weights(w_attn, vectors)
    all_tokens = row_gather(after(tokens, plan.started))
    all_grads = row_gather(after(cotangent, all_tokens[1]))
    blocks = plan.mlp_weights(w_up, w_down)
    lines = vec[: 8 * model].reshape(8, model)
    up_bias = vec[8 * model :].reshape(n_dp, 4, plan.width)
    up_bias = reorder(pick(up_bias.transpose(1, 0, 2), ctx), plan.order).reshape(1, -1)

    ranks = [ctx ^ j for j in BLOCKS]
    starts = segments[:, 0].reshape(micro, 4, rows).transpose(1, 0, 2)
    starts = jnp.concatenate([pick(starts, r) for r in ranks], axis=1)
    places = jnp.concatenate([r * rows + jnp.arange(rows, dtype=jnp.int32) for r in ranks])
    places = jnp.broadcast_to(places[None], starts.shape)
    row_info = jnp.stack([starts, places] + [places] * 6, axis=1)
    col_info = row_info.transpose(0, 2, 1)

    all_tokens[0] = after(tokens, all_grads[1], blocks[1], blocks[2])
    normed_one, qkv, probs, heads, weight, *halves = attend(
        place, all_tokens, lines, near, side, col_info, row_info
    )
    branch = chip_sum(*core_sum(*halves))
    middle, normed_two = middle_rows(after(tokens, blocks[3]), *branch, lines)
    x_all, grad_all, active, grad_hidden, *halves, up_sum = feed_forward(
        row_gather(normed_two), all_grads, blocks, up_bias
    )
    back = core_sum(*halves[3:])
    feed = core_sum(*halves[:3])

    def flat(values):
        return values.reshape(-1, values.shape[-1])

    active = after(active, back[1])
    parts = feed_grads(flat(active), flat(grad_all), flat(grad_hidden), flat(x_all))
    grad_middle, branch, sums = middle_pull(cotangent, middle, *chip_sum(*back), lines)
    branches = row_gather(branch)
    up_owned, down_owned = plan.mlp_owned(parts, branch, branches[1])
    feed = chip_sum(feed[0], feed[1], after(feed[2], branches[1]))

    *halves, k0, k1, k2, k3, s0, s1, s2, s3, bias_sums = attend_pull(
        place, branches, weight, qkv, probs, heads, normed_one
    )
    mixed = mixed_rows(after(middle, halves[0]), *feed, lines)
    attn_owned = plan.attn_owned([k0, k1, k2, k3], [s0, s1, s2, s3])
    input_grad, first_sums = input_pull(tokens, grad_middle, *chip_sum(*core_sum(*halves)), lines)

    up_rows = reorder_back(up_sum.reshape(n_dp, plan.width), plan.order)
    mine = (jnp.arange(4) == ctx).astype(F32)
    table = jnp.concatenate([first_sums, bias_sums, sums], axis=0)
    vector_part = jnp.concatenate(
        [table.reshape(-1), (up_rows[:, None, :] * mine[None, :, None]).reshape(-1)]
    )
    vector_owned = plan.vector_owned(vector_part)
    return (mixed, input_grad, attn_owned.T, up_owned.T, down_owned, vector_owned)


def solution(mesh):
    return jax.shard_map(
        shards,
        mesh=mesh,
        in_specs=(
            P(None, BOTH, None),
            P(None, BOTH, None),
            P(None, BOTH),
            P(None, BOTH),
            P(BOTH, None),
            P(BOTH),
            P(None, "dp", None),
        ),
        out_specs=(
            P(None, BOTH, None),
            P(None, BOTH, None),
            P(None, BOTH),
            P(None, BOTH),
            P(BOTH, None),
            P(BOTH),
        ),
        check_vma=False,
    )
```

```python
import jax
import jax.numpy as jnp
from jax import lax
from jax.experimental import pallas as pl
from jax.experimental.layout import Layout, with_layout_constraint
from jax.experimental.pallas import tpu as pltpu
from jax.sharding import PartitionSpec as P

HEAD_DIM = 64
HALO = 32
BODY = 128
NEG_FILL = -1e30
EPSILON = 1e-05
BF = jnp.bfloat16
F32 = jnp.float32
BOTH = ("dp", "ctx")
CORE_PAIRS = [(0, 1), (1, 0), (2, 3), (3, 2)]
CHIP_PAIRS = [(0, 2), (2, 0), (1, 3), (3, 1)]
BLOCKS = (0, 2, 1, 3)
SHIFTS = (0, 1, 3, 2)
CUT = 144
SIDE_PAIRS = [(p, p ^ 1) for p in range(8)]


def shift_pairs(step):
    return [(z * 2 + y, ((z + step) % 4) * 2 + y) for z in range(4) for y in range(2)]


def dot(left, right, left_dim, right_dim):
    return lax.dot_general(
        left, right, (((left_dim,), (right_dim,)), ((), ())), preferred_element_type=F32
    )


def norm_stats(values):
    centred = values - jnp.mean(values, axis=-1, keepdims=True)
    scale = lax.rsqrt(jnp.mean(centred * centred, axis=-1, keepdims=True) + EPSILON)
    return centred * scale, scale


def norm_pull(grad, hat, scale, gain):
    grad_hat = grad * gain
    along = jnp.mean(grad_hat * hat, axis=-1, keepdims=True)
    return scale * (grad_hat - jnp.mean(grad_hat, axis=-1, keepdims=True) - hat * along)


def row_major(value):
    return with_layout_constraint(value, Layout(tuple(range(value.ndim))))


def send(value, axes, pairs):
    rows = value.shape[-2]
    if rows % 16:
        return lax.ppermute(value, axes, pairs)
    cut = value.reshape(value.shape[:-2] + (rows // 16, 16, value.shape[-1]))
    return lax.ppermute(cut, axes, pairs).reshape(value.shape)


def hold(values, *others):
    return lax.optimization_barrier(tuple(values) + tuple(others))[: len(values)]


def to_core(value):
    return send(value, "ctx", CORE_PAIRS)


def to_chip(value):
    return send(value, "ctx", CHIP_PAIRS)


def to_side(value):
    return send(value, "dp", SIDE_PAIRS)


def to_shift(value, step, back=False):
    pairs = shift_pairs(step)
    return send(value, "dp", [(b, a) for a, b in pairs] if back else pairs)


def row_gather(mine):
    across = to_chip(mine)
    return [mine, across, to_core(mine), to_core(across)]


def half_sum(other, arrived):
    rows = other.shape[1]
    return (other.astype(F32) + arrived[:, rows:].astype(F32)).astype(BF)


def row_scatter(keep, other, away):
    arrived = to_core(away)
    return keep, arrived, to_chip(half_sum(other, arrived))


def dp_order(z, y):
    return [((z - k) % 4) * 2 + (y ^ s) for k in SHIFTS for s in range(2)]


def pick(stacked, index):
    return lax.dynamic_index_in_dim(stacked, index, axis=0, keepdims=False)


def reorder(table, order):
    hot = (order[:, None] == jnp.arange(table.shape[0])[None, :]).astype(F32)
    return jnp.sum(hot[:, :, None] * table[None], axis=1)


def reorder_back(table, order):
    hot = (order[:, None] == jnp.arange(table.shape[0])[None, :]).astype(F32)
    return jnp.sum(hot[:, :, None] * table[:, None, :], axis=0)


def ctx_table(mine, ctx):
    across = lax.ppermute(mine[None], "ctx", CHIP_PAIRS)
    pair = jnp.concatenate([mine[None], across], axis=0)
    table = jnp.concatenate([pair, lax.ppermute(pair, "ctx", CORE_PAIRS)], axis=0)
    return reorder_back(table.astype(F32), jnp.stack([ctx ^ j for j in BLOCKS]))


def head_rows(table, ctx, last):
    middle = 8 * HEAD_DIM
    first = lax.dynamic_slice_in_dim(table, 128 * ctx, 128, axis=0)
    second = lax.dynamic_slice_in_dim(table, middle + HEAD_DIM + 128 * ctx, 128, axis=0)
    mid = table[middle : middle + HEAD_DIM]
    return jnp.concatenate([first, second, jnp.where(last, mid, jnp.zeros_like(mid))], axis=0)


def head_rows_back(mine, ctx, last):
    middle = 8 * HEAD_DIM
    table = jnp.zeros((2 * middle + HEAD_DIM,) + mine.shape[1:], mine.dtype)
    table = lax.dynamic_update_slice_in_dim(table, mine[:128], 128 * ctx, axis=0)
    table = lax.dynamic_update_slice_in_dim(
        table, mine[128:256], middle + HEAD_DIM + 128 * ctx, axis=0
    )
    mid = jnp.where(last, mine[256:], jnp.zeros_like(mine[256:]))
    return lax.dynamic_update_slice_in_dim(table, mid, middle, axis=0)


def gelu_parts(hidden):
    factor = 0.7978845608028654
    square = hidden * hidden
    bent = jnp.tanh(factor * hidden * (1.0 + 0.044715 * square))
    active = 0.5 * hidden * (1.0 + bent)
    slope = 0.5 * (1.0 + bent) + 0.5 * hidden * (1.0 - bent * bent) * factor * (
        1.0 + 3 * 0.044715 * square
    )
    return active, slope


def full(shape):
    return pl.BlockSpec(shape, lambda *_: (0,) * len(shape))


def per(shape, step=1):
    return pl.BlockSpec((1,) + shape, lambda i: (i // step,) + (0,) * len(shape))


def params(mib):
    return pltpu.CompilerParams(vmem_limit_bytes=mib * 1024 * 1024)


def whole(array):
    return full(array.shape)


SCALARS = pl.BlockSpec(memory_space=pltpu.SMEM)


def shape_of(dtype, *dims):
    return jax.ShapeDtypeStruct(dims, dtype)


def head_places(shape, axis, ctx):
    own = lax.broadcasted_iota(jnp.int32, shape, axis)
    middle = 8 * HEAD_DIM
    shift = jnp.where(own < BODY, BODY * ctx, middle + HEAD_DIM - BODY + BODY * ctx)
    shift = jnp.where(own < 2 * BODY, shift, middle - 2 * BODY)
    return jnp.where((own < 2 * BODY) | (ctx == 3), own + shift, -1)


def write_halves(values, rows, keep_ref, other_ref, send_ref):
    keep_ref[0] = values[:rows]
    other_ref[0] = values[rows : 2 * rows].astype(BF)
    send_ref[0] = values[2 * rows :].astype(BF)


def attend_kernel(
    place_ref, x0, x1, x2, x3, n0, n1, n2, n3, s0, s1, s2, s3, row_ref,
    normed_ref, qkv_ref, probs_ref, heads_ref, weight_ref, vec_ref, line_ref,
    keep_ref, other_ref, send_ref, mask_ref, bias_ref,
):
    count = probs_ref.shape[1]
    width = count * HEAD_DIM
    model = vec_ref.shape[1]
    part = model // 2
    rows = x0.shape[1]

    @pl.when(pl.program_id(0) == 0)
    def _():
        z, y, ctx = place_ref[0], place_ref[1], place_ref[2]
        for k, pair in zip(SHIFTS, ((n0, s0), (n1, s1), (n2, s2), (n3, s3))):
            owner = lax.rem(z + 4 - k, 4)
            region = owner * width
            for block_ref, half in zip(pair, (y, 1 - y)):
                lines = block_ref[BODY + HALO :, :].astype(F32)
                for i in range(3):
                    line_ref[pl.ds(3 * (2 * owner + half) + i, 1), :] = lines[i : i + 1, :part]
                to = pl.multiple_of(region + BODY * half, HEAD_DIM)
                weight_ref[pl.ds(to, BODY), :] = block_ref[:BODY, :]
                to = pl.multiple_of(region + 2 * BODY + HALO * half, HALO)
                weight_ref[pl.ds(to, HALO), :] = block_ref[BODY : BODY + HALO, :]
        for i in range(8):
            vec_ref[i : i + 1, :part] = line_ref[2 * i : 2 * i + 1, :]
            vec_ref[i : i + 1, part:] = line_ref[2 * i + 1 : 2 * i + 2, :]
        own = head_places((model, width), 1, ctx)
        hot = (lax.broadcasted_iota(jnp.int32, (model, width), 0) == own).astype(F32).astype(BF)
        bias_ref[...] = dot(vec_ref[...].astype(BF), hot, 1, 0)

    gain, bias = vec_ref[0:1, :], vec_ref[1:2, :]
    for i, x_ref in enumerate((x0, x1, x2, x3)):
        hat, _ = norm_stats(x_ref[0].astype(F32))
        normed_ref[0, i * rows : (i + 1) * rows, :] = (hat * gain + bias).astype(BF)
    normed = normed_ref[0]
    for i, line in ((0, 2), (1, None), (2, 3)):
        part = dot(normed, weight_ref[i * width : (i + 1) * width, :], 1, 1)
        if line is not None:
            part = part + bias_ref[line : line + 1, :]
        qkv_ref[0, :, i * width : (i + 1) * width] = part.astype(BF)
    row = row_ref[0].astype(F32)
    first, own = row[0:1], row[1:2]
    square = (128, row.shape[1])
    first_col = jnp.transpose(jnp.broadcast_to(first, square))[:, :1]
    own_col = jnp.transpose(jnp.broadcast_to(own, square))[:, :1]
    allowed = (own <= own_col) & (first == first_col)
    mask_ref[...] = jnp.where(allowed, 0.0, NEG_FILL)
    for head in range(count):
        lanes = [slice(i * width + head * HEAD_DIM, i * width + (head + 1) * HEAD_DIM) for i in range(3)]
        queries, keys, values = [qkv_ref[0, :, part] for part in lanes]
        queries = queries * jnp.asarray(HEAD_DIM ** (-0.5), BF)
        scores = dot(queries, keys, 1, 1) + mask_ref[...]
        weights = jnp.exp(scores - jnp.max(scores, axis=1, keepdims=True))
        probs = (weights * (1.0 / jnp.sum(weights, axis=1, keepdims=True))).astype(BF)
        probs_ref[0, head] = probs
        heads_ref[0, :, lanes[0]] = dot(probs, values, 1, 0).astype(BF)
    branch = dot(heads_ref[0], weight_ref[3 * width :, :], 1, 0)
    write_halves(branch, rows, keep_ref, other_ref, send_ref)


def attend(place, blocks, near, side, row):
    micro, rows, model = blocks[0].shape
    group = 4 * rows
    width = 2 * (BODY + HALO)
    count = width // HEAD_DIM
    return pl.pallas_call(
        attend_kernel,
        grid=(micro,),
        in_specs=[SCALARS] + [per((rows, model))] * 4
        + [whole(b) for b in near + side] + [per(row.shape[1:])],
        out_specs=[
            per((group, model)), per((group, 3 * width)), per((count, group, group)),
            per((group, width)), full((4 * width, model)), full((8, model)), full((24, model // 2)),
            per((rows, model)), per((rows, model)), per((2 * rows, model)),
        ],
        out_shape=[
            shape_of(BF, micro, group, model), shape_of(BF, micro, group, 3 * width),
            shape_of(BF, micro, count, group, group), shape_of(BF, micro, group, width),
            shape_of(BF, 4 * width, model), shape_of(F32, 8, model),
            shape_of(F32, 24, model // 2), shape_of(F32, micro, rows, model),
            shape_of(BF, micro, rows, model), shape_of(BF, micro, 2 * rows, model),
        ],
        scratch_shapes=[pltpu.VMEM((group, group), F32), pltpu.VMEM((8, width), F32)],
        compiler_params=params(56),
        cost_estimate=pl.CostEstimate(
            flops=2 * micro * group * model * 4 * width,
            bytes_accessed=12 * micro * group * model,
            transcendentals=micro * count * group * group,
        ),
        name="attend",
    )(place, *blocks, *near, *side, row)


def middle_kernel(x_ref, keep_ref, arrived_ref, across_ref, vec_ref, middle_ref, normed_ref):
    rows = x_ref.shape[1]
    branch = keep_ref[0] + arrived_ref[0, :rows, :].astype(F32) + across_ref[0].astype(F32)
    middle = x_ref[0].astype(F32) + branch + vec_ref[4:5, :]
    middle_ref[0] = middle
    hat, _ = norm_stats(middle)
    normed_ref[0] = (hat * vec_ref[5:6, :] + vec_ref[6:7, :]).astype(BF)


def middle_rows(x, keep, arrived, across, vec):
    micro, rows, model = x.shape
    one = per((rows, model))
    return pl.pallas_call(
        middle_kernel,
        grid=(micro,),
        in_specs=[one, one, per((2 * rows, model)), one, whole(vec)],
        out_specs=[one, one],
        out_shape=[shape_of(F32, micro, rows, model), shape_of(BF, micro, rows, model)],
        name="middle_rows",
    )(x, keep, arrived, across, vec)


def feed_kernel(
    x0, x1, x2, x3, g0, g1, g2, g3, b0, b1, b2, b3, b4, b5, b6, b7, c6, c7, bias_ref,
    x_ref, grad_ref, active_ref, grad_hidden_ref,
    feed_keep, feed_other, feed_send, back_keep, back_other, back_send, sum_ref,
    up_ref, down_ref,
):
    rows = x0.shape[1]
    each = b0.shape[0] // 2

    @pl.when(pl.program_id(0) == 0)
    def _():
        for i, block_ref in enumerate((b0, b1, b2, b3, b4, b5, b6, b7)):
            rest = block_ref.shape[0] - each
            up_ref[i * each : (i + 1) * each, :] = block_ref[:each, :]
            down_ref[i * each : i * each + rest, :] = block_ref[each:, :]
        for i, block_ref in ((6, c6), (7, c7)):
            down_ref[(i + 1) * each - block_ref.shape[0] : (i + 1) * each, :] = block_ref[...]
        sum_ref[...] = jnp.zeros_like(sum_ref)

    for i, (a, b) in enumerate(((x0, g0), (x1, g1), (x2, g2), (x3, g3))):
        x_ref[0, i * rows : (i + 1) * rows, :] = a[0]
        grad_ref[0, i * rows : (i + 1) * rows, :] = b[0]
    active, slope = gelu_parts(dot(x_ref[0], up_ref[...], 1, 1) + bias_ref[...])
    active_ref[0] = active.astype(BF)
    grad_hidden = (dot(grad_ref[0], down_ref[...], 1, 1) * slope).astype(BF)
    grad_hidden_ref[0] = grad_hidden
    sum_ref[...] += jnp.sum(grad_hidden.astype(F32), axis=0, keepdims=True)
    write_halves(dot(grad_hidden, up_ref[...], 1, 0), rows, back_keep, back_other, back_send)
    write_halves(dot(active_ref[0], down_ref[...], 1, 0), rows, feed_keep, feed_other, feed_send)


def feed_forward(x, grads, blocks, bias):
    micro, rows, model = x[0].shape
    group = 4 * rows
    hidden = 4 * blocks[0].shape[0]
    one, two, big = per((rows, model)), per((2 * rows, model)), per((group, model))
    wide = per((group, hidden))
    halves = [
        shape_of(F32, micro, rows, model), shape_of(BF, micro, rows, model),
        shape_of(BF, micro, 2 * rows, model),
    ]
    return pl.pallas_call(
        feed_kernel,
        grid=(micro,),
        in_specs=[one] * 8 + [whole(b) for b in blocks] + [whole(bias)],
        out_specs=[big, big, wide, wide] + [one, one, two] * 2 + [full((1, hidden))],
        out_shape=[shape_of(BF, micro, group, model)] * 2
        + [shape_of(BF, micro, group, hidden)] * 2 + halves * 2 + [shape_of(F32, 1, hidden)],
        scratch_shapes=[pltpu.VMEM((hidden, model), BF)] * 2,
        compiler_params=params(60),
        cost_estimate=pl.CostEstimate(
            flops=8 * micro * group * model * hidden,
            bytes_accessed=16 * micro * group * model,
            transcendentals=micro * group * hidden,
        ),
        name="feed_forward",
    )(*x, *grads, *blocks, bias)


def feed_grads_kernel(active_ref, grad_ref, grad_hidden_ref, x_ref, *rest):
    outs, total_ref = rest[:8], rest[8]
    each = outs[0].shape[0] // 2
    step = pl.program_id(0)
    hidden = active_ref.shape[1]
    cut = hidden // 256 * 128
    for left_ref, right_ref, part in ((grad_hidden_ref, x_ref, 0), (active_ref, grad_ref, 1)):

        @pl.when(step == part)
        def _():
            total_ref[:cut, :] = dot(left_ref[:, :cut], right_ref[...], 0, 0)
            total_ref[cut:, :] = dot(left_ref[:, cut:], right_ref[...], 0, 0)
            for i, out_ref in enumerate(outs):
                rows = total_ref[i * each : (i + 1) * each, :].astype(BF)
                out_ref[part * each : (part + 1) * each, :] = rows


def feed_grads(active, grad, grad_hidden, x):
    rows, hidden = active.shape
    model = grad.shape[1]
    block = (hidden // 4, model)
    return pl.pallas_call(
        feed_grads_kernel,
        grid=(2,),
        in_specs=[whole(a) for a in (active, grad, grad_hidden, x)],
        out_specs=[full(block)] * 8,
        out_shape=[shape_of(BF, *block)] * 8,
        scratch_shapes=[pltpu.VMEM((hidden, model), F32)],
        compiler_params=params(56),
        cost_estimate=pl.CostEstimate(
            flops=4 * rows * model * hidden, bytes_accessed=12 * rows * model, transcendentals=0
        ),
        name="feed_grads",
    )(active, grad, grad_hidden, x)


def middle_pull_kernel(
    out_ref, middle_ref, keep_ref, arrived_ref, across_ref, vec_ref, grad_ref, branch_ref, sum_ref
):
    rows = out_ref.shape[1]
    back = keep_ref[0] + arrived_ref[0, :rows, :].astype(F32) + across_ref[0].astype(F32)
    hat, scale = norm_stats(middle_ref[0])
    out = out_ref[0].astype(F32)
    grad = out + norm_pull(back, hat, scale, vec_ref[5:6, :])
    grad_ref[0] = grad
    branch = grad.astype(BF)
    branch_ref[0] = branch

    @pl.when(pl.program_id(0) == 0)
    def _():
        sum_ref[...] = jnp.zeros_like(sum_ref)

    for i, terms in enumerate((branch.astype(F32), back * hat, back, out)):
        sum_ref[i : i + 1, :] += jnp.sum(terms, axis=0, keepdims=True)


def middle_pull(out, middle, keep, arrived, across, vec):
    micro, rows, model = out.shape
    one = per((rows, model))
    return pl.pallas_call(
        middle_pull_kernel,
        grid=(micro,),
        in_specs=[one, one, one, per((2 * rows, model)), one, whole(vec)],
        out_specs=[one, one, full((4, model))],
        out_shape=[
            shape_of(F32, micro, rows, model), shape_of(BF, micro, rows, model),
            shape_of(F32, 4, model),
        ],
        name="middle_pull",
    )(out, middle, keep, arrived, across, vec)


def attend_pull_kernel(
    place_ref, g0, g1, g2, g3, weight_ref, qkv_ref, probs_ref, heads_ref, normed_ref,
    keep_ref, other_ref, send_ref, k0, k1, k2, k3, s0, s1, s2, s3, bias_ref,
    grad_ref, grad_qkv_ref, total_ref, sum_ref,
):
    count = probs_ref.shape[1]
    width = count * HEAD_DIM
    rows = g0.shape[1]
    model = g0.shape[2]
    scale = HEAD_DIM ** (-0.5)
    step = pl.program_id(0)
    for i, block_ref in enumerate((g0, g1, g2, g3)):
        grad_ref[i * rows : (i + 1) * rows, :] = block_ref[0]
    grad_heads = dot(grad_ref[...], weight_ref[3 * width :, :], 1, 1).astype(BF)
    for head in range(count):
        lanes = [slice(i * width + head * HEAD_DIM, i * width + (head + 1) * HEAD_DIM) for i in range(3)]
        queries, keys, values = [qkv_ref[0, :, part] for part in lanes]
        probs = probs_ref[0, head]
        grad = grad_heads[:, lanes[0]]
        delta = jnp.sum(
            grad.astype(F32) * heads_ref[0, :, lanes[0]].astype(F32), axis=1, keepdims=True
        )
        grad_scores = (probs.astype(F32) * (dot(grad, values, 1, 1) - delta)).astype(BF)
        grad_qkv_ref[:, lanes[0]] = (scale * dot(grad_scores, keys, 1, 0)).astype(BF)
        grad_qkv_ref[:, lanes[1]] = (scale * dot(grad_scores, queries, 0, 0)).astype(BF)
        grad_qkv_ref[:, lanes[2]] = dot(probs, grad, 0, 0).astype(BF)
    write_halves(dot(grad_qkv_ref[...], weight_ref[: 3 * width, :], 1, 0), rows, keep_ref, other_ref, send_ref)
    qkv_part = dot(grad_qkv_ref[...], normed_ref[0], 0, 0)
    out_part = dot(heads_ref[0], grad_ref[...], 0, 0)
    sums = jnp.sum(grad_qkv_ref[...].astype(F32), axis=0, keepdims=True)

    @pl.when(step == 0)
    def _():
        total_ref[: 3 * width, :] = qkv_part
        total_ref[3 * width :, :] = out_part
        sum_ref[...] = jnp.broadcast_to(sums, sum_ref.shape)

    @pl.when(step > 0)
    def _():
        total_ref[: 3 * width, :] += qkv_part
        total_ref[3 * width :, :] += out_part
        sum_ref[...] += sums

    @pl.when(step == pl.num_programs(0) - 1)
    def _():
        z, y, ctx = place_ref[0], place_ref[1], place_ref[2]
        for k, pair in zip(SHIFTS, ((k0, s0), (k1, s1), (k2, s2), (k3, s3))):
            region = lax.rem(z + 4 - k, 4) * width
            for out_ref, half in zip(pair, (y, 1 - y)):
                start = pl.multiple_of(region + BODY * half, HEAD_DIM)
                out_ref[:BODY, :] = total_ref[pl.ds(start, BODY), :].astype(BF)
                start = pl.multiple_of(region + 2 * BODY + HALO * half, HALO)
                out_ref[BODY:, :] = total_ref[pl.ds(start, HALO), :].astype(BF)
        own = head_places((width, model), 0, ctx)
        hot = (lax.broadcasted_iota(jnp.int32, (width, model), 1) == own).astype(F32)
        for i, part in enumerate((0, 2)):
            line = lax.dot_general(
                sum_ref[:, part * width : (part + 1) * width],
                hot,
                (((1,), (0,)), ((), ())),
                preferred_element_type=F32,
                precision=lax.Precision.HIGHEST,
            )
            bias_ref[i : i + 1, :] = line[0:1]


def attend_pull(place, grads, weight, qkv, probs, heads, normed):
    micro, rows, model = grads[0].shape
    group = 4 * rows
    width = heads.shape[2]
    count = width // HEAD_DIM
    block = (BODY + HALO, model)
    one = per((rows, model))
    return pl.pallas_call(
        attend_pull_kernel,
        grid=(micro,),
        in_specs=[SCALARS] + [one] * 4 + [
            whole(weight), per((group, 3 * width)), per((count, group, group)),
            per((group, width)), per((group, model)),
        ],
        out_specs=[one, one, per((2 * rows, model))] + [full(block)] * 8 + [full((2, model))],
        out_shape=[
            shape_of(F32, micro, rows, model), shape_of(BF, micro, rows, model),
            shape_of(BF, micro, 2 * rows, model),
        ] + [shape_of(BF, *block)] * 8 + [shape_of(F32, 2, model)],
        scratch_shapes=[
            pltpu.VMEM((group, model), BF), pltpu.VMEM((group, 3 * width), BF),
            pltpu.VMEM((4 * width, model), F32), pltpu.VMEM((8, 3 * width), F32),
        ],
        compiler_params=params(60),
        cost_estimate=pl.CostEstimate(
            flops=2 * micro * group * model * 10 * width,
            bytes_accessed=12 * micro * group * model,
            transcendentals=0,
        ),
        name="attend_pull",
    )(place, *grads, weight, qkv, probs, heads, normed)


def input_pull_kernel(
    x_ref, grad_ref, keep_ref, arrived_ref, across_ref, vec_ref, out_ref, sum_ref
):
    rows = x_ref.shape[1]
    back = keep_ref[0] + arrived_ref[0, :rows, :].astype(F32) + across_ref[0].astype(F32)
    hat, scale = norm_stats(x_ref[0].astype(F32))
    out = grad_ref[0] + norm_pull(back, hat, scale, vec_ref[0:1, :])
    out_ref[0] = jnp.transpose(out).astype(BF)

    @pl.when(pl.program_id(0) == 0)
    def _():
        sum_ref[...] = jnp.zeros_like(sum_ref)

    for i, terms in enumerate((back * hat, back)):
        sum_ref[i : i + 1, :] += jnp.sum(terms, axis=0, keepdims=True)


def input_pull(x, grad, keep, arrived, across, vec):
    micro, rows, model = x.shape
    one = per((rows, model))
    out, sums = pl.pallas_call(
        input_pull_kernel,
        grid=(micro,),
        in_specs=[one, one, one, per((2 * rows, model)), one, whole(vec)],
        out_specs=[per((model, rows)), full((2, model))],
        out_shape=[shape_of(BF, micro, model, rows), shape_of(F32, 2, model)],
        name="input_pull",
    )(x, grad, keep, arrived, across, vec)
    return out.transpose(0, 2, 1), sums


def mixed_kernel(middle_ref, keep_ref, arrived_ref, across_ref, vec_ref, out_ref):
    rows = middle_ref.shape[1]
    feed = keep_ref[0] + arrived_ref[0, :rows, :].astype(F32) + across_ref[0].astype(F32)
    out_ref[0] = jnp.transpose(middle_ref[0] + feed + vec_ref[7:8, :]).astype(BF)


def mixed_rows(middle, keep, arrived, across, vec):
    micro, rows, model = middle.shape
    one = per((rows, model))
    return pl.pallas_call(
        mixed_kernel,
        grid=(micro,),
        in_specs=[one, one, per((2 * rows, model)), one, whole(vec)],
        out_specs=per((model, rows)),
        out_shape=shape_of(BF, micro, model, rows),
        name="mixed_rows",
    )(middle, keep, arrived, across, vec).transpose(0, 2, 1)


def row_places(segments, rows):
    ctx = lax.axis_index("ctx")
    ranks = [ctx ^ j for j in BLOCKS]
    starts = segments[:, 0].reshape(-1, 4, rows).transpose(1, 0, 2)
    starts = jnp.concatenate([pick(starts, r) for r in ranks], axis=1)
    places = jnp.concatenate([r * rows + jnp.arange(rows, dtype=jnp.int32) for r in ranks])
    places = jnp.broadcast_to(places[None], starts.shape)
    return jnp.stack([starts, places] + [places] * 6, axis=1)


def own_up_bias(lines, order, width):
    table = lines[16:].reshape(order.shape[0], 4, width).transpose(1, 0, 2)
    return reorder(pick(table, lax.axis_index("ctx")), order).reshape(1, -1)


def vector_parts(first_sums, bias_sums, sums, up_sum, order, width):
    up_rows = reorder_back(up_sum.reshape(order.shape[0], width), order)
    mine = (jnp.arange(4) == lax.axis_index("ctx")).astype(F32)
    table = jnp.concatenate([first_sums, bias_sums, sums], axis=0)
    up_part = (up_rows[:, None, :] * mine[None, :, None]).reshape(-1)
    return jnp.concatenate([table.reshape(-1), up_part])


def flat(values):
    return values.reshape(-1, values.shape[-1])


def halo_pairs(back):
    pairs = []
    for p in range(8):
        for c in range(4):
            to = (c - 1) % 4 if (p % 2 == 1) != back else (c + 1) % 4
            pairs.append((p * 4 + c, p * 4 + to))
    return pairs


def aligned_block(w_attn, vectors, odd, ctx):
    turned = row_major(w_attn.T)
    width, model = turned.shape
    table = ctx_table(vectors, ctx).astype(BF).reshape(3, model // 2)
    edge = jnp.where(odd, turned[:HALO], turned[width - HALO :])
    halo = lax.ppermute(edge, BOTH, halo_pairs(False))
    none = jnp.zeros_like(halo)
    wide = jnp.concatenate(
        [jnp.where(odd, none, halo), turned, jnp.where(odd, halo, none)], axis=0
    )
    shift = HALO * odd.astype(jnp.int32)
    body = lax.dynamic_slice_in_dim(wide, HALO - 8 * ctx + shift, BODY, axis=0)
    extra = lax.dynamic_slice_in_dim(wide, width + shift, HALO, axis=0)
    extra = jnp.where(ctx == 3, extra, jnp.zeros_like(extra))
    lines = jnp.pad(table, ((0, 13), (0, model // 2)))
    return jnp.concatenate([body, extra, lines], axis=0)


def aligned_owned(own, odd, ctx, width):
    last = ctx == 3
    body, extra = own[:BODY], own[BODY:]
    tail = jnp.where(last, extra, body[BODY - HALO :])
    halo = lax.ppermute(jnp.where(odd, tail, body[:HALO]), BOTH, halo_pairs(True))
    halo = jnp.where(last & jnp.logical_not(odd), extra, halo)
    wide = jnp.where(
        odd, jnp.concatenate([halo, body], axis=0), jnp.concatenate([body, halo], axis=0)
    )
    return lax.dynamic_slice_in_dim(wide, 8 * ctx, width, axis=0)


def vector_rows(part, ctx):
    each = part.shape[0] // 32
    table = part.reshape(8, 4, each).transpose(1, 0, 2)
    table = jnp.stack([pick(table, ctx ^ j) for j in BLOCKS])
    mine = table[:2] + lax.ppermute(table[2:], "ctx", CORE_PAIRS)
    return mine[0] + lax.ppermute(mine[1], "ctx", CHIP_PAIRS)


def vector_sides(mine, y):
    sides = mine.reshape(4, 2, -1).transpose(1, 0, 2)
    return pick(sides, y) + lax.ppermute(pick(sides, 1 - y), "dp", SIDE_PAIRS)


def vector_owned(mine, z):
    total = pick(mine, z)
    for k in (1, 2, 3):
        total = total + to_shift(pick(mine, (z - k) % 4)[None], k, True)[0]
    return total


def both(keep, arrived):
    return keep.astype(F32) + arrived.astype(F32)


def aligned(tokens, cotangent, w_attn, w_up, w_down, vectors, segments):
    rows = tokens.shape[1]
    width = w_attn.shape[1]
    ctx, dp = lax.axis_index("ctx"), lax.axis_index("dp")
    z, y = dp // 2, dp % 2
    odd = y == 1
    place = jnp.stack([z, y, ctx]).astype(jnp.int32)
    order = jnp.stack(dp_order(z, y))
    tokens, cotangent = row_major(tokens), row_major(cotangent)
    row_info = row_places(segments, rows)
    feed = jnp.concatenate([w_up.T, w_down], axis=0)

    n0 = aligned_block(w_attn, vectors, odd, ctx)
    n0, t0, place, row_info = hold([n0, tokens, place, row_info])
    (b0,) = hold([feed], n0)
    n1, n3, s0, t1, c0 = to_shift(n0, 1), to_shift(n0, 3), to_side(n0), to_chip(t0), to_side(b0)
    n0, n1, n3, s0, t0, t1, g0, b0, c0 = hold([n0, n1, n3, s0, t0, t1, cotangent, b0, c0])
    n2, s1, s3, g1 = to_shift(n0, 2), to_side(n1), to_side(n3), to_chip(g0)
    n0, n1, n2, n3, s0, s1, s3, t0, t1, g0, g1, b0 = hold(
        [n0, n1, n2, n3, s0, s1, s3, t0, t1, g0, g1, b0]
    )
    s2, b1, t2, t3 = to_side(n2), to_shift(b0, 1), to_core(t0), to_core(t1)
    n0, n1, n2, n3, s0, s1, s2, s3, t0, t1, t2, t3, g0, g1, b0, b1 = hold(
        [n0, n1, n2, n3, s0, s1, s2, s3, t0, t1, t2, t3, g0, g1, b0, b1]
    )
    b3, c1, g2, g3 = to_shift(b0, 3), to_side(b1), to_core(g0), to_core(g1)
    normed_one, qkv, probs, heads, weight, lines, rest, keep, other, away = attend(
        place, [t0, t1, t2, t3], [n0, n1, n3, n2], [s0, s1, s3, s2], row_info
    )
    away, keep, other, b0, b1, b3, c1, g0, g1, g2, g3 = hold(
        [away, keep, other, b0, b1, b3, c1, g0, g1, g2, g3]
    )
    arrived = to_core(away)
    away, arrived, keep, b0, b3 = hold([half_sum(other, arrived), arrived, keep, b0, b3])
    across, b2, c3 = to_chip(away), to_shift(b0[:CUT], 2), to_side(b3)
    across, arrived, keep, b0, b2, c3 = hold([across, arrived, keep, b0, b2, c3])
    middle, h0 = middle_rows(tokens, keep, arrived, across, lines)
    h0, middle, b0, b2 = hold([h0, middle, b0, b2])
    h1, h2, d2, c2 = to_chip(h0), to_core(h0), to_shift(b0[CUT:], 2), to_side(b2)
    h0, h1, h2, d2, c2 = hold([h0, h1, h2, d2, c2])
    h3, e2 = to_core(h1), to_side(d2)
    up_bias = own_up_bias(rest, order, width)
    h0, h1, h2, h3, b0, c0, b1, c1, b3, c3, b2, c2, d2, e2, up_bias = hold(
        [h0, h1, h2, h3, b0, c0, b1, c1, b3, c3, b2, c2, d2, e2, up_bias]
    )
    x_all, grad_all, active, grad_hidden, *halves, up_sum = feed_forward(
        [h0, h1, h2, h3], [g0, g1, g2, g3], [b0, c0, b1, c1, b3, c3, b2, c2, d2, e2], up_bias
    )
    feed_keep, feed_other, feed_away, keep, other, away = halves

    arrived = to_core(away)
    away, arrived, keep, active = hold([half_sum(other, arrived), arrived, keep, active])
    across, feed_arrived = to_chip(away), to_core(feed_away)
    p0, q0, p1, q1, p3, q3, p2, q2 = feed_grads(
        flat(active), flat(grad_all), flat(grad_hidden), flat(x_all)
    )
    across, arrived, keep, q2, feed_arrived = hold([across, arrived, keep, q2, feed_arrived])
    grad_middle, h0, sums = middle_pull(cotangent, middle, keep, arrived, across, lines)
    h0, q2, grad_middle = hold([h0, q2, grad_middle])
    h1, h2, q2 = to_chip(h0), to_core(h0), to_side(q2)
    h0, h1, h2, q2, q1, q3 = hold([h0, h1, h2, q2, q1, q3])
    h3, p2 = to_core(h1), both(p2, q2)
    h0, h1, h2, h3, p2, q1, q3, q0 = hold([h0, h1, h2, h3, p2.astype(BF), q1, q3, q0])
    r2, q3, q1 = to_shift(p2, 2, True), to_side(q3), to_side(q1)
    keep, other, away, *blocks, bias_sums = attend_pull(
        place, [h0, h1, h2, h3], weight, qkv, probs, heads, normed_one
    )
    away, r2, q3, q1, q0, p0, *blocks = hold([away, r2, q3, q1, q0, p0] + blocks)
    k0, k1, k3, k2, l0, l1, l3, l2 = blocks
    p3, p1 = both(p3, q3).astype(BF), both(p1, q1).astype(BF)
    arrived, r3, q0 = to_core(away), to_shift(p3, 3, True), to_side(q0)
    away, arrived, keep, r3, q0, p1, k2, l2 = hold(
        [half_sum(other, arrived), arrived, keep, r3, q0, p1, k2, l2]
    )
    across, r1, l2 = to_chip(away), to_shift(p1, 1, True), to_side(l2)
    across, arrived, keep, r1, k2, l1, l3, feed_away = hold(
        [
            across, arrived, keep, r1, both(k2, l2).astype(BF), l1, l3,
            half_sum(feed_other, feed_arrived),
        ]
    )
    k2, l1, l3, feed_across = to_shift(k2, 2, True), to_side(l1), to_side(l3), to_chip(feed_away)
    input_grad, first_sums = input_pull(tokens, grad_middle, keep, arrived, across, lines)
    part = vector_parts(first_sums, bias_sums, sums, up_sum, order, width)
    part = vector_rows(part, ctx)
    k2, k1, k3, l0, feed_across, part, input_grad = hold(
        [
            k2, both(k1, l1).astype(BF), both(k3, l3).astype(BF), l0, feed_across, part,
            input_grad,
        ]
    )
    k1, k3, l0 = to_shift(k1, 1, True), to_shift(k3, 3, True), to_side(l0)
    mixed = mixed_rows(middle, feed_keep, feed_arrived, feed_across, lines)
    feed_owned = both(p0, q0) + r1.astype(F32) + r2.astype(F32) + r3.astype(F32)
    sides = vector_sides(part, y)
    k1, k2, k3, l0, sides, mixed, feed_owned = hold([k1, k2, k3, l0, sides, mixed, feed_owned])
    own = both(k0, l0) + k1.astype(F32) + k2.astype(F32) + k3.astype(F32)
    attn_owned = aligned_owned(own, odd, ctx, width)
    return (
        mixed, input_grad, attn_owned.T, feed_owned[:width].T, feed_owned[width:],
        vector_owned(sides, z),
    )


def plain(tokens, cotangent, w_attn, w_up, w_down, vectors, segments):
    micro, rows, model = tokens.shape
    width = w_attn.shape[1]
    ctx = lax.axis_index("ctx")
    last = ctx == lax.axis_size("ctx") - 1
    place = jnp.stack([jnp.zeros((), ctx.dtype), jnp.zeros((), ctx.dtype), ctx])
    order = jnp.arange(lax.axis_size("dp"))
    table = lax.all_gather(w_attn.T, BOTH, axis=0, tiled=True)
    lines = lax.all_gather(vectors, BOTH, axis=0, tiled=True).reshape(24, model // 2)
    lines = jnp.pad(lines, ((0, 0), (0, model // 2)))
    near, side = [], []
    for region in (-k % 4 for k in SHIFTS):
        part = head_rows(table[region * model : (region + 1) * model], ctx, last)
        for blocks, half in ((near, 0), (side, 1)):
            line = 3 * (2 * region + half)
            blocks.append(
                jnp.concatenate(
                    [
                        part[BODY * half : BODY * (half + 1)],
                        part[2 * BODY + HALO * half : 2 * BODY + HALO * (half + 1)],
                        jnp.pad(lines[line : line + 3], ((0, 13), (0, 0))),
                    ],
                    axis=0,
                )
            )
    up = lax.all_gather(w_up.T, "dp", axis=0, tiled=True)
    down = lax.all_gather(w_down, "dp", axis=0, tiled=True)
    each = up.shape[0] // 8
    blocks = [
        jnp.concatenate([w[i * each : (i + 1) * each] for w in (up, down)], axis=0)
        for i in range(8)
    ]
    blocks = blocks[:6] + [b[:CUT] for b in blocks[6:]] + [b[CUT:] for b in blocks[6:]]

    normed_one, qkv, probs, heads, weight, lines, rest, *halves = attend(
        place, row_gather(tokens), near, side, row_places(segments, rows)
    )
    middle, normed_two = middle_rows(tokens, *row_scatter(*halves), lines)
    x_all, grad_all, active, grad_hidden, *halves, up_sum = feed_forward(
        row_gather(normed_two), row_gather(cotangent), blocks, own_up_bias(rest, order, width)
    )
    mixed = mixed_rows(middle, *row_scatter(*halves[:3]), lines)
    grad_middle, branch, sums = middle_pull(cotangent, middle, *row_scatter(*halves[3:]), lines)
    parts = feed_grads(flat(active), flat(grad_all), flat(grad_hidden), flat(x_all))
    up_owned, down_owned = [
        lax.psum_scatter(
            jnp.concatenate([p[i * each : (i + 1) * each] for p in parts], axis=0),
            "dp", scatter_dimension=0, tiled=True,
        ).astype(F32)
        for i in range(2)
    ]
    *halves, k0, k1, k2, k3, s0, s1, s2, s3, bias_sums = attend_pull(
        place, row_gather(branch), weight, qkv, probs, heads, normed_one
    )
    input_grad, first_sums = input_pull(tokens, grad_middle, *row_scatter(*halves), lines)
    parts = []
    for region in range(4):
        at = SHIFTS.index(-region % 4)
        first, second = (k0, k1, k2, k3)[at], (s0, s1, s2, s3)[at]
        part = [first[:BODY], second[:BODY], first[BODY:], second[BODY:]]
        parts.append(head_rows_back(jnp.concatenate(part, axis=0), ctx, last))
    attn_owned = lax.psum_scatter(
        jnp.concatenate(parts, axis=0), BOTH, scatter_dimension=0, tiled=True
    ).astype(F32)
    part = vector_parts(first_sums, bias_sums, sums, up_sum, order, width)
    vector_grad = lax.psum_scatter(part, BOTH, scatter_dimension=0, tiled=True)
    return (mixed, input_grad, attn_owned.T, up_owned.T, down_owned, vector_grad)


def shards(*arrays):
    fits = lax.axis_size("dp") == 8 and lax.axis_size("ctx") == 4
    return (aligned if fits and arrays[2].shape == (1088, 136) else plain)(*arrays)


def solution(mesh):
    return jax.shard_map(
        shards,
        mesh=mesh,
        in_specs=(
            P(None, BOTH, None),
            P(None, BOTH, None),
            P(None, BOTH),
            P(None, BOTH),
            P(BOTH, None),
            P(BOTH),
            P(None, "dp", None),
        ),
        out_specs=(
            P(None, BOTH, None),
            P(None, BOTH, None),
            P(None, BOTH),
            P(None, BOTH),
            P(BOTH, None),
            P(BOTH),
        ),
        check_vma=False,
    )
```

```python
from functools import partial

import jax
import jax.numpy as jnp
from jax import lax
from jax.experimental import pallas as pl
from jax.experimental.layout import Layout, with_layout_constraint
from jax.experimental.pallas import tpu as pltpu
from jax.sharding import PartitionSpec as P

HEAD_DIM = 64
HALO = 32
BODY = 128
NEG_FILL = -1e30
EPSILON = 1e-05
BF = jnp.bfloat16
F32 = jnp.float32
BOTH = ("dp", "ctx")
CORE_PAIRS = [(0, 1), (1, 0), (2, 3), (3, 2)]
CHIP_PAIRS = [(0, 2), (2, 0), (1, 3), (3, 1)]
BLOCKS = (0, 2, 1, 3)
SHIFTS = (0, 1, 3, 2)
ORDER = ((2, 1), (2, 0), (0, 0), (0, 1), (1, 0), (1, 1), (3, 0), (3, 1))
THIRDS = (64, 160)
CUT = 144
BACK_CUT = 112
SIDE_PAIRS = [(p, p ^ 1) for p in range(8)]


def shift_pairs(step):
    return [(z * 2 + y, ((z + step) % 4) * 2 + y) for z in range(4) for y in range(2)]


def dot(left, right, left_dim, right_dim):
    return lax.dot_general(
        left, right, (((left_dim,), (right_dim,)), ((), ())), preferred_element_type=F32
    )


def norm_stats(values):
    centred = values - jnp.mean(values, axis=-1, keepdims=True)
    scale = lax.rsqrt(jnp.mean(centred * centred, axis=-1, keepdims=True) + EPSILON)
    return centred * scale, scale


def norm_pull(grad, hat, scale, gain):
    grad_hat = grad * gain
    along = jnp.mean(grad_hat * hat, axis=-1, keepdims=True)
    return scale * (grad_hat - jnp.mean(grad_hat, axis=-1, keepdims=True) - hat * along)


def row_major(value):
    return with_layout_constraint(value, Layout(tuple(range(value.ndim))))


def send(value, axes, pairs):
    rows = value.shape[-2]
    if rows % 16:
        return lax.ppermute(value, axes, pairs)
    cut = value.reshape(value.shape[:-2] + (rows // 16, 16, value.shape[-1]))
    return lax.ppermute(cut, axes, pairs).reshape(value.shape)


def hold(values, *others):
    return lax.optimization_barrier(tuple(values) + tuple(others))[: len(values)]


def to_core(value):
    return send(value, "ctx", CORE_PAIRS)


def to_chip(value):
    return send(value, "ctx", CHIP_PAIRS)


def to_side(value):
    return send(value, "dp", SIDE_PAIRS)


def to_shift(value, step, back=False):
    pairs = shift_pairs(step)
    return send(value, "dp", [(b, a) for a, b in pairs] if back else pairs)


def row_gather(mine):
    across = to_chip(mine)
    return [mine, across, to_core(mine), to_core(across)]


def half_sum(other, arrived):
    rows = other.shape[1]
    return (other.astype(F32) + arrived[:, rows:].astype(F32)).astype(BF)


def row_scatter(keep, other, away):
    arrived = to_core(away)
    return keep, arrived, to_chip(half_sum(other, arrived))


def dp_order(z, y):
    return [((z - k) % 4) * 2 + (y ^ s) for k, s in ORDER]


def pick(stacked, index):
    return lax.dynamic_index_in_dim(stacked, index, axis=0, keepdims=False)


def reorder(table, order):
    hot = (order[:, None] == jnp.arange(table.shape[0])[None, :]).astype(F32)
    return jnp.sum(hot[:, :, None] * table[None], axis=1)


def reorder_back(table, order):
    hot = (order[:, None] == jnp.arange(table.shape[0])[None, :]).astype(F32)
    return jnp.sum(hot[:, :, None] * table[:, None, :], axis=0)


def ctx_table(mine, ctx):
    across = lax.ppermute(mine[None], "ctx", CHIP_PAIRS)
    pair = jnp.concatenate([mine[None], across], axis=0)
    table = jnp.concatenate([pair, lax.ppermute(pair, "ctx", CORE_PAIRS)], axis=0)
    return reorder_back(table.astype(F32), jnp.stack([ctx ^ j for j in BLOCKS]))


def head_rows(table, ctx, last):
    middle = 8 * HEAD_DIM
    first = lax.dynamic_slice_in_dim(table, 128 * ctx, 128, axis=0)
    second = lax.dynamic_slice_in_dim(table, middle + HEAD_DIM + 128 * ctx, 128, axis=0)
    mid = table[middle : middle + HEAD_DIM]
    return jnp.concatenate([first, second, jnp.where(last, mid, jnp.zeros_like(mid))], axis=0)


def head_rows_back(mine, ctx, last):
    middle = 8 * HEAD_DIM
    table = jnp.zeros((2 * middle + HEAD_DIM,) + mine.shape[1:], mine.dtype)
    table = lax.dynamic_update_slice_in_dim(table, mine[:128], 128 * ctx, axis=0)
    table = lax.dynamic_update_slice_in_dim(
        table, mine[128:256], middle + HEAD_DIM + 128 * ctx, axis=0
    )
    mid = jnp.where(last, mine[256:], jnp.zeros_like(mine[256:]))
    return lax.dynamic_update_slice_in_dim(table, mid, middle, axis=0)


def gelu_parts(hidden):
    factor = 0.7978845608028654
    square = hidden * hidden
    bent = jnp.tanh(factor * hidden * (1.0 + 0.044715 * square))
    active = 0.5 * hidden * (1.0 + bent)
    slope = 0.5 * (1.0 + bent) + 0.5 * hidden * (1.0 - bent * bent) * factor * (
        1.0 + 3 * 0.044715 * square
    )
    return active, slope


def full(shape):
    return pl.BlockSpec(shape, lambda *_: (0,) * len(shape))


def per(shape, step=1):
    return pl.BlockSpec((1,) + shape, lambda i: (i // step,) + (0,) * len(shape))


def params(mib):
    return pltpu.CompilerParams(vmem_limit_bytes=mib * 1024 * 1024)


def whole(array):
    return full(array.shape)


SCALARS = pl.BlockSpec(memory_space=pltpu.SMEM)


def shape_of(dtype, *dims):
    return jax.ShapeDtypeStruct(dims, dtype)


def head_places(shape, axis, ctx):
    own = lax.broadcasted_iota(jnp.int32, shape, axis)
    middle = 8 * HEAD_DIM
    shift = jnp.where(own < BODY, BODY * ctx, middle + HEAD_DIM - BODY + BODY * ctx)
    shift = jnp.where(own < 2 * BODY, shift, middle - 2 * BODY)
    return jnp.where((own < 2 * BODY) | (ctx == 3), own + shift, -1)


def write_halves(values, rows, keep_ref, other_ref, send_ref):
    keep_ref[0] = values[:rows]
    other_ref[0] = values[rows : 2 * rows].astype(BF)
    send_ref[0] = values[2 * rows :].astype(BF)


def assemble(place_ref, near, side, weight_ref):
    width = weight_ref.shape[0] // 4
    z, y = place_ref[0], place_ref[1]
    for k, pair in zip(SHIFTS, zip(near, side)):
        region = lax.rem(z + 4 - k, 4) * width
        for block_ref, half in zip(pair, (y, 1 - y)):
            to = pl.multiple_of(region + BODY * half, HEAD_DIM)
            weight_ref[pl.ds(to, BODY), :] = block_ref[:BODY, :]
            to = pl.multiple_of(region + 2 * BODY + HALO * half, HALO)
            weight_ref[pl.ds(to, HALO), :] = block_ref[BODY : BODY + HALO, :]


def write_mask(row_ref, mask_ref):
    row = row_ref[0].astype(F32)
    first, own = row[0:1], row[1:2]
    square = (128, row.shape[1])
    first_col = jnp.transpose(jnp.broadcast_to(first, square))[:, :1]
    own_col = jnp.transpose(jnp.broadcast_to(own, square))[:, :1]
    allowed = (own <= own_col) & (first == first_col)
    mask_ref[...] = jnp.where(allowed, 0.0, NEG_FILL)


def attend_kernel(
    place_ref, x0, x1, x2, x3, n0, n1, n2, n3, s0, s1, s2, s3, row_ref,
    normed_ref, qkv_ref, log_ref, heads_ref, vec_ref, line_ref,
    keep_ref, other_ref, send_ref, weight_ref, mask_ref, bias_ref,
):
    width = heads_ref.shape[2]
    count = width // HEAD_DIM
    model = vec_ref.shape[1]
    part = model // 2
    rows = x0.shape[1]

    @pl.when(pl.program_id(0) == 0)
    def _():
        z, y, ctx = place_ref[0], place_ref[1], place_ref[2]
        assemble(place_ref, (n0, n1, n2, n3), (s0, s1, s2, s3), weight_ref)
        for k, pair in zip(SHIFTS, ((n0, s0), (n1, s1), (n2, s2), (n3, s3))):
            owner = lax.rem(z + 4 - k, 4)
            for block_ref, half in zip(pair, (y, 1 - y)):
                lines = block_ref[BODY + HALO :, :].astype(F32)
                for i in range(3):
                    line_ref[pl.ds(3 * (2 * owner + half) + i, 1), :] = lines[i : i + 1, :part]
        for i in range(8):
            vec_ref[i : i + 1, :part] = line_ref[2 * i : 2 * i + 1, :]
            vec_ref[i : i + 1, part:] = line_ref[2 * i + 1 : 2 * i + 2, :]
        own = head_places((model, width), 1, ctx)
        hot = (lax.broadcasted_iota(jnp.int32, (model, width), 0) == own).astype(F32).astype(BF)
        own_vec = dot(vec_ref[...].astype(BF), hot, 1, 0)
        bias_ref[:, :width] = own_vec[2:3]
        bias_ref[:, width : 2 * width] = jnp.zeros((1, width), F32)
        bias_ref[:, 2 * width :] = own_vec[3:4]

    gain, bias = vec_ref[0:1, :], vec_ref[1:2, :]
    for i, x_ref in enumerate((x0, x1, x2, x3)):
        hat, _ = norm_stats(x_ref[0].astype(F32))
        normed_ref[0, i * rows : (i + 1) * rows, :] = (hat * gain + bias).astype(BF)
    normed = normed_ref[0]
    qkv_ref[0] = (dot(normed, weight_ref[: 3 * width, :], 1, 1) + bias_ref[...]).astype(BF)
    write_mask(row_ref, mask_ref)
    for head in range(count):
        lanes = [slice(i * width + head * HEAD_DIM, i * width + (head + 1) * HEAD_DIM) for i in range(3)]
        queries, keys, values = [qkv_ref[0, :, part] for part in lanes]
        queries = queries * jnp.asarray(HEAD_DIM ** (-0.5), BF)
        scores = dot(queries, keys, 1, 1) + mask_ref[...]
        top = jnp.max(scores, axis=1, keepdims=True)
        weights = jnp.exp(scores - top)
        total = jnp.sum(weights, axis=1, keepdims=True)
        probs = (weights * (1.0 / total)).astype(BF)
        log_ref[0, :, head : head + 1] = top + jnp.log(total)
        heads_ref[0, :, lanes[0]] = dot(probs, values, 1, 0).astype(BF)
    branch = dot(heads_ref[0], weight_ref[3 * width :, :], 1, 0)
    write_halves(branch, rows, keep_ref, other_ref, send_ref)


def attend(place, blocks, near, side, row):
    micro, rows, model = blocks[0].shape
    group = 4 * rows
    width = 2 * (BODY + HALO)
    count = width // HEAD_DIM
    return pl.pallas_call(
        attend_kernel,
        grid=(micro,),
        in_specs=[SCALARS] + [per((rows, model))] * 4
        + [whole(b) for b in near + side] + [per(row.shape[1:])],
        out_specs=[
            per((group, model)), per((group, 3 * width)), per((group, 128)),
            per((group, width)), full((8, model)), full((24, model // 2)),
            per((rows, model)), per((rows, model)), per((2 * rows, model)),
        ],
        out_shape=[
            shape_of(BF, micro, group, model), shape_of(BF, micro, group, 3 * width),
            shape_of(F32, micro, group, 128), shape_of(BF, micro, group, width),
            shape_of(F32, 8, model),
            shape_of(F32, 24, model // 2), shape_of(F32, micro, rows, model),
            shape_of(BF, micro, rows, model), shape_of(BF, micro, 2 * rows, model),
        ],
        scratch_shapes=[
            pltpu.VMEM((4 * width, model), BF), pltpu.VMEM((group, group), F32),
            pltpu.VMEM((1, 3 * width), F32),
        ],
        compiler_params=params(56),
        cost_estimate=pl.CostEstimate(
            flops=2 * micro * group * model * 4 * width,
            bytes_accessed=12 * micro * group * model,
            transcendentals=micro * count * group * group,
        ),
        name="attend",
    )(place, *blocks, *near, *side, row)


def middle_kernel(x_ref, keep_ref, arrived_ref, across_ref, vec_ref, middle_ref, normed_ref):
    rows = x_ref.shape[1]
    branch = keep_ref[0] + arrived_ref[0, :rows, :].astype(F32) + across_ref[0].astype(F32)
    middle = x_ref[0].astype(F32) + branch + vec_ref[4:5, :]
    middle_ref[0] = middle
    hat, _ = norm_stats(middle)
    normed_ref[0] = (hat * vec_ref[5:6, :] + vec_ref[6:7, :]).astype(BF)


def middle_rows(x, keep, arrived, across, vec):
    micro, rows, model = x.shape
    one = per((rows, model))
    return pl.pallas_call(
        middle_kernel,
        grid=(micro,),
        in_specs=[one, one, per((2 * rows, model)), one, whole(vec)],
        out_specs=[one, one],
        out_shape=[shape_of(F32, micro, rows, model), shape_of(BF, micro, rows, model)],
        name="middle_rows",
    )(x, keep, arrived, across, vec)


def stack_parts(parts, refs, low, high, to_ref):
    for (block, start), part_ref in zip(parts, refs):
        first, last = max(start, low), min(start + part_ref.shape[0], high)
        to = block * (high - low) - low
        to_ref[to + first : to + last, :] = part_ref[first - start : last - start, :]


def parts_between(blocks, low, high):
    parts, arrays = [], []
    for block, pieces in enumerate(blocks):
        start = 0
        for piece in pieces:
            if start < high and start + piece.shape[0] > low:
                parts.append((block, start))
                arrays.append(piece)
            start += piece.shape[0]
    return parts, arrays


def pull_kernel(parts, g0, g1, g2, g3, *rest):
    *part_refs, pull_ref, grad_ref, down_ref = rest
    rows = g0.shape[1]
    each = down_ref.shape[0] // 8

    @pl.when(pl.program_id(0) == 0)
    def _():
        stack_parts(parts, part_refs, 0, each, down_ref)

    for i, block_ref in enumerate((g0, g1, g2, g3)):
        grad_ref[i * rows : (i + 1) * rows, :] = block_ref[0]
    pull_ref[0] = dot(grad_ref[...], down_ref[...], 1, 1).astype(BF)


def feed_pull(grads, blocks):
    micro, rows, model = grads[0].shape
    group = 4 * rows
    each = sum(p.shape[0] for p in blocks[0]) // 2
    hidden = 8 * each
    parts, arrays = parts_between(blocks, 0, each)
    return pl.pallas_call(
        partial(pull_kernel, parts),
        grid=(micro,),
        in_specs=[per((rows, model))] * 4 + [whole(b) for b in arrays],
        out_specs=per((group, hidden)),
        out_shape=shape_of(BF, micro, group, hidden),
        scratch_shapes=[pltpu.VMEM((group, model), BF), pltpu.VMEM((hidden, model), BF)],
        compiler_params=params(56),
        cost_estimate=pl.CostEstimate(
            flops=2 * micro * group * model * hidden,
            bytes_accessed=8 * micro * group * model,
            transcendentals=0,
        ),
        name="feed_pull",
    )(*grads, *arrays)


def feed_kernel(parts, x0, x1, x2, x3, pull_ref, bias_ref, *rest):
    *part_refs, active_ref, grad_hidden_ref, keep_ref, other_ref, send_ref, sum_ref, x_ref, up_ref = rest
    rows = x0.shape[1]
    each = up_ref.shape[0] // 8

    @pl.when(pl.program_id(0) == 0)
    def _():
        stack_parts(parts, part_refs, each, 2 * each, up_ref)
        sum_ref[...] = jnp.zeros_like(sum_ref)

    for i, block_ref in enumerate((x0, x1, x2, x3)):
        x_ref[i * rows : (i + 1) * rows, :] = block_ref[0]
    active, slope = gelu_parts(dot(x_ref[...], up_ref[...], 1, 1) + bias_ref[...])
    active_ref[0] = active.astype(BF)
    grad_hidden = (pull_ref[0].astype(F32) * slope).astype(BF)
    grad_hidden_ref[0] = grad_hidden
    sum_ref[...] += jnp.sum(grad_hidden.astype(F32), axis=0, keepdims=True)
    write_halves(dot(grad_hidden, up_ref[...], 1, 0), rows, keep_ref, other_ref, send_ref)


def halves_of(micro, rows, model):
    specs = [per((rows, model)), per((rows, model)), per((2 * rows, model))]
    return specs, [
        shape_of(F32, micro, rows, model), shape_of(BF, micro, rows, model),
        shape_of(BF, micro, 2 * rows, model),
    ]


def feed_forward(x, pull, blocks, bias):
    micro, rows, model = x[0].shape
    group = 4 * rows
    hidden = pull.shape[2]
    specs, shapes = halves_of(micro, rows, model)
    parts, arrays = parts_between(blocks, hidden // 8, hidden // 4)
    return pl.pallas_call(
        partial(feed_kernel, parts),
        grid=(micro,),
        in_specs=[per((rows, model))] * 4 + [per((group, hidden)), whole(bias)]
        + [whole(b) for b in arrays],
        out_specs=[per((group, hidden))] * 2 + specs + [full((1, hidden))],
        out_shape=[shape_of(BF, micro, group, hidden)] * 2 + shapes + [shape_of(F32, 1, hidden)],
        scratch_shapes=[pltpu.VMEM((group, model), BF), pltpu.VMEM((hidden, model), BF)],
        compiler_params=params(56),
        cost_estimate=pl.CostEstimate(
            flops=4 * micro * group * model * hidden,
            bytes_accessed=12 * micro * group * model,
            transcendentals=micro * group * hidden,
        ),
        name="feed_forward",
    )(*x, pull, bias, *arrays)


def feed_out_kernel(parts, active_ref, *rest):
    *part_refs, keep_ref, other_ref, send_ref, down_ref = rest

    @pl.when(pl.program_id(0) == 0)
    def _():
        stack_parts(parts, part_refs, 0, down_ref.shape[0] // 8, down_ref)

    write_halves(
        dot(active_ref[0], down_ref[...], 1, 0), keep_ref.shape[1], keep_ref, other_ref, send_ref
    )


def feed_out(active, blocks):
    micro, group, hidden = active.shape
    parts, arrays = parts_between(blocks, 0, hidden // 8)
    model = arrays[0].shape[1]
    specs, shapes = halves_of(micro, group // 4, model)
    return pl.pallas_call(
        partial(feed_out_kernel, parts),
        grid=(micro,),
        in_specs=[per((group, hidden))] + [whole(b) for b in arrays],
        out_specs=specs,
        out_shape=shapes,
        scratch_shapes=[pltpu.VMEM((hidden, model), BF)],
        compiler_params=params(56),
        cost_estimate=pl.CostEstimate(
            flops=2 * micro * group * model * hidden,
            bytes_accessed=8 * micro * group * model,
            transcendentals=0,
        ),
        name="feed_out",
    )(active, *arrays)


def rows_from(refs, to_ref):
    micro, rows, _ = refs[0].shape
    for m in range(micro):
        for i, block_ref in enumerate(refs):
            at = (4 * m + i) * rows
            to_ref[at : at + rows, :] = block_ref[m]


def feed_grads_kernel(active_ref, grad_hidden_ref, g0, g1, g2, g3, x0, x1, x2, x3, *rest):
    *outs, total_ref, right_ref = rest
    each = outs[0].shape[0] // 2
    step = pl.program_id(0)
    hidden = active_ref.shape[1]
    cut = hidden // 256 * 128
    for left_ref, refs, part in (
        (active_ref, (g0, g1, g2, g3), 0), (grad_hidden_ref, (x0, x1, x2, x3), 1)
    ):

        @pl.when(step == part)
        def _():
            rows_from(refs, right_ref)
            total_ref[:cut, :] = dot(left_ref[:, :cut], right_ref[...], 0, 0)
            total_ref[cut:, :] = dot(left_ref[:, cut:], right_ref[...], 0, 0)
            for i, out_ref in enumerate(outs):
                rows = total_ref[(i + 1) * each : (i + 2) * each, :].astype(BF)
                out_ref[part * each : (part + 1) * each, :] = rows


def feed_grads(active, grad_hidden, grad, x):
    rows, hidden = active.shape
    model = grad[0].shape[2]
    block = (hidden // 4, model)
    arrays = [active, grad_hidden, *grad, *x]
    return pl.pallas_call(
        feed_grads_kernel,
        grid=(2,),
        in_specs=[whole(a) for a in arrays],
        out_specs=[full(block)] * 7,
        out_shape=[shape_of(BF, *block)] * 7,
        scratch_shapes=[pltpu.VMEM((hidden, model), F32), pltpu.VMEM((rows, model), BF)],
        compiler_params=params(56),
        cost_estimate=pl.CostEstimate(
            flops=4 * rows * model * hidden, bytes_accessed=12 * rows * model, transcendentals=0
        ),
        name="feed_grads",
    )(*arrays)


def feed_grads_first_kernel(
    active_ref, grad_hidden_ref, g0, g1, g2, g3, x0, x1, x2, x3, out_ref, total_ref, right_ref
):
    each = out_ref.shape[0] // 2
    step = pl.program_id(0)
    for left_ref, refs, part in (
        (active_ref, (g0, g1, g2, g3), 0), (grad_hidden_ref, (x0, x1, x2, x3), 1)
    ):
        rows_from(refs, right_ref)
        rows = dot(left_ref[...], right_ref[...], 0, 0)[:each]
        at = slice(part * each, (part + 1) * each)

        @pl.when(step == 0)
        def _():
            total_ref[at, :] = rows

        @pl.when(step > 0)
        def _():
            total_ref[at, :] += rows

    @pl.when(step == pl.num_programs(0) - 1)
    def _():
        out_ref[...] = total_ref[...].astype(BF)


def feed_grads_first(active, grad_hidden, grad, x):
    rows, hidden = active.shape
    micro, own, model = grad[0].shape
    group = 4 * own
    block = (hidden // 4, model)
    left = pl.BlockSpec((group, 256), lambda i: (i, 0))
    return pl.pallas_call(
        feed_grads_first_kernel,
        grid=(micro,),
        in_specs=[left] * 2 + [per((own, model))] * 8,
        out_specs=full(block),
        out_shape=shape_of(BF, *block),
        scratch_shapes=[pltpu.VMEM(block, F32), pltpu.VMEM((group, model), BF)],
        compiler_params=params(56),
        cost_estimate=pl.CostEstimate(
            flops=rows * model * hidden // 2, bytes_accessed=8 * rows * model, transcendentals=0
        ),
        name="feed_grads_first",
    )(active, grad_hidden, *grad, *x)


def middle_pull_kernel(
    out_ref, middle_ref, keep_ref, arrived_ref, across_ref, vec_ref, grad_ref, branch_ref, sum_ref
):
    rows = out_ref.shape[1]
    back = keep_ref[0] + arrived_ref[0, :rows, :].astype(F32) + across_ref[0].astype(F32)
    hat, scale = norm_stats(middle_ref[0])
    out = out_ref[0].astype(F32)
    grad = out + norm_pull(back, hat, scale, vec_ref[5:6, :])
    grad_ref[0] = grad
    branch = grad.astype(BF)
    branch_ref[0] = branch

    @pl.when(pl.program_id(0) == 0)
    def _():
        sum_ref[...] = jnp.zeros_like(sum_ref)

    for i, terms in enumerate((branch.astype(F32), back * hat, back, out)):
        sum_ref[i : i + 1, :] += jnp.sum(terms, axis=0, keepdims=True)


def middle_pull(out, middle, keep, arrived, across, vec):
    micro, rows, model = out.shape
    one = per((rows, model))
    return pl.pallas_call(
        middle_pull_kernel,
        grid=(micro,),
        in_specs=[one, one, one, per((2 * rows, model)), one, whole(vec)],
        out_specs=[one, one, full((4, model))],
        out_shape=[
            shape_of(F32, micro, rows, model), shape_of(BF, micro, rows, model),
            shape_of(F32, 4, model),
        ],
        name="middle_pull",
    )(out, middle, keep, arrived, across, vec)


def attend_pull_kernel(
    place_ref, g0, g1, g2, g3, n0, n1, n2, n3, m0, m1, m2, m3, row_ref,
    qkv_ref, log_ref, heads_ref, normed_ref,
    keep_ref, other_ref, send_ref, k0, k1, k2, k3, s0, s1, s2, s3, bias_ref,
    grad_ref, grad_qkv_ref, total_ref, sum_ref, weight_ref, mask_ref,
):
    width = heads_ref.shape[2]
    count = width // HEAD_DIM
    rows = g0.shape[1]
    model = g0.shape[2]
    scale = HEAD_DIM ** (-0.5)
    step = pl.program_id(0)

    @pl.when(step == 0)
    def _():
        assemble(place_ref, (n0, n1, n2, n3), (m0, m1, m2, m3), weight_ref)

    write_mask(row_ref, mask_ref)
    for i, block_ref in enumerate((g0, g1, g2, g3)):
        grad_ref[i * rows : (i + 1) * rows, :] = block_ref[0]
    grad_heads = dot(grad_ref[...], weight_ref[3 * width :, :], 1, 1).astype(BF)
    for head in range(count):
        lanes = [slice(i * width + head * HEAD_DIM, i * width + (head + 1) * HEAD_DIM) for i in range(3)]
        queries, keys, values = [qkv_ref[0, :, part] for part in lanes]
        scores = dot(queries * jnp.asarray(scale, BF), keys, 1, 1) + mask_ref[...]
        probs = jnp.exp(scores - log_ref[0, :, head : head + 1])
        grad = grad_heads[:, lanes[0]]
        delta = jnp.sum(
            grad.astype(F32) * heads_ref[0, :, lanes[0]].astype(F32), axis=1, keepdims=True
        )
        grad_scores = (probs * (dot(grad, values, 1, 1) - delta)).astype(BF)
        grad_qkv_ref[:, lanes[0]] = (scale * dot(grad_scores, keys, 1, 0)).astype(BF)
        grad_qkv_ref[:, lanes[1]] = (scale * dot(grad_scores, queries, 0, 0)).astype(BF)
        grad_qkv_ref[:, lanes[2]] = dot(probs.astype(BF), grad, 0, 0).astype(BF)
    write_halves(dot(grad_qkv_ref[...], weight_ref[: 3 * width, :], 1, 0), rows, keep_ref, other_ref, send_ref)
    qkv_part = dot(grad_qkv_ref[...], normed_ref[0], 0, 0)
    out_part = dot(heads_ref[0], grad_ref[...], 0, 0)
    sums = jnp.sum(grad_qkv_ref[...].astype(F32), axis=0, keepdims=True)

    @pl.when(step == 0)
    def _():
        total_ref[: 3 * width, :] = qkv_part
        total_ref[3 * width :, :] = out_part
        sum_ref[...] = jnp.broadcast_to(sums, sum_ref.shape)

    @pl.when(step > 0)
    def _():
        total_ref[: 3 * width, :] += qkv_part
        total_ref[3 * width :, :] += out_part
        sum_ref[...] += sums

    @pl.when(step == pl.num_programs(0) - 1)
    def _():
        z, y, ctx = place_ref[0], place_ref[1], place_ref[2]
        for k, pair in zip(SHIFTS, ((k0, s0), (k1, s1), (k2, s2), (k3, s3))):
            region = lax.rem(z + 4 - k, 4) * width
            for out_ref, half in zip(pair, (y, 1 - y)):
                start = pl.multiple_of(region + BODY * half, HEAD_DIM)
                out_ref[:BODY, :] = total_ref[pl.ds(start, BODY), :].astype(BF)
                start = pl.multiple_of(region + 2 * BODY + HALO * half, HALO)
                out_ref[BODY:, :] = total_ref[pl.ds(start, HALO), :].astype(BF)
        own = head_places((width, model), 0, ctx)
        hot = (lax.broadcasted_iota(jnp.int32, (width, model), 1) == own).astype(F32)
        for i, part in enumerate((0, 2)):
            line = lax.dot_general(
                sum_ref[:, part * width : (part + 1) * width],
                hot,
                (((1,), (0,)), ((), ())),
                preferred_element_type=F32,
                precision=lax.Precision.HIGHEST,
            )
            bias_ref[i : i + 1, :] = line[0:1]


def attend_pull(place, grads, near, side, row, qkv, log_total, heads, normed):
    micro, rows, model = grads[0].shape
    group = 4 * rows
    width = heads.shape[2]
    count = width // HEAD_DIM
    block = (BODY + HALO, model)
    one = per((rows, model))
    return pl.pallas_call(
        attend_pull_kernel,
        grid=(micro,),
        in_specs=[SCALARS] + [one] * 4 + [whole(b) for b in near + side] + [
            per(row.shape[1:]), per((group, 3 * width)), per((group, 128)),
            per((group, width)), per((group, model)),
        ],
        out_specs=[one, one, per((2 * rows, model))] + [full(block)] * 8 + [full((2, model))],
        out_shape=[
            shape_of(F32, micro, rows, model), shape_of(BF, micro, rows, model),
            shape_of(BF, micro, 2 * rows, model),
        ] + [shape_of(BF, *block)] * 8 + [shape_of(F32, 2, model)],
        scratch_shapes=[
            pltpu.VMEM((group, model), BF), pltpu.VMEM((group, 3 * width), BF),
            pltpu.VMEM((4 * width, model), F32), pltpu.VMEM((8, 3 * width), F32),
            pltpu.VMEM((4 * width, model), BF), pltpu.VMEM((group, group), F32),
        ],
        compiler_params=params(60),
        cost_estimate=pl.CostEstimate(
            flops=2 * micro * group * model * 10 * width,
            bytes_accessed=12 * micro * group * model,
            transcendentals=micro * count * group * group,
        ),
        name="attend_pull",
    )(place, *grads, *near, *side, row, qkv, log_total, heads, normed)


def input_pull_kernel(
    x_ref, grad_ref, keep_ref, arrived_ref, across_ref, vec_ref, out_ref, sum_ref
):
    rows = x_ref.shape[1]
    back = keep_ref[0] + arrived_ref[0, :rows, :].astype(F32) + across_ref[0].astype(F32)
    hat, scale = norm_stats(x_ref[0].astype(F32))
    out = grad_ref[0] + norm_pull(back, hat, scale, vec_ref[0:1, :])
    out_ref[0] = jnp.transpose(out).astype(BF)

    @pl.when(pl.program_id(0) == 0)
    def _():
        sum_ref[...] = jnp.zeros_like(sum_ref)

    for i, terms in enumerate((back * hat, back)):
        sum_ref[i : i + 1, :] += jnp.sum(terms, axis=0, keepdims=True)


def input_pull(x, grad, keep, arrived, across, vec):
    micro, rows, model = x.shape
    one = per((rows, model))
    out, sums = pl.pallas_call(
        input_pull_kernel,
        grid=(micro,),
        in_specs=[one, one, one, per((2 * rows, model)), one, whole(vec)],
        out_specs=[per((model, rows)), full((2, model))],
        out_shape=[shape_of(BF, micro, model, rows), shape_of(F32, 2, model)],
        name="input_pull",
    )(x, grad, keep, arrived, across, vec)
    return out.transpose(0, 2, 1), sums


def mixed_kernel(middle_ref, keep_ref, arrived_ref, across_ref, vec_ref, out_ref):
    rows = middle_ref.shape[1]
    feed = keep_ref[0] + arrived_ref[0, :rows, :].astype(F32) + across_ref[0].astype(F32)
    out_ref[0] = jnp.transpose(middle_ref[0] + feed + vec_ref[7:8, :]).astype(BF)


def mixed_rows(middle, keep, arrived, across, vec):
    micro, rows, model = middle.shape
    one = per((rows, model))
    return pl.pallas_call(
        mixed_kernel,
        grid=(micro,),
        in_specs=[one, one, per((2 * rows, model)), one, whole(vec)],
        out_specs=per((model, rows)),
        out_shape=shape_of(BF, micro, model, rows),
        name="mixed_rows",
    )(middle, keep, arrived, across, vec).transpose(0, 2, 1)


def row_places(segments, rows):
    ctx = lax.axis_index("ctx")
    ranks = [ctx ^ j for j in BLOCKS]
    starts = segments[:, 0].reshape(-1, 4, rows).transpose(1, 0, 2)
    starts = jnp.concatenate([pick(starts, r) for r in ranks], axis=1)
    places = jnp.concatenate([r * rows + jnp.arange(rows, dtype=jnp.int32) for r in ranks])
    places = jnp.broadcast_to(places[None], starts.shape)
    return jnp.stack([starts, places] + [places] * 6, axis=1)


def own_up_bias(lines, order, width):
    table = lines[16:].reshape(order.shape[0], 4, width).transpose(1, 0, 2)
    return reorder(pick(table, lax.axis_index("ctx")), order).reshape(1, -1)


def vector_parts(first_sums, bias_sums, sums, up_sum, order, width):
    up_rows = reorder_back(up_sum.reshape(order.shape[0], width), order)
    mine = (jnp.arange(4) == lax.axis_index("ctx")).astype(F32)
    table = jnp.concatenate([first_sums, bias_sums, sums], axis=0)
    up_part = (up_rows[:, None, :] * mine[None, :, None]).reshape(-1)
    return jnp.concatenate([table.reshape(-1), up_part])


def flat(values):
    return values.reshape(-1, values.shape[-1])


def halo_pairs(back):
    pairs = []
    for p in range(8):
        for c in range(4):
            to = (c - 1) % 4 if (p % 2 == 1) != back else (c + 1) % 4
            pairs.append((p * 4 + c, p * 4 + to))
    return pairs


def aligned_block(w_attn, vectors, odd, ctx):
    turned = row_major(w_attn.T)
    width, model = turned.shape
    table = ctx_table(vectors, ctx).astype(BF).reshape(3, model // 2)
    edge = jnp.where(odd, turned[:HALO], turned[width - HALO :])
    halo = lax.ppermute(edge, BOTH, halo_pairs(False))
    none = jnp.zeros_like(halo)
    wide = jnp.concatenate(
        [jnp.where(odd, none, halo), turned, jnp.where(odd, halo, none)], axis=0
    )
    shift = HALO * odd.astype(jnp.int32)
    body = lax.dynamic_slice_in_dim(wide, HALO - 8 * ctx + shift, BODY, axis=0)
    extra = lax.dynamic_slice_in_dim(wide, width + shift, HALO, axis=0)
    extra = jnp.where(ctx == 3, extra, jnp.zeros_like(extra))
    lines = jnp.pad(table, ((0, 13), (0, model // 2)))
    return jnp.concatenate([body, extra, lines], axis=0)


def aligned_owned(own, odd, ctx, width):
    last = ctx == 3
    body, extra = own[:BODY], own[BODY:]
    tail = jnp.where(last, extra, body[BODY - HALO :])
    halo = lax.ppermute(jnp.where(odd, tail, body[:HALO]), BOTH, halo_pairs(True))
    halo = jnp.where(last & jnp.logical_not(odd), extra, halo)
    wide = jnp.where(
        odd, jnp.concatenate([halo, body], axis=0), jnp.concatenate([body, halo], axis=0)
    )
    return lax.dynamic_slice_in_dim(wide, 8 * ctx, width, axis=0)


def vector_sides(part, y, ctx):
    table = part.reshape(8, 4, -1).transpose(1, 0, 2)
    mine = jnp.stack([pick(table, ctx ^ j) for j in (0, 1)])
    far = jnp.stack([pick(table, ctx ^ j) for j in (2, 3)])
    mine = mine + lax.ppermute(far, "ctx", CHIP_PAIRS)
    mine = mine[0] + lax.ppermute(mine[1], "ctx", CORE_PAIRS)
    sides = mine.reshape(4, 2, -1).transpose(1, 0, 2)
    return pick(sides, y) + lax.ppermute(pick(sides, 1 - y), "dp", SIDE_PAIRS)


def vector_owned(mine, z):
    total = pick(mine, z)
    for k in (1, 2, 3):
        total = total + to_shift(pick(mine, (z - k) % 4)[None], k, True)[0]
    return total


def both(keep, arrived):
    return keep.astype(F32) + arrived.astype(F32)


def aligned(tokens, cotangent, w_attn, w_up, w_down, vectors, segments):
    rows = tokens.shape[1]
    width = w_attn.shape[1]
    ctx, dp = lax.axis_index("ctx"), lax.axis_index("dp")
    z, y = dp // 2, dp % 2
    odd = y == 1
    place = jnp.stack([z, y, ctx]).astype(jnp.int32)
    order = jnp.stack(dp_order(z, y))
    tokens, cotangent = row_major(tokens), row_major(cotangent)
    row_info = row_places(segments, rows)
    feed = jnp.concatenate([w_down, w_up.T], axis=0)

    n0 = aligned_block(w_attn, vectors, odd, ctx)
    n0, t0, place, row_info, b0 = hold([n0, tokens, place, row_info, feed])
    n1, n3, s0, t1, c0 = (
        to_shift(n0, 1), to_shift(n0, 3), to_side(n0), to_chip(t0), to_side(b0[:CUT])
    )
    n0, n1, n3, s0, t0, t1, g0, b0, c0 = hold([n0, n1, n3, s0, t0, t1, cotangent, b0, c0])
    n2, s1, s3, g1 = to_shift(n0, 2), to_side(n1), to_side(n3), to_chip(g0)
    n0, n1, n2, n3, s0, s1, s3, t0, t1, g0, g1, b0 = hold(
        [n0, n1, n2, n3, s0, s1, s3, t0, t1, g0, g1, b0]
    )
    s2, b1, t2, t3 = to_side(n2), to_shift(b0, 1), to_core(t0), to_core(t1)
    n0, n1, n2, n3, s0, s1, s2, s3, t0, t1, t2, t3, g0, g1, b0, b1 = hold(
        [n0, n1, n2, n3, s0, s1, s2, s3, t0, t1, t2, t3, g0, g1, b0, b1]
    )
    b3, b2, c1 = to_shift(b0, 3), to_shift(b0[: THIRDS[0]], 2), to_side(b1)
    g2, g3 = to_core(g0), to_core(g1)
    normed_one, qkv, log_total, heads, lines, rest, keep, other, away = attend(
        place, [t0, t1, t2, t3], [n0, n1, n3, n2], [s0, s1, s3, s2], row_info
    )
    away, keep, other, b0, b1, b2, b3, c1, g0, g1, g2, g3 = hold(
        [away, keep, other, b0, b1, b2, b3, c1, g0, g1, g2, g3]
    )
    arrived = to_core(away)
    away, arrived, keep, b0, b2, b3 = hold([half_sum(other, arrived), arrived, keep, b0, b2, b3])
    across, d2, c3, c2 = (
        to_chip(away), to_shift(b0[THIRDS[0] : THIRDS[1]], 2), to_side(b3), to_side(b2)
    )
    across, arrived, keep, b0, d2, c3, c2 = hold([across, arrived, keep, b0, d2, c3, c2])
    middle, h0 = middle_rows(tokens, keep, arrived, across, lines)
    h0, middle, b0, d2 = hold([h0, middle, b0, d2])
    h1, h2, e2, f2 = to_chip(h0), to_core(h0), to_shift(b0[THIRDS[1] :], 2), to_side(d2)
    d0 = to_side(b0[CUT:])
    up_bias = own_up_bias(rest, order, width)
    h0, h1, h2, e2, f2, d0, up_bias = hold([h0, h1, h2, e2, f2, d0, up_bias])
    h3, a2 = to_core(h1), to_side(e2)
    blocks = [[c2, f2, a2], [b2, d2, e2], [b0], [c0, d0], [b1], [c1], [b3], [c3]]
    pull = feed_pull([g0, g1, g2, g3], blocks)
    h0, h1, h2, h3, pull = hold([h0, h1, h2, h3, pull], a2)
    active, grad_hidden, keep, other, away, up_sum = feed_forward(
        [h0, h1, h2, h3], pull, blocks, up_bias
    )
    x_all, grad_all = [h0, h1, h2, h3], [g0, g1, g2, g3]

    arrived = to_core(away)
    q2 = feed_grads_first(flat(active), flat(grad_hidden), grad_all, x_all)
    away, arrived, keep, active, q2 = hold(
        [half_sum(other, arrived), arrived, keep, active, q2]
    )
    across, q2 = to_chip(away), to_side(q2)
    p2, p0, q0, p1, q1, p3, q3 = feed_grads(flat(active), flat(grad_hidden), grad_all, x_all)
    across, arrived, keep, p2, q2 = hold([across, arrived, keep, p2, q2])
    grad_middle, h0, sums = middle_pull(cotangent, middle, keep, arrived, across, lines)
    h0, p2, q3, grad_middle, active = hold([h0, both(p2, q2).astype(BF), q3, grad_middle, active])
    h1, h2, r2, q3 = to_chip(h0), to_core(h0), to_shift(p2[:BACK_CUT], 2, True), to_side(q3)
    feed_keep, feed_other, feed_away = feed_out(active, blocks)
    h0, h1, h2, r2, q3, p2, feed_away = hold([h0, h1, h2, r2, q3, p2, feed_away])
    h3, feed_arrived = to_core(h1), to_core(feed_away)
    h0, h1, h2, h3, p2, p3, q1, q0, feed_arrived = hold(
        [h0, h1, h2, h3, p2, both(p3, q3).astype(BF), q1, q0, feed_arrived]
    )
    t2, r3 = to_shift(p2[BACK_CUT:], 2, True), to_shift(p3, 3, True)
    q1, q0 = to_side(q1), to_side(q0)
    keep, other, away, *parts, bias_sums = attend_pull(
        place, [h0, h1, h2, h3], [n0, n1, n3, n2], [s0, s1, s3, s2], row_info,
        qkv, log_total, heads, normed_one,
    )
    away, t2, r3, q1, q0, p0, p1, *parts = hold([away, t2, r3, q1, q0, p0, p1] + parts)
    k0, k1, k3, k2, l0, l1, l3, l2 = parts
    arrived = to_core(away)
    away, arrived, keep, p1, l1, l2, l3 = hold(
        [half_sum(other, arrived), arrived, keep, both(p1, q1).astype(BF), l1, l2, l3]
    )
    r1, across, l2, l1 = to_shift(p1, 1, True), to_chip(away), to_side(l2), to_side(l1)
    across, arrived, keep, r1, k1, k2, l0, l3, feed_away = hold(
        [
            across, arrived, keep, r1, both(k1, l1).astype(BF), both(k2, l2).astype(BF),
            l0, l3, half_sum(feed_other, feed_arrived),
        ]
    )
    k2, k1, l3, l0, feed_across = (
        to_shift(k2, 2, True), to_shift(k1, 1, True), to_side(l3), to_side(l0),
        to_chip(feed_away),
    )
    input_grad, first_sums = input_pull(tokens, grad_middle, keep, arrived, across, lines)
    part = vector_parts(first_sums, bias_sums, sums, up_sum, order, width)
    k1, k2, k3, l0, part, feed_across, input_grad = hold(
        [k1, k2, both(k3, l3).astype(BF), l0, part, feed_across, input_grad]
    )
    k3, part = to_shift(k3, 3, True), vector_sides(part, y, ctx)
    mixed = mixed_rows(middle, feed_keep, feed_arrived, feed_across, lines)
    terms = [p0, q0, r1, jnp.concatenate([r2, t2], axis=0), r3]
    down_owned = sum(t[:width].astype(F32) for t in terms)
    up_owned = sum(t[width:].astype(F32) for t in terms).T
    k3, part, mixed, down_owned, up_owned = hold([k3, part, mixed, down_owned, up_owned])
    own = both(k0, l0) + k1.astype(F32) + k2.astype(F32) + k3.astype(F32)
    attn_owned = aligned_owned(own, odd, ctx, width)
    return (
        mixed, input_grad, attn_owned.T, up_owned, down_owned, vector_owned(part, z),
    )


def plain(tokens, cotangent, w_attn, w_up, w_down, vectors, segments):
    micro, rows, model = tokens.shape
    width = w_attn.shape[1]
    ctx = lax.axis_index("ctx")
    last = ctx == lax.axis_size("ctx") - 1
    place = jnp.stack([jnp.zeros((), ctx.dtype), jnp.zeros((), ctx.dtype), ctx])
    order = jnp.arange(lax.axis_size("dp"))
    table = lax.all_gather(w_attn.T, BOTH, axis=0, tiled=True)
    lines = lax.all_gather(vectors, BOTH, axis=0, tiled=True).reshape(24, model // 2)
    lines = jnp.pad(lines, ((0, 0), (0, model // 2)))
    near, side = [], []
    for region in (-k % 4 for k in SHIFTS):
        part = head_rows(table[region * model : (region + 1) * model], ctx, last)
        for blocks, half in ((near, 0), (side, 1)):
            line = 3 * (2 * region + half)
            blocks.append(
                jnp.concatenate(
                    [
                        part[BODY * half : BODY * (half + 1)],
                        part[2 * BODY + HALO * half : 2 * BODY + HALO * (half + 1)],
                        jnp.pad(lines[line : line + 3], ((0, 13), (0, 0))),
                    ],
                    axis=0,
                )
            )
    up = lax.all_gather(w_up.T, "dp", axis=0, tiled=True)
    down = lax.all_gather(w_down, "dp", axis=0, tiled=True)
    each = up.shape[0] // 8
    blocks = [
        jnp.concatenate([w[i * each : (i + 1) * each] for w in (down, up)], axis=0)
        for i in range(8)
    ]
    blocks = [[b] for b in blocks]
    row_info = row_places(segments, rows)

    normed_one, qkv, log_total, heads, lines, rest, *halves = attend(
        place, row_gather(tokens), near, side, row_info
    )
    middle, normed_two = middle_rows(tokens, *row_scatter(*halves), lines)
    x_all, grad_all = row_gather(normed_two), row_gather(cotangent)
    active, grad_hidden, *halves, up_sum = feed_forward(
        x_all, feed_pull(grad_all, blocks), blocks, own_up_bias(rest, order, width)
    )
    mixed = mixed_rows(middle, *row_scatter(*feed_out(active, blocks)), lines)
    grad_middle, branch, sums = middle_pull(cotangent, middle, *row_scatter(*halves), lines)
    arrays = flat(active), flat(grad_hidden), grad_all, x_all
    parts = [feed_grads_first(*arrays)] + list(feed_grads(*arrays))
    down_owned, up_owned = [
        lax.psum_scatter(
            jnp.concatenate([p[i * each : (i + 1) * each] for p in parts], axis=0),
            "dp", scatter_dimension=0, tiled=True,
        ).astype(F32)
        for i in range(2)
    ]
    *halves, k0, k1, k2, k3, s0, s1, s2, s3, bias_sums = attend_pull(
        place, row_gather(branch), near, side, row_info, qkv, log_total, heads, normed_one
    )
    input_grad, first_sums = input_pull(tokens, grad_middle, *row_scatter(*halves), lines)
    parts = []
    for region in range(4):
        at = SHIFTS.index(-region % 4)
        first, second = (k0, k1, k2, k3)[at], (s0, s1, s2, s3)[at]
        part = [first[:BODY], second[:BODY], first[BODY:], second[BODY:]]
        parts.append(head_rows_back(jnp.concatenate(part, axis=0), ctx, last))
    attn_owned = lax.psum_scatter(
        jnp.concatenate(parts, axis=0), BOTH, scatter_dimension=0, tiled=True
    ).astype(F32)
    part = vector_parts(first_sums, bias_sums, sums, up_sum, order, width)
    vector_grad = lax.psum_scatter(part, BOTH, scatter_dimension=0, tiled=True)
    return (mixed, input_grad, attn_owned.T, up_owned.T, down_owned, vector_grad)


def shards(*arrays):
    fits = lax.axis_size("dp") == 8 and lax.axis_size("ctx") == 4
    return (aligned if fits and arrays[2].shape == (1088, 136) else plain)(*arrays)


def solution(mesh):
    return jax.shard_map(
        shards,
        mesh=mesh,
        in_specs=(
            P(None, BOTH, None),
            P(None, BOTH, None),
            P(None, BOTH),
            P(None, BOTH),
            P(BOTH, None),
            P(BOTH),
            P(None, "dp", None),
        ),
        out_specs=(
            P(None, BOTH, None),
            P(None, BOTH, None),
            P(None, BOTH),
            P(None, BOTH),
            P(BOTH, None),
            P(BOTH),
        ),
        check_vma=False,
    )
```

```python
from functools import partial

import jax
import jax.numpy as jnp
from jax import lax
from jax.experimental import pallas as pl
from jax.experimental.layout import Layout, with_layout_constraint
from jax.experimental.pallas import tpu as pltpu
from jax.sharding import PartitionSpec as P

HEAD_DIM = 64
HALO = 32
BODY = 128
NEG_FILL = -1e30
EPSILON = 1e-05
BF = jnp.bfloat16
F32 = jnp.float32
BOTH = ("dp", "ctx")
CORE_PAIRS = [(0, 1), (1, 0), (2, 3), (3, 2)]
CHIP_PAIRS = [(0, 2), (2, 0), (1, 3), (3, 1)]
BLOCKS = (0, 2, 1, 3)
SHIFTS = (0, 1, 3, 2)
ORDER = ((2, 1), (2, 0), (0, 0), (0, 1), (1, 0), (1, 1), (3, 0), (3, 1))
THIRDS = (64, 160)
CUT = 144
BACK_CUT = 112
SIDE_PAIRS = [(p, p ^ 1) for p in range(8)]


def shift_pairs(step):
    return [(z * 2 + y, ((z + step) % 4) * 2 + y) for z in range(4) for y in range(2)]


def dot(left, right, left_dim, right_dim):
    return lax.dot_general(
        left, right, (((left_dim,), (right_dim,)), ((), ())), preferred_element_type=F32
    )


def norm_stats(values):
    centred = values - jnp.mean(values, axis=-1, keepdims=True)
    scale = lax.rsqrt(jnp.mean(centred * centred, axis=-1, keepdims=True) + EPSILON)
    return centred * scale, scale


def norm_pull(grad, hat, scale, gain):
    grad_hat = grad * gain
    along = jnp.mean(grad_hat * hat, axis=-1, keepdims=True)
    return scale * (grad_hat - jnp.mean(grad_hat, axis=-1, keepdims=True) - hat * along)


def row_major(value):
    return with_layout_constraint(value, Layout(tuple(range(value.ndim))))


def send(value, axes, pairs):
    rows = value.shape[-2]
    if rows % 16:
        return lax.ppermute(value, axes, pairs)
    cut = value.reshape(value.shape[:-2] + (rows // 16, 16, value.shape[-1]))
    return lax.ppermute(cut, axes, pairs).reshape(value.shape)


def hold(values, *others):
    return lax.optimization_barrier(tuple(values) + tuple(others))[: len(values)]


def to_core(value):
    return send(value, "ctx", CORE_PAIRS)


def to_chip(value):
    return send(value, "ctx", CHIP_PAIRS)


def to_side(value):
    return send(value, "dp", SIDE_PAIRS)


def to_shift(value, step, back=False):
    pairs = shift_pairs(step)
    return send(value, "dp", [(b, a) for a, b in pairs] if back else pairs)


def row_gather(mine):
    across = to_chip(mine)
    return [mine, across, to_core(mine), to_core(across)]


def half_sum(other, arrived):
    rows = other.shape[1]
    return (other.astype(F32) + arrived[:, rows:].astype(F32)).astype(BF)


def row_scatter(keep, other, away):
    arrived = to_core(away)
    return keep, arrived, to_chip(half_sum(other, arrived))


def dp_order(z, y):
    return [((z - k) % 4) * 2 + (y ^ s) for k, s in ORDER]


def pick(stacked, index):
    return lax.dynamic_index_in_dim(stacked, index, axis=0, keepdims=False)


def reorder(table, order):
    hot = (order[:, None] == jnp.arange(table.shape[0])[None, :]).astype(F32)
    return jnp.sum(hot[:, :, None] * table[None], axis=1)


def reorder_back(table, order):
    hot = (order[:, None] == jnp.arange(table.shape[0])[None, :]).astype(F32)
    return jnp.sum(hot[:, :, None] * table[:, None, :], axis=0)


def ctx_table(mine, ctx):
    across = lax.ppermute(mine[None], "ctx", CHIP_PAIRS)
    pair = jnp.concatenate([mine[None], across], axis=0)
    table = jnp.concatenate([pair, lax.ppermute(pair, "ctx", CORE_PAIRS)], axis=0)
    return reorder_back(table.astype(F32), jnp.stack([ctx ^ j for j in BLOCKS]))


def head_rows(table, ctx, last):
    middle = 8 * HEAD_DIM
    first = lax.dynamic_slice_in_dim(table, 128 * ctx, 128, axis=0)
    second = lax.dynamic_slice_in_dim(table, middle + HEAD_DIM + 128 * ctx, 128, axis=0)
    mid = table[middle : middle + HEAD_DIM]
    return jnp.concatenate([first, second, jnp.where(last, mid, jnp.zeros_like(mid))], axis=0)


def head_rows_back(mine, ctx, last):
    middle = 8 * HEAD_DIM
    table = jnp.zeros((2 * middle + HEAD_DIM,) + mine.shape[1:], mine.dtype)
    table = lax.dynamic_update_slice_in_dim(table, mine[:128], 128 * ctx, axis=0)
    table = lax.dynamic_update_slice_in_dim(
        table, mine[128:256], middle + HEAD_DIM + 128 * ctx, axis=0
    )
    mid = jnp.where(last, mine[256:], jnp.zeros_like(mine[256:]))
    return lax.dynamic_update_slice_in_dim(table, mid, middle, axis=0)


def gelu_parts(hidden):
    factor = 0.7978845608028654
    square = hidden * hidden
    bent = jnp.tanh(factor * hidden * (1.0 + 0.044715 * square))
    active = 0.5 * hidden * (1.0 + bent)
    slope = 0.5 * (1.0 + bent) + 0.5 * hidden * (1.0 - bent * bent) * factor * (
        1.0 + 3 * 0.044715 * square
    )
    return active, slope


def full(shape):
    return pl.BlockSpec(shape, lambda *_: (0,) * len(shape))


def per(shape, step=1):
    return pl.BlockSpec((1,) + shape, lambda i: (i // step,) + (0,) * len(shape))


def params(mib):
    return pltpu.CompilerParams(vmem_limit_bytes=mib * 1024 * 1024)


def whole(array):
    return full(array.shape)


SCALARS = pl.BlockSpec(memory_space=pltpu.SMEM)


def shape_of(dtype, *dims):
    return jax.ShapeDtypeStruct(dims, dtype)


def head_places(shape, axis, ctx):
    own = lax.broadcasted_iota(jnp.int32, shape, axis)
    middle = 8 * HEAD_DIM
    shift = jnp.where(own < BODY, BODY * ctx, middle + HEAD_DIM - BODY + BODY * ctx)
    shift = jnp.where(own < 2 * BODY, shift, middle - 2 * BODY)
    return jnp.where((own < 2 * BODY) | (ctx == 3), own + shift, -1)


def write_halves(values, rows, keep_ref, other_ref, send_ref):
    keep_ref[0] = values[:rows]
    other_ref[0] = values[rows : 2 * rows].astype(BF)
    send_ref[0] = values[2 * rows :].astype(BF)


def assemble(place_ref, near, side, weight_ref):
    width = weight_ref.shape[0] // 4
    z, y = place_ref[0], place_ref[1]
    for k, pair in zip(SHIFTS, zip(near, side)):
        region = lax.rem(z + 4 - k, 4) * width
        for block_ref, half in zip(pair, (y, 1 - y)):
            to = pl.multiple_of(region + BODY * half, HEAD_DIM)
            weight_ref[pl.ds(to, BODY), :] = block_ref[:BODY, :]
            to = pl.multiple_of(region + 2 * BODY + HALO * half, HALO)
            weight_ref[pl.ds(to, HALO), :] = block_ref[BODY : BODY + HALO, :]


def write_mask(row_ref, mask_ref):
    row = row_ref[0].astype(F32)
    first, own = row[0:1], row[1:2]
    square = (128, row.shape[1])
    first_col = jnp.transpose(jnp.broadcast_to(first, square))[:, :1]
    own_col = jnp.transpose(jnp.broadcast_to(own, square))[:, :1]
    allowed = (own_col <= own) & (first_col == first)
    mask_ref[...] = jnp.where(allowed, 0.0, NEG_FILL)


def attend_kernel(
    place_ref, x0, x1, x2, x3, n0, n1, n2, n3, s0, s1, s2, s3, row_ref,
    normed_ref, qkv_ref, log_ref, heads_ref, vec_ref, line_ref,
    keep_ref, other_ref, send_ref, weight_ref, mask_ref, bias_ref,
):
    width = heads_ref.shape[2]
    count = width // HEAD_DIM
    model = vec_ref.shape[1]
    part = model // 2
    rows = x0.shape[1]

    @pl.when(pl.program_id(0) == 0)
    def _():
        z, y, ctx = place_ref[0], place_ref[1], place_ref[2]
        assemble(place_ref, (n0, n1, n2, n3), (s0, s1, s2, s3), weight_ref)
        for k, pair in zip(SHIFTS, ((n0, s0), (n1, s1), (n2, s2), (n3, s3))):
            owner = lax.rem(z + 4 - k, 4)
            for block_ref, half in zip(pair, (y, 1 - y)):
                lines = block_ref[BODY + HALO :, :].astype(F32)
                for i in range(3):
                    line_ref[pl.ds(3 * (2 * owner + half) + i, 1), :] = lines[i : i + 1, :part]
        for i in range(8):
            vec_ref[i : i + 1, :part] = line_ref[2 * i : 2 * i + 1, :]
            vec_ref[i : i + 1, part:] = line_ref[2 * i + 1 : 2 * i + 2, :]
        own = head_places((model, width), 1, ctx)
        hot = (lax.broadcasted_iota(jnp.int32, (model, width), 0) == own).astype(F32).astype(BF)
        own_vec = dot(vec_ref[...].astype(BF), hot, 1, 0)
        bias_ref[:, :width] = own_vec[2:3]
        bias_ref[:, width : 2 * width] = jnp.zeros((1, width), F32)
        bias_ref[:, 2 * width :] = own_vec[3:4]

    gain, bias = vec_ref[0:1, :], vec_ref[1:2, :]
    for i, x_ref in enumerate((x0, x1, x2, x3)):
        hat, _ = norm_stats(x_ref[0].astype(F32))
        normed_ref[0, i * rows : (i + 1) * rows, :] = (hat * gain + bias).astype(BF)
    normed = normed_ref[0]
    qkv_ref[0] = (dot(normed, weight_ref[: 3 * width, :], 1, 1) + bias_ref[...]).astype(BF)
    write_mask(row_ref, mask_ref)
    for head in range(count):
        lanes = [slice(i * width + head * HEAD_DIM, i * width + (head + 1) * HEAD_DIM) for i in range(3)]
        queries, keys, values = [qkv_ref[0, :, part] for part in lanes]
        queries = queries * jnp.asarray(HEAD_DIM ** (-0.5), BF)
        scores = dot(keys, queries, 1, 1) + mask_ref[...]
        top = jnp.max(scores, axis=0, keepdims=True)
        weights = jnp.exp(scores - top)
        total = jnp.sum(weights, axis=0, keepdims=True)
        probs = (weights * (1.0 / total)).astype(BF)
        log_ref[0, head : head + 1, :] = top + jnp.log(total)
        heads_ref[0, :, lanes[0]] = jnp.transpose(dot(values, probs, 0, 0)).astype(BF)
    branch = dot(heads_ref[0], weight_ref[3 * width :, :], 1, 0)
    write_halves(branch, rows, keep_ref, other_ref, send_ref)


def attend(place, blocks, near, side, row):
    micro, rows, model = blocks[0].shape
    group = 4 * rows
    width = 2 * (BODY + HALO)
    count = width // HEAD_DIM
    return pl.pallas_call(
        attend_kernel,
        grid=(micro,),
        in_specs=[SCALARS] + [per((rows, model))] * 4
        + [whole(b) for b in near + side] + [per(row.shape[1:])],
        out_specs=[
            per((group, model)), per((group, 3 * width)), per((8, group)),
            per((group, width)), full((8, model)), full((24, model // 2)),
            per((rows, model)), per((rows, model)), per((2 * rows, model)),
        ],
        out_shape=[
            shape_of(BF, micro, group, model), shape_of(BF, micro, group, 3 * width),
            shape_of(F32, micro, 8, group), shape_of(BF, micro, group, width),
            shape_of(F32, 8, model),
            shape_of(F32, 24, model // 2), shape_of(F32, micro, rows, model),
            shape_of(BF, micro, rows, model), shape_of(BF, micro, 2 * rows, model),
        ],
        scratch_shapes=[
            pltpu.VMEM((4 * width, model), BF), pltpu.VMEM((group, group), F32),
            pltpu.VMEM((1, 3 * width), F32),
        ],
        compiler_params=params(56),
        cost_estimate=pl.CostEstimate(
            flops=2 * micro * group * model * 4 * width,
            bytes_accessed=12 * micro * group * model,
            transcendentals=micro * count * group * group,
        ),
        name="attend",
    )(place, *blocks, *near, *side, row)


def middle_kernel(x_ref, keep_ref, arrived_ref, across_ref, vec_ref, middle_ref, normed_ref):
    rows = x_ref.shape[1]
    branch = keep_ref[0] + arrived_ref[0, :rows, :].astype(F32) + across_ref[0].astype(F32)
    middle = x_ref[0].astype(F32) + branch + vec_ref[4:5, :]
    middle_ref[0] = middle
    hat, _ = norm_stats(middle)
    normed_ref[0] = (hat * vec_ref[5:6, :] + vec_ref[6:7, :]).astype(BF)


def middle_rows(x, keep, arrived, across, vec):
    micro, rows, model = x.shape
    one = per((rows, model))
    return pl.pallas_call(
        middle_kernel,
        grid=(micro,),
        in_specs=[one, one, per((2 * rows, model)), one, whole(vec)],
        out_specs=[one, one],
        out_shape=[shape_of(F32, micro, rows, model), shape_of(BF, micro, rows, model)],
        name="middle_rows",
    )(x, keep, arrived, across, vec)


def stack_parts(parts, refs, low, high, to_ref):
    for (block, start), part_ref in zip(parts, refs):
        first, last = max(start, low), min(start + part_ref.shape[0], high)
        to = block * (high - low) - low
        to_ref[to + first : to + last, :] = part_ref[first - start : last - start, :]


def parts_between(blocks, low, high):
    parts, arrays = [], []
    for block, pieces in enumerate(blocks):
        start = 0
        for piece in pieces:
            if start < high and start + piece.shape[0] > low:
                parts.append((block, start))
                arrays.append(piece)
            start += piece.shape[0]
    return parts, arrays


def pull_kernel(parts, g0, g1, g2, g3, *rest):
    *part_refs, pull_ref, grad_ref, down_ref = rest
    rows = g0.shape[1]
    each = down_ref.shape[0] // 8

    @pl.when(pl.program_id(0) == 0)
    def _():
        stack_parts(parts, part_refs, 0, each, down_ref)

    for i, block_ref in enumerate((g0, g1, g2, g3)):
        grad_ref[i * rows : (i + 1) * rows, :] = block_ref[0]
    pull_ref[0] = dot(grad_ref[...], down_ref[...], 1, 1).astype(BF)


def feed_pull(grads, blocks):
    micro, rows, model = grads[0].shape
    group = 4 * rows
    each = sum(p.shape[0] for p in blocks[0]) // 2
    hidden = 8 * each
    parts, arrays = parts_between(blocks, 0, each)
    return pl.pallas_call(
        partial(pull_kernel, parts),
        grid=(micro,),
        in_specs=[per((rows, model))] * 4 + [whole(b) for b in arrays],
        out_specs=per((group, hidden)),
        out_shape=shape_of(BF, micro, group, hidden),
        scratch_shapes=[pltpu.VMEM((group, model), BF), pltpu.VMEM((hidden, model), BF)],
        compiler_params=params(56),
        cost_estimate=pl.CostEstimate(
            flops=2 * micro * group * model * hidden,
            bytes_accessed=8 * micro * group * model,
            transcendentals=0,
        ),
        name="feed_pull",
    )(*grads, *arrays)


def feed_kernel(parts, x0, x1, x2, x3, pull_ref, bias_ref, *rest):
    *part_refs, active_ref, grad_hidden_ref, keep_ref, other_ref, send_ref, sum_ref, x_ref, up_ref = rest
    rows = x0.shape[1]
    each = up_ref.shape[0] // 8

    @pl.when(pl.program_id(0) == 0)
    def _():
        stack_parts(parts, part_refs, each, 2 * each, up_ref)
        sum_ref[...] = jnp.zeros_like(sum_ref)

    for i, block_ref in enumerate((x0, x1, x2, x3)):
        x_ref[i * rows : (i + 1) * rows, :] = block_ref[0]
    active, slope = gelu_parts(dot(x_ref[...], up_ref[...], 1, 1) + bias_ref[...])
    active_ref[0] = active.astype(BF)
    grad_hidden = (pull_ref[0].astype(F32) * slope).astype(BF)
    grad_hidden_ref[0] = grad_hidden
    sum_ref[...] += jnp.sum(grad_hidden.astype(F32), axis=0, keepdims=True)
    write_halves(dot(grad_hidden, up_ref[...], 1, 0), rows, keep_ref, other_ref, send_ref)


def halves_of(micro, rows, model):
    specs = [per((rows, model)), per((rows, model)), per((2 * rows, model))]
    return specs, [
        shape_of(F32, micro, rows, model), shape_of(BF, micro, rows, model),
        shape_of(BF, micro, 2 * rows, model),
    ]


def feed_forward(x, pull, blocks, bias):
    micro, rows, model = x[0].shape
    group = 4 * rows
    hidden = pull.shape[2]
    specs, shapes = halves_of(micro, rows, model)
    parts, arrays = parts_between(blocks, hidden // 8, hidden // 4)
    return pl.pallas_call(
        partial(feed_kernel, parts),
        grid=(micro,),
        in_specs=[per((rows, model))] * 4 + [per((group, hidden)), whole(bias)]
        + [whole(b) for b in arrays],
        out_specs=[per((group, hidden))] * 2 + specs + [full((1, hidden))],
        out_shape=[shape_of(BF, micro, group, hidden)] * 2 + shapes + [shape_of(F32, 1, hidden)],
        scratch_shapes=[pltpu.VMEM((group, model), BF), pltpu.VMEM((hidden, model), BF)],
        compiler_params=params(56),
        cost_estimate=pl.CostEstimate(
            flops=4 * micro * group * model * hidden,
            bytes_accessed=12 * micro * group * model,
            transcendentals=micro * group * hidden,
        ),
        name="feed_forward",
    )(*x, pull, bias, *arrays)


def feed_out_kernel(parts, active_ref, *rest):
    *part_refs, keep_ref, other_ref, send_ref, down_ref = rest

    @pl.when(pl.program_id(0) == 0)
    def _():
        stack_parts(parts, part_refs, 0, down_ref.shape[0] // 8, down_ref)

    write_halves(
        dot(active_ref[0], down_ref[...], 1, 0), keep_ref.shape[1], keep_ref, other_ref, send_ref
    )


def feed_out(active, blocks):
    micro, group, hidden = active.shape
    parts, arrays = parts_between(blocks, 0, hidden // 8)
    model = arrays[0].shape[1]
    specs, shapes = halves_of(micro, group // 4, model)
    return pl.pallas_call(
        partial(feed_out_kernel, parts),
        grid=(micro,),
        in_specs=[per((group, hidden))] + [whole(b) for b in arrays],
        out_specs=specs,
        out_shape=shapes,
        scratch_shapes=[pltpu.VMEM((hidden, model), BF)],
        compiler_params=params(56),
        cost_estimate=pl.CostEstimate(
            flops=2 * micro * group * model * hidden,
            bytes_accessed=8 * micro * group * model,
            transcendentals=0,
        ),
        name="feed_out",
    )(active, *arrays)


def rows_from(refs, to_ref):
    micro, rows, _ = refs[0].shape
    for m in range(micro):
        for i, block_ref in enumerate(refs):
            at = (4 * m + i) * rows
            to_ref[at : at + rows, :] = block_ref[m]


def feed_grads_kernel(active_ref, grad_hidden_ref, g0, g1, g2, g3, x0, x1, x2, x3, *rest):
    *outs, total_ref, right_ref = rest
    each = outs[0].shape[0] // 2
    step = pl.program_id(0)
    hidden = active_ref.shape[1]
    cut = hidden // 256 * 128
    for left_ref, refs, part in (
        (active_ref, (g0, g1, g2, g3), 0), (grad_hidden_ref, (x0, x1, x2, x3), 1)
    ):

        @pl.when(step == part)
        def _():
            rows_from(refs, right_ref)
            total_ref[:cut, :] = dot(left_ref[:, :cut], right_ref[...], 0, 0)
            total_ref[cut:, :] = dot(left_ref[:, cut:], right_ref[...], 0, 0)
            for i, out_ref in enumerate(outs):
                rows = total_ref[(i + 1) * each : (i + 2) * each, :].astype(BF)
                out_ref[part * each : (part + 1) * each, :] = rows


def feed_grads(active, grad_hidden, grad, x):
    rows, hidden = active.shape
    model = grad[0].shape[2]
    block = (hidden // 4, model)
    arrays = [active, grad_hidden, *grad, *x]
    return pl.pallas_call(
        feed_grads_kernel,
        grid=(2,),
        in_specs=[whole(a) for a in arrays],
        out_specs=[full(block)] * 7,
        out_shape=[shape_of(BF, *block)] * 7,
        scratch_shapes=[pltpu.VMEM((hidden, model), F32), pltpu.VMEM((rows, model), BF)],
        compiler_params=params(56),
        cost_estimate=pl.CostEstimate(
            flops=4 * rows * model * hidden, bytes_accessed=12 * rows * model, transcendentals=0
        ),
        name="feed_grads",
    )(*arrays)


def feed_grads_first_kernel(
    active_ref, grad_hidden_ref, g0, g1, g2, g3, x0, x1, x2, x3, out_ref, total_ref, right_ref
):
    each = out_ref.shape[0] // 2
    step = pl.program_id(0)
    for left_ref, refs, part in (
        (active_ref, (g0, g1, g2, g3), 0), (grad_hidden_ref, (x0, x1, x2, x3), 1)
    ):
        rows_from(refs, right_ref)
        rows = dot(left_ref[...], right_ref[...], 0, 0)[:each]
        at = slice(part * each, (part + 1) * each)

        @pl.when(step == 0)
        def _():
            total_ref[at, :] = rows

        @pl.when(step > 0)
        def _():
            total_ref[at, :] += rows

    @pl.when(step == pl.num_programs(0) - 1)
    def _():
        out_ref[...] = total_ref[...].astype(BF)


def feed_grads_first(active, grad_hidden, grad, x):
    rows, hidden = active.shape
    micro, own, model = grad[0].shape
    group = 4 * own
    block = (hidden // 4, model)
    left = pl.BlockSpec((group, 256), lambda i: (i, 0))
    return pl.pallas_call(
        feed_grads_first_kernel,
        grid=(micro,),
        in_specs=[left] * 2 + [per((own, model))] * 8,
        out_specs=full(block),
        out_shape=shape_of(BF, *block),
        scratch_shapes=[pltpu.VMEM(block, F32), pltpu.VMEM((group, model), BF)],
        compiler_params=params(56),
        cost_estimate=pl.CostEstimate(
            flops=rows * model * hidden // 2, bytes_accessed=8 * rows * model, transcendentals=0
        ),
        name="feed_grads_first",
    )(active, grad_hidden, *grad, *x)


def middle_pull_kernel(
    out_ref, middle_ref, keep_ref, arrived_ref, across_ref, vec_ref, grad_ref, branch_ref, sum_ref
):
    rows = out_ref.shape[1]
    back = keep_ref[0] + arrived_ref[0, :rows, :].astype(F32) + across_ref[0].astype(F32)
    hat, scale = norm_stats(middle_ref[0])
    out = out_ref[0].astype(F32)
    grad = out + norm_pull(back, hat, scale, vec_ref[5:6, :])
    grad_ref[0] = grad
    branch = grad.astype(BF)
    branch_ref[0] = branch

    @pl.when(pl.program_id(0) == 0)
    def _():
        sum_ref[...] = jnp.zeros_like(sum_ref)

    for i, terms in enumerate((branch.astype(F32), back * hat, back, out)):
        sum_ref[i : i + 1, :] += jnp.sum(terms, axis=0, keepdims=True)


def middle_pull(out, middle, keep, arrived, across, vec):
    micro, rows, model = out.shape
    one = per((rows, model))
    return pl.pallas_call(
        middle_pull_kernel,
        grid=(micro,),
        in_specs=[one, one, one, per((2 * rows, model)), one, whole(vec)],
        out_specs=[one, one, full((4, model))],
        out_shape=[
            shape_of(F32, micro, rows, model), shape_of(BF, micro, rows, model),
            shape_of(F32, 4, model),
        ],
        name="middle_pull",
    )(out, middle, keep, arrived, across, vec)


def attend_pull_kernel(
    place_ref, g0, g1, g2, g3, n0, n1, n2, n3, m0, m1, m2, m3, row_ref,
    qkv_ref, log_ref, heads_ref, normed_ref,
    keep_ref, other_ref, send_ref, k0, k1, k2, k3, s0, s1, s2, s3, bias_ref,
    grad_ref, grad_qkv_ref, total_ref, sum_ref, weight_ref, mask_ref,
):
    width = heads_ref.shape[2]
    count = width // HEAD_DIM
    rows = g0.shape[1]
    model = g0.shape[2]
    scale = HEAD_DIM ** (-0.5)
    step = pl.program_id(0)

    @pl.when(step == 0)
    def _():
        assemble(place_ref, (n0, n1, n2, n3), (m0, m1, m2, m3), weight_ref)

    write_mask(row_ref, mask_ref)
    for i, block_ref in enumerate((g0, g1, g2, g3)):
        grad_ref[i * rows : (i + 1) * rows, :] = block_ref[0]
    grad_heads = dot(grad_ref[...], weight_ref[3 * width :, :], 1, 1).astype(BF)
    for head in range(count):
        lanes = [slice(i * width + head * HEAD_DIM, i * width + (head + 1) * HEAD_DIM) for i in range(3)]
        queries, keys, values = [qkv_ref[0, :, part] for part in lanes]
        scores = dot(keys, queries * jnp.asarray(scale, BF), 1, 1) + mask_ref[...]
        probs = jnp.exp(scores - log_ref[0, head : head + 1, :])
        grad = grad_heads[:, lanes[0]]
        product = grad.astype(F32) * heads_ref[0, :, lanes[0]].astype(F32)
        delta = jnp.sum(jnp.transpose(product), axis=0, keepdims=True)
        grad_scores = (probs * (dot(values, grad, 1, 1) - delta)).astype(BF)
        grad_qkv_ref[:, lanes[0]] = jnp.transpose(scale * dot(keys, grad_scores, 0, 0)).astype(BF)
        grad_qkv_ref[:, lanes[1]] = (scale * dot(grad_scores, queries, 1, 0)).astype(BF)
        grad_qkv_ref[:, lanes[2]] = dot(probs.astype(BF), grad, 1, 0).astype(BF)
    write_halves(dot(grad_qkv_ref[...], weight_ref[: 3 * width, :], 1, 0), rows, keep_ref, other_ref, send_ref)
    qkv_part = dot(grad_qkv_ref[...], normed_ref[0], 0, 0)
    out_part = dot(heads_ref[0], grad_ref[...], 0, 0)
    sums = jnp.sum(grad_qkv_ref[...].astype(F32), axis=0, keepdims=True)

    @pl.when(step == 0)
    def _():
        total_ref[: 3 * width, :] = qkv_part
        total_ref[3 * width :, :] = out_part
        sum_ref[...] = jnp.broadcast_to(sums, sum_ref.shape)

    @pl.when(step > 0)
    def _():
        total_ref[: 3 * width, :] += qkv_part
        total_ref[3 * width :, :] += out_part
        sum_ref[...] += sums

    @pl.when(step == pl.num_programs(0) - 1)
    def _():
        z, y, ctx = place_ref[0], place_ref[1], place_ref[2]
        for k, pair in zip(SHIFTS, ((k0, s0), (k1, s1), (k2, s2), (k3, s3))):
            region = lax.rem(z + 4 - k, 4) * width
            for out_ref, half in zip(pair, (y, 1 - y)):
                start = pl.multiple_of(region + BODY * half, HEAD_DIM)
                out_ref[:BODY, :] = total_ref[pl.ds(start, BODY), :].astype(BF)
                start = pl.multiple_of(region + 2 * BODY + HALO * half, HALO)
                out_ref[BODY:, :] = total_ref[pl.ds(start, HALO), :].astype(BF)
        own = head_places((width, model), 0, ctx)
        hot = (lax.broadcasted_iota(jnp.int32, (width, model), 1) == own).astype(F32)
        for i, part in enumerate((0, 2)):
            line = lax.dot_general(
                sum_ref[:, part * width : (part + 1) * width],
                hot,
                (((1,), (0,)), ((), ())),
                preferred_element_type=F32,
                precision=lax.Precision.HIGHEST,
            )
            bias_ref[i : i + 1, :] = line[0:1]


def attend_pull(place, grads, near, side, row, qkv, log_total, heads, normed):
    micro, rows, model = grads[0].shape
    group = 4 * rows
    width = heads.shape[2]
    count = width // HEAD_DIM
    block = (BODY + HALO, model)
    one = per((rows, model))
    return pl.pallas_call(
        attend_pull_kernel,
        grid=(micro,),
        in_specs=[SCALARS] + [one] * 4 + [whole(b) for b in near + side] + [
            per(row.shape[1:]), per((group, 3 * width)), per((8, group)),
            per((group, width)), per((group, model)),
        ],
        out_specs=[one, one, per((2 * rows, model))] + [full(block)] * 8 + [full((2, model))],
        out_shape=[
            shape_of(F32, micro, rows, model), shape_of(BF, micro, rows, model),
            shape_of(BF, micro, 2 * rows, model),
        ] + [shape_of(BF, *block)] * 8 + [shape_of(F32, 2, model)],
        scratch_shapes=[
            pltpu.VMEM((group, model), BF), pltpu.VMEM((group, 3 * width), BF),
            pltpu.VMEM((4 * width, model), F32), pltpu.VMEM((8, 3 * width), F32),
            pltpu.VMEM((4 * width, model), BF), pltpu.VMEM((group, group), F32),
        ],
        compiler_params=params(60),
        cost_estimate=pl.CostEstimate(
            flops=2 * micro * group * model * 10 * width,
            bytes_accessed=12 * micro * group * model,
            transcendentals=micro * count * group * group,
        ),
        name="attend_pull",
    )(place, *grads, *near, *side, row, qkv, log_total, heads, normed)


def input_pull_kernel(
    x_ref, grad_ref, keep_ref, arrived_ref, across_ref, vec_ref, out_ref, sum_ref
):
    rows = x_ref.shape[1]
    back = keep_ref[0] + arrived_ref[0, :rows, :].astype(F32) + across_ref[0].astype(F32)
    hat, scale = norm_stats(x_ref[0].astype(F32))
    out = grad_ref[0] + norm_pull(back, hat, scale, vec_ref[0:1, :])
    out_ref[0] = jnp.transpose(out).astype(BF)

    @pl.when(pl.program_id(0) == 0)
    def _():
        sum_ref[...] = jnp.zeros_like(sum_ref)

    for i, terms in enumerate((back * hat, back)):
        sum_ref[i : i + 1, :] += jnp.sum(terms, axis=0, keepdims=True)


def input_pull(x, grad, keep, arrived, across, vec):
    micro, rows, model = x.shape
    one = per((rows, model))
    out, sums = pl.pallas_call(
        input_pull_kernel,
        grid=(micro,),
        in_specs=[one, one, one, per((2 * rows, model)), one, whole(vec)],
        out_specs=[per((model, rows)), full((2, model))],
        out_shape=[shape_of(BF, micro, model, rows), shape_of(F32, 2, model)],
        name="input_pull",
    )(x, grad, keep, arrived, across, vec)
    return out.transpose(0, 2, 1), sums


def mixed_kernel(middle_ref, keep_ref, arrived_ref, across_ref, vec_ref, out_ref):
    rows = middle_ref.shape[1]
    feed = keep_ref[0] + arrived_ref[0, :rows, :].astype(F32) + across_ref[0].astype(F32)
    out_ref[0] = jnp.transpose(middle_ref[0] + feed + vec_ref[7:8, :]).astype(BF)


def mixed_rows(middle, keep, arrived, across, vec):
    micro, rows, model = middle.shape
    one = per((rows, model))
    return pl.pallas_call(
        mixed_kernel,
        grid=(micro,),
        in_specs=[one, one, per((2 * rows, model)), one, whole(vec)],
        out_specs=per((model, rows)),
        out_shape=shape_of(BF, micro, model, rows),
        name="mixed_rows",
    )(middle, keep, arrived, across, vec).transpose(0, 2, 1)


def row_places(segments, rows):
    ctx = lax.axis_index("ctx")
    ranks = [ctx ^ j for j in BLOCKS]
    starts = segments[:, 0].reshape(-1, 4, rows).transpose(1, 0, 2)
    starts = jnp.concatenate([pick(starts, r) for r in ranks], axis=1)
    places = jnp.concatenate([r * rows + jnp.arange(rows, dtype=jnp.int32) for r in ranks])
    places = jnp.broadcast_to(places[None], starts.shape)
    return jnp.stack([starts, places] + [places] * 6, axis=1)


def own_up_bias(lines, order, width):
    table = lines[16:].reshape(order.shape[0], 4, width).transpose(1, 0, 2)
    return reorder(pick(table, lax.axis_index("ctx")), order).reshape(1, -1)


def vector_parts(first_sums, bias_sums, sums, up_sum, order, width):
    up_rows = reorder_back(up_sum.reshape(order.shape[0], width), order)
    mine = (jnp.arange(4) == lax.axis_index("ctx")).astype(F32)
    table = jnp.concatenate([first_sums, bias_sums, sums], axis=0)
    up_part = (up_rows[:, None, :] * mine[None, :, None]).reshape(-1)
    return jnp.concatenate([table.reshape(-1), up_part])


def flat(values):
    return values.reshape(-1, values.shape[-1])


def halo_pairs(back):
    pairs = []
    for p in range(8):
        for c in range(4):
            to = (c - 1) % 4 if (p % 2 == 1) != back else (c + 1) % 4
            pairs.append((p * 4 + c, p * 4 + to))
    return pairs


def aligned_block(w_attn, vectors, odd, ctx):
    turned = row_major(w_attn.T)
    width, model = turned.shape
    table = ctx_table(vectors, ctx).astype(BF).reshape(3, model // 2)
    edge = jnp.where(odd, turned[:HALO], turned[width - HALO :])
    halo = lax.ppermute(edge, BOTH, halo_pairs(False))
    none = jnp.zeros_like(halo)
    wide = jnp.concatenate(
        [jnp.where(odd, none, halo), turned, jnp.where(odd, halo, none)], axis=0
    )
    shift = HALO * odd.astype(jnp.int32)
    body = lax.dynamic_slice_in_dim(wide, HALO - 8 * ctx + shift, BODY, axis=0)
    extra = lax.dynamic_slice_in_dim(wide, width + shift, HALO, axis=0)
    extra = jnp.where(ctx == 3, extra, jnp.zeros_like(extra))
    lines = jnp.pad(table, ((0, 13), (0, model // 2)))
    return jnp.concatenate([body, extra, lines], axis=0)


def aligned_owned(own, odd, ctx, width):
    last = ctx == 3
    body, extra = own[:BODY], own[BODY:]
    tail = jnp.where(last, extra, body[BODY - HALO :])
    halo = lax.ppermute(jnp.where(odd, tail, body[:HALO]), BOTH, halo_pairs(True))
    halo = jnp.where(last & jnp.logical_not(odd), extra, halo)
    wide = jnp.where(
        odd, jnp.concatenate([halo, body], axis=0), jnp.concatenate([body, halo], axis=0)
    )
    return lax.dynamic_slice_in_dim(wide, 8 * ctx, width, axis=0)


def vector_rows(part, ctx):
    table = part.reshape(8, 4, -1).transpose(1, 0, 2)
    mine = jnp.stack([pick(table, ctx ^ j) for j in (0, 1)])
    far = jnp.stack([pick(table, ctx ^ j) for j in (2, 3)])
    mine = mine + lax.ppermute(far, "ctx", CHIP_PAIRS)
    return mine[0] + lax.ppermute(mine[1], "ctx", CORE_PAIRS)


def vector_sides(mine, y):
    sides = mine.reshape(4, 2, -1).transpose(1, 0, 2)
    return pick(sides, y) + lax.ppermute(pick(sides, 1 - y), "dp", SIDE_PAIRS)


def vector_owned(mine, z):
    total = pick(mine, z)
    for k in (1, 2, 3):
        total = total + to_shift(pick(mine, (z - k) % 4)[None], k, True)[0]
    return total


def both(keep, arrived):
    return keep.astype(F32) + arrived.astype(F32)


def aligned(tokens, cotangent, w_attn, w_up, w_down, vectors, segments):
    rows = tokens.shape[1]
    width = w_attn.shape[1]
    ctx, dp = lax.axis_index("ctx"), lax.axis_index("dp")
    z, y = dp // 2, dp % 2
    odd = y == 1
    place = jnp.stack([z, y, ctx]).astype(jnp.int32)
    order = jnp.stack(dp_order(z, y))
    tokens, cotangent = row_major(tokens), row_major(cotangent)
    row_info = row_places(segments, rows)
    feed = jnp.concatenate([w_down, w_up.T], axis=0)

    n0 = aligned_block(w_attn, vectors, odd, ctx)
    n0, t0, place, row_info, b0 = hold([n0, tokens, place, row_info, feed])
    n1, n3, s0, t1, c0 = (
        to_shift(n0, 1), to_shift(n0, 3), to_side(n0), to_chip(t0), to_side(b0[:CUT])
    )
    n0, n1, n3, s0, t0, t1, g0, b0, c0 = hold([n0, n1, n3, s0, t0, t1, cotangent, b0, c0])
    n2, s1, s3, g1 = to_shift(n0, 2), to_side(n1), to_side(n3), to_chip(g0)
    n0, n1, n2, n3, s0, s1, s3, t0, t1, g0, g1, b0 = hold(
        [n0, n1, n2, n3, s0, s1, s3, t0, t1, g0, g1, b0]
    )
    s2, b1, t2, t3 = to_side(n2), to_shift(b0, 1), to_core(t0), to_core(t1)
    n0, n1, n2, n3, s0, s1, s2, s3, t0, t1, t2, t3, g0, g1, b0, b1 = hold(
        [n0, n1, n2, n3, s0, s1, s2, s3, t0, t1, t2, t3, g0, g1, b0, b1]
    )
    b3, b2, c1, d0 = (
        to_shift(b0, 3), to_shift(b0[: THIRDS[0]], 2), to_side(b1), to_side(b0[CUT:])
    )
    normed_one, qkv, log_total, heads, lines, rest, keep, other, away = attend(
        place, [t0, t1, t2, t3], [n0, n1, n3, n2], [s0, s1, s3, s2], row_info
    )
    away, keep, other, b0, b1, b2, b3, c1, d0, g0, g1 = hold(
        [away, keep, other, b0, b1, b2, b3, c1, d0, g0, g1]
    )
    arrived = to_core(away)
    away, arrived, keep, b0, b2, b3, g0, g1 = hold(
        [half_sum(other, arrived), arrived, keep, b0, b2, b3, g0, g1]
    )
    across, d2, c3 = to_chip(away), to_shift(b0[THIRDS[0] : THIRDS[1]], 2), to_side(b3)
    g2, g3 = to_core(g0), to_core(g1)
    across, arrived, keep, b0, d2, c3, b2, g2, g3 = hold(
        [across, arrived, keep, b0, d2, c3, b2, g2, g3]
    )
    middle, h0 = middle_rows(tokens, keep, arrived, across, lines)
    h0, middle, b0, d2, b2 = hold([h0, middle, b0, d2, b2])
    h1, e2, f2, c2 = to_chip(h0), to_shift(b0[THIRDS[1] :], 2), to_side(d2), to_side(b2)
    up_bias = own_up_bias(rest, order, width)
    h0, h1, e2, f2, c2, up_bias = hold([h0, h1, e2, f2, c2, up_bias])
    h2, h3, a2 = to_core(h0), to_core(h1), to_side(e2)
    blocks = [[c2, f2, a2], [b2, d2, e2], [b0], [c0, d0], [b1], [c1], [b3], [c3]]
    pull = feed_pull([g0, g1, g2, g3], blocks)
    h0, h1, h2, h3, pull = hold([h0, h1, h2, h3, pull], a2)
    active, grad_hidden, keep, other, away, up_sum = feed_forward(
        [h0, h1, h2, h3], pull, blocks, up_bias
    )
    x_all, grad_all = [h0, h1, h2, h3], [g0, g1, g2, g3]

    arrived = to_core(away)
    q2 = feed_grads_first(flat(active), flat(grad_hidden), grad_all, x_all)
    away, arrived, keep, active, q2 = hold(
        [half_sum(other, arrived), arrived, keep, active, q2]
    )
    across, q2 = to_chip(away), to_side(q2)
    p2, p0, q0, p1, q1, p3, q3 = feed_grads(flat(active), flat(grad_hidden), grad_all, x_all)
    across, arrived, keep, p2, q2 = hold([across, arrived, keep, p2, q2])
    grad_middle, h0, sums = middle_pull(cotangent, middle, keep, arrived, across, lines)
    h0, p2, q3, grad_middle, active = hold([h0, both(p2, q2).astype(BF), q3, grad_middle, active])
    h1, h2, r2, q3 = to_chip(h0), to_core(h0), to_shift(p2[:BACK_CUT], 2, True), to_side(q3)
    feed_keep, feed_other, feed_away = feed_out(active, blocks)
    h0, h1, h2, r2, q3, p2, feed_away = hold([h0, h1, h2, r2, q3, p2, feed_away])
    h3, feed_arrived = to_core(h1), to_core(feed_away)
    h0, h1, h2, h3, p2, p3, q1, q0, feed_arrived = hold(
        [h0, h1, h2, h3, p2, both(p3, q3).astype(BF), q1, q0, feed_arrived]
    )
    t2, r3 = to_shift(p2[BACK_CUT:], 2, True), to_shift(p3, 3, True)
    q1, q0 = to_side(q1), to_side(q0)
    keep, other, away, *parts, bias_sums = attend_pull(
        place, [h0, h1, h2, h3], [n0, n1, n3, n2], [s0, s1, s3, s2], row_info,
        qkv, log_total, heads, normed_one,
    )
    away, t2, r3, q1, q0, p0, p1, *parts = hold([away, t2, r3, q1, q0, p0, p1] + parts)
    k0, k1, k3, k2, l0, l1, l3, l2 = parts
    arrived = to_core(away)
    away, arrived, keep, p1, l1, l2, l3 = hold(
        [half_sum(other, arrived), arrived, keep, both(p1, q1).astype(BF), l1, l2, l3]
    )
    r1, across, l2, l1 = to_shift(p1, 1, True), to_chip(away), to_side(l2), to_side(l1)
    across, arrived, keep, r1, k1, k2, l0, l3, feed_away = hold(
        [
            across, arrived, keep, r1, both(k1, l1).astype(BF), both(k2, l2).astype(BF),
            l0, l3, half_sum(feed_other, feed_arrived),
        ]
    )
    k2, k1, l3, l0, feed_across = (
        to_shift(k2, 2, True), to_shift(k1, 1, True), to_side(l3), to_side(l0),
        to_chip(feed_away),
    )
    input_grad, first_sums = input_pull(tokens, grad_middle, keep, arrived, across, lines)
    part = vector_parts(first_sums, bias_sums, sums, up_sum, order, width)
    k1, k2, k3, l0, part, feed_across, input_grad = hold(
        [k1, k2, both(k3, l3).astype(BF), l0, part, feed_across, input_grad]
    )
    k3, part = to_shift(k3, 3, True), vector_rows(part, ctx)
    k1, k2, k3, part = hold([k1, k2, k3, part])
    own = both(k0, l0) + k1.astype(F32) + k2.astype(F32) + k3.astype(F32)
    attn_owned = aligned_owned(own, odd, ctx, width).T
    part = vector_sides(part, y)
    mixed = mixed_rows(middle, feed_keep, feed_arrived, feed_across, lines)
    terms = [p0, q0, r1, jnp.concatenate([r2, t2], axis=0), r3]
    down_owned = sum(t[:width].astype(F32) for t in terms)
    up_owned = sum(t[width:].astype(F32) for t in terms).T
    part, mixed, down_owned, up_owned, attn_owned = hold(
        [part, mixed, down_owned, up_owned, attn_owned]
    )
    return mixed, input_grad, attn_owned, up_owned, down_owned, vector_owned(part, z)


def plain(tokens, cotangent, w_attn, w_up, w_down, vectors, segments):
    micro, rows, model = tokens.shape
    width = w_attn.shape[1]
    ctx = lax.axis_index("ctx")
    last = ctx == lax.axis_size("ctx") - 1
    place = jnp.stack([jnp.zeros((), ctx.dtype), jnp.zeros((), ctx.dtype), ctx])
    order = jnp.arange(lax.axis_size("dp"))
    table = lax.all_gather(w_attn.T, BOTH, axis=0, tiled=True)
    lines = lax.all_gather(vectors, BOTH, axis=0, tiled=True).reshape(24, model // 2)
    lines = jnp.pad(lines, ((0, 0), (0, model // 2)))
    near, side = [], []
    for region in (-k % 4 for k in SHIFTS):
        part = head_rows(table[region * model : (region + 1) * model], ctx, last)
        for blocks, half in ((near, 0), (side, 1)):
            line = 3 * (2 * region + half)
            blocks.append(
                jnp.concatenate(
                    [
                        part[BODY * half : BODY * (half + 1)],
                        part[2 * BODY + HALO * half : 2 * BODY + HALO * (half + 1)],
                        jnp.pad(lines[line : line + 3], ((0, 13), (0, 0))),
                    ],
                    axis=0,
                )
            )
    up = lax.all_gather(w_up.T, "dp", axis=0, tiled=True)
    down = lax.all_gather(w_down, "dp", axis=0, tiled=True)
    each = up.shape[0] // 8
    blocks = [
        jnp.concatenate([w[i * each : (i + 1) * each] for w in (down, up)], axis=0)
        for i in range(8)
    ]
    blocks = [[b] for b in blocks]
    row_info = row_places(segments, rows)

    normed_one, qkv, log_total, heads, lines, rest, *halves = attend(
        place, row_gather(tokens), near, side, row_info
    )
    middle, normed_two = middle_rows(tokens, *row_scatter(*halves), lines)
    x_all, grad_all = row_gather(normed_two), row_gather(cotangent)
    active, grad_hidden, *halves, up_sum = feed_forward(
        x_all, feed_pull(grad_all, blocks), blocks, own_up_bias(rest, order, width)
    )
    mixed = mixed_rows(middle, *row_scatter(*feed_out(active, blocks)), lines)
    grad_middle, branch, sums = middle_pull(cotangent, middle, *row_scatter(*halves), lines)
    arrays = flat(active), flat(grad_hidden), grad_all, x_all
    parts = [feed_grads_first(*arrays)] + list(feed_grads(*arrays))
    down_owned, up_owned = [
        lax.psum_scatter(
            jnp.concatenate([p[i * each : (i + 1) * each] for p in parts], axis=0),
            "dp", scatter_dimension=0, tiled=True,
        ).astype(F32)
        for i in range(2)
    ]
    *halves, k0, k1, k2, k3, s0, s1, s2, s3, bias_sums = attend_pull(
        place, row_gather(branch), near, side, row_info, qkv, log_total, heads, normed_one
    )
    input_grad, first_sums = input_pull(tokens, grad_middle, *row_scatter(*halves), lines)
    parts = []
    for region in range(4):
        at = SHIFTS.index(-region % 4)
        first, second = (k0, k1, k2, k3)[at], (s0, s1, s2, s3)[at]
        part = [first[:BODY], second[:BODY], first[BODY:], second[BODY:]]
        parts.append(head_rows_back(jnp.concatenate(part, axis=0), ctx, last))
    attn_owned = lax.psum_scatter(
        jnp.concatenate(parts, axis=0), BOTH, scatter_dimension=0, tiled=True
    ).astype(F32)
    part = vector_parts(first_sums, bias_sums, sums, up_sum, order, width)
    vector_grad = lax.psum_scatter(part, BOTH, scatter_dimension=0, tiled=True)
    return (mixed, input_grad, attn_owned.T, up_owned.T, down_owned, vector_grad)


def shards(*arrays):
    fits = lax.axis_size("dp") == 8 and lax.axis_size("ctx") == 4
    return (aligned if fits and arrays[2].shape == (1088, 136) else plain)(*arrays)


def solution(mesh):
    return jax.shard_map(
        shards,
        mesh=mesh,
        in_specs=(
            P(None, BOTH, None),
            P(None, BOTH, None),
            P(None, BOTH),
            P(None, BOTH),
            P(BOTH, None),
            P(BOTH),
            P(None, "dp", None),
        ),
        out_specs=(
            P(None, BOTH, None),
            P(None, BOTH, None),
            P(None, BOTH),
            P(None, BOTH),
            P(BOTH, None),
            P(BOTH),
        ),
        check_vma=False,
    )
```

```python
from functools import partial

import jax
import jax.numpy as jnp
from jax import lax
from jax.experimental import pallas as pl
from jax.experimental.layout import Layout, with_layout_constraint
from jax.experimental.pallas import tpu as pltpu
from jax.sharding import PartitionSpec as P

HEAD_DIM = 64
HALO = 32
BODY = 128
NEG_FILL = -1e30
EPSILON = 1e-05
BF = jnp.bfloat16
F32 = jnp.float32
BOTH = ("dp", "ctx")
CORE_PAIRS = [(0, 1), (1, 0), (2, 3), (3, 2)]
CHIP_PAIRS = [(0, 2), (2, 0), (1, 3), (3, 1)]
BLOCKS = (0, 2, 1, 3)
SHIFTS = (0, 1, 3, 2)
ORDER = ((2, 1), (2, 0), (0, 0), (0, 1), (1, 0), (1, 1), (3, 0), (3, 1))
THIRDS = (64, 160)
CUT = 144
BACK_CUT = 112
SIDE_PAIRS = [(p, p ^ 1) for p in range(8)]


def shift_pairs(step):
    return [(z * 2 + y, ((z + step) % 4) * 2 + y) for z in range(4) for y in range(2)]


def dot(left, right, left_dim, right_dim):
    return lax.dot_general(
        left, right, (((left_dim,), (right_dim,)), ((), ())), preferred_element_type=F32
    )


def norm_stats(values):
    centred = values - jnp.mean(values, axis=-1, keepdims=True)
    scale = lax.rsqrt(jnp.mean(centred * centred, axis=-1, keepdims=True) + EPSILON)
    return centred * scale, scale


def norm_pull(grad, hat, scale, gain):
    grad_hat = grad * gain
    along = jnp.mean(grad_hat * hat, axis=-1, keepdims=True)
    return scale * (grad_hat - jnp.mean(grad_hat, axis=-1, keepdims=True) - hat * along)


def row_major(value):
    return with_layout_constraint(value, Layout(tuple(range(value.ndim))))


def send(value, axes, pairs):
    rows = value.shape[-2]
    if rows % 16:
        return lax.ppermute(value, axes, pairs)
    cut = value.reshape(value.shape[:-2] + (rows // 16, 16, value.shape[-1]))
    return lax.ppermute(cut, axes, pairs).reshape(value.shape)


def hold(values, *others):
    return lax.optimization_barrier(tuple(values) + tuple(others))[: len(values)]


def to_core(value):
    return send(value, "ctx", CORE_PAIRS)


def to_chip(value):
    return send(value, "ctx", CHIP_PAIRS)


def to_side(value):
    return send(value, "dp", SIDE_PAIRS)


def to_shift(value, step, back=False):
    pairs = shift_pairs(step)
    return send(value, "dp", [(b, a) for a, b in pairs] if back else pairs)


def row_gather(mine):
    across = to_chip(mine)
    return [mine, across, to_core(mine), to_core(across)]


def half_sum(other, arrived):
    rows = other.shape[1]
    return (other.astype(F32) + arrived[:, rows:].astype(F32)).astype(BF)


def row_scatter(keep, other, away):
    arrived = to_core(away)
    return keep, arrived, to_chip(half_sum(other, arrived))


def dp_order(z, y):
    return [((z - k) % 4) * 2 + (y ^ s) for k, s in ORDER]


def pick(stacked, index):
    return lax.dynamic_index_in_dim(stacked, index, axis=0, keepdims=False)


def reorder(table, order):
    hot = (order[:, None] == jnp.arange(table.shape[0])[None, :]).astype(F32)
    return jnp.sum(hot[:, :, None] * table[None], axis=1)


def reorder_back(table, order):
    hot = (order[:, None] == jnp.arange(table.shape[0])[None, :]).astype(F32)
    return jnp.sum(hot[:, :, None] * table[:, None, :], axis=0)


def ctx_table(mine, ctx):
    across = lax.ppermute(mine[None], "ctx", CHIP_PAIRS)
    pair = jnp.concatenate([mine[None], across], axis=0)
    table = jnp.concatenate([pair, lax.ppermute(pair, "ctx", CORE_PAIRS)], axis=0)
    return reorder_back(table.astype(F32), jnp.stack([ctx ^ j for j in BLOCKS]))


def head_rows(table, ctx, last):
    middle = 8 * HEAD_DIM
    first = lax.dynamic_slice_in_dim(table, 128 * ctx, 128, axis=0)
    second = lax.dynamic_slice_in_dim(table, middle + HEAD_DIM + 128 * ctx, 128, axis=0)
    mid = table[middle : middle + HEAD_DIM]
    return jnp.concatenate([first, second, jnp.where(last, mid, jnp.zeros_like(mid))], axis=0)


def head_rows_back(mine, ctx, last):
    middle = 8 * HEAD_DIM
    table = jnp.zeros((2 * middle + HEAD_DIM,) + mine.shape[1:], mine.dtype)
    table = lax.dynamic_update_slice_in_dim(table, mine[:128], 128 * ctx, axis=0)
    table = lax.dynamic_update_slice_in_dim(
        table, mine[128:256], middle + HEAD_DIM + 128 * ctx, axis=0
    )
    mid = jnp.where(last, mine[256:], jnp.zeros_like(mine[256:]))
    return lax.dynamic_update_slice_in_dim(table, mid, middle, axis=0)


def gelu_parts(hidden):
    factor = 0.7978845608028654
    square = hidden * hidden
    bent = jnp.tanh(factor * hidden * (1.0 + 0.044715 * square))
    active = 0.5 * hidden * (1.0 + bent)
    slope = 0.5 * (1.0 + bent) + 0.5 * hidden * (1.0 - bent * bent) * factor * (
        1.0 + 3 * 0.044715 * square
    )
    return active, slope


def full(shape):
    return pl.BlockSpec(shape, lambda *_: (0,) * len(shape))


def per(shape, step=1):
    return pl.BlockSpec((1,) + shape, lambda i: (i // step,) + (0,) * len(shape))


def params(mib):
    return pltpu.CompilerParams(vmem_limit_bytes=mib * 1024 * 1024)


def whole(array):
    return full(array.shape)


SCALARS = pl.BlockSpec(memory_space=pltpu.SMEM)


def shape_of(dtype, *dims):
    return jax.ShapeDtypeStruct(dims, dtype)


def head_places(shape, axis, ctx):
    own = lax.broadcasted_iota(jnp.int32, shape, axis)
    middle = 8 * HEAD_DIM
    shift = jnp.where(own < BODY, BODY * ctx, middle + HEAD_DIM - BODY + BODY * ctx)
    shift = jnp.where(own < 2 * BODY, shift, middle - 2 * BODY)
    return jnp.where((own < 2 * BODY) | (ctx == 3), own + shift, -1)


def write_halves(values, rows, keep_ref, other_ref, send_ref):
    keep_ref[0] = values[:rows]
    other_ref[0] = values[rows : 2 * rows].astype(BF)
    send_ref[0] = values[2 * rows :].astype(BF)


def assemble(place_ref, near, side, weight_ref):
    width = weight_ref.shape[0] // 4
    z, y = place_ref[0], place_ref[1]
    for k, pair in zip(SHIFTS, zip(near, side)):
        region = lax.rem(z + 4 - k, 4) * width
        for block_ref, half in zip(pair, (y, 1 - y)):
            to = pl.multiple_of(region + BODY * half, HEAD_DIM)
            weight_ref[pl.ds(to, BODY), :] = block_ref[:BODY, :]
            to = pl.multiple_of(region + 2 * BODY + HALO * half, HALO)
            weight_ref[pl.ds(to, HALO), :] = block_ref[BODY : BODY + HALO, :]


def write_mask(row_ref, mask_ref):
    row = row_ref[0].astype(F32)
    first, own = row[0:1], row[1:2]
    square = (128, row.shape[1])
    first_col = jnp.transpose(jnp.broadcast_to(first, square))[:, :1]
    own_col = jnp.transpose(jnp.broadcast_to(own, square))[:, :1]
    allowed = (own_col <= own) & (first_col == first)
    mask_ref[...] = jnp.where(allowed, 0.0, NEG_FILL)


def attend_kernel(
    place_ref, x0, x1, x2, x3, n0, n1, n2, n3, s0, s1, s2, s3, row_ref,
    normed_ref, qkv_ref, log_ref, heads_ref, vec_ref, line_ref,
    keep_ref, other_ref, send_ref, weight_ref, mask_ref, bias_ref,
):
    width = heads_ref.shape[2]
    count = width // HEAD_DIM
    model = vec_ref.shape[1]
    part = model // 2
    rows = x0.shape[1]

    @pl.when(pl.program_id(0) == 0)
    def _():
        z, y, ctx = place_ref[0], place_ref[1], place_ref[2]
        assemble(place_ref, (n0, n1, n2, n3), (s0, s1, s2, s3), weight_ref)
        for k, pair in zip(SHIFTS, ((n0, s0), (n1, s1), (n2, s2), (n3, s3))):
            owner = lax.rem(z + 4 - k, 4)
            for block_ref, half in zip(pair, (y, 1 - y)):
                lines = block_ref[BODY + HALO :, :].astype(F32)
                for i in range(3):
                    line_ref[pl.ds(3 * (2 * owner + half) + i, 1), :] = lines[i : i + 1, :part]
        for i in range(8):
            vec_ref[i : i + 1, :part] = line_ref[2 * i : 2 * i + 1, :]
            vec_ref[i : i + 1, part:] = line_ref[2 * i + 1 : 2 * i + 2, :]
        own = head_places((model, width), 1, ctx)
        hot = (lax.broadcasted_iota(jnp.int32, (model, width), 0) == own).astype(F32).astype(BF)
        own_vec = dot(vec_ref[...].astype(BF), hot, 1, 0)
        bias_ref[:, :width] = own_vec[2:3]
        bias_ref[:, width : 2 * width] = jnp.zeros((1, width), F32)
        bias_ref[:, 2 * width :] = own_vec[3:4]

    gain, bias = vec_ref[0:1, :], vec_ref[1:2, :]
    for i, x_ref in enumerate((x0, x1, x2, x3)):
        hat, _ = norm_stats(x_ref[0].astype(F32))
        normed_ref[0, i * rows : (i + 1) * rows, :] = (hat * gain + bias).astype(BF)
    normed = normed_ref[0]
    qkv_ref[0] = (dot(normed, weight_ref[: 3 * width, :], 1, 1) + bias_ref[...]).astype(BF)
    write_mask(row_ref, mask_ref)
    for head in range(count):
        lanes = [slice(i * width + head * HEAD_DIM, i * width + (head + 1) * HEAD_DIM) for i in range(3)]
        queries, keys, values = [qkv_ref[0, :, part] for part in lanes]
        queries = queries * jnp.asarray(HEAD_DIM ** (-0.5), BF)
        scores = dot(keys, queries, 1, 1) + mask_ref[...]
        top = jnp.max(scores, axis=0, keepdims=True)
        weights = jnp.exp(scores - top)
        total = jnp.sum(weights, axis=0, keepdims=True)
        probs = (weights * (1.0 / total)).astype(BF)
        log_ref[0, head : head + 1, :] = top + jnp.log(total)
        heads_ref[0, :, lanes[0]] = jnp.transpose(dot(values, probs, 0, 0)).astype(BF)
    branch = dot(heads_ref[0], weight_ref[3 * width :, :], 1, 0)
    write_halves(branch, rows, keep_ref, other_ref, send_ref)


def attend(place, blocks, near, side, row):
    micro, rows, model = blocks[0].shape
    group = 4 * rows
    width = 2 * (BODY + HALO)
    count = width // HEAD_DIM
    return pl.pallas_call(
        attend_kernel,
        grid=(micro,),
        in_specs=[SCALARS] + [per((rows, model))] * 4
        + [whole(b) for b in near + side] + [per(row.shape[1:])],
        out_specs=[
            per((group, model)), per((group, 3 * width)), per((8, group)),
            per((group, width)), full((8, model)), full((24, model // 2)),
            per((rows, model)), per((rows, model)), per((2 * rows, model)),
        ],
        out_shape=[
            shape_of(BF, micro, group, model), shape_of(BF, micro, group, 3 * width),
            shape_of(F32, micro, 8, group), shape_of(BF, micro, group, width),
            shape_of(F32, 8, model),
            shape_of(F32, 24, model // 2), shape_of(F32, micro, rows, model),
            shape_of(BF, micro, rows, model), shape_of(BF, micro, 2 * rows, model),
        ],
        scratch_shapes=[
            pltpu.VMEM((4 * width, model), BF), pltpu.VMEM((group, group), F32),
            pltpu.VMEM((1, 3 * width), F32),
        ],
        compiler_params=params(56),
        cost_estimate=pl.CostEstimate(
            flops=2 * micro * group * model * 4 * width,
            bytes_accessed=12 * micro * group * model,
            transcendentals=micro * count * group * group,
        ),
        name="attend",
    )(place, *blocks, *near, *side, row)


def middle_kernel(x_ref, keep_ref, arrived_ref, across_ref, vec_ref, middle_ref, normed_ref):
    rows = x_ref.shape[1]
    branch = keep_ref[0] + arrived_ref[0, :rows, :].astype(F32) + across_ref[0].astype(F32)
    middle = x_ref[0].astype(F32) + branch + vec_ref[4:5, :]
    middle_ref[0] = middle
    hat, _ = norm_stats(middle)
    normed_ref[0] = (hat * vec_ref[5:6, :] + vec_ref[6:7, :]).astype(BF)


def middle_rows(x, keep, arrived, across, vec):
    micro, rows, model = x.shape
    one = per((rows, model))
    return pl.pallas_call(
        middle_kernel,
        grid=(micro,),
        in_specs=[one, one, per((2 * rows, model)), one, whole(vec)],
        out_specs=[one, one],
        out_shape=[shape_of(F32, micro, rows, model), shape_of(BF, micro, rows, model)],
        name="middle_rows",
    )(x, keep, arrived, across, vec)


def stack_parts(parts, refs, low, high, to_ref):
    for (block, start), part_ref in zip(parts, refs):
        first, last = max(start, low), min(start + part_ref.shape[0], high)
        to = block * (high - low) - low
        to_ref[to + first : to + last, :] = part_ref[first - start : last - start, :]


def parts_between(blocks, low, high):
    parts, arrays = [], []
    for block, pieces in enumerate(blocks):
        start = 0
        for piece in pieces:
            if start < high and start + piece.shape[0] > low:
                parts.append((block, start))
                arrays.append(piece)
            start += piece.shape[0]
    return parts, arrays


def pull_kernel(parts, g0, g1, g2, g3, *rest):
    *part_refs, pull_ref, grad_ref, down_ref = rest
    rows = g0.shape[1]
    each = down_ref.shape[0] // 8

    @pl.when(pl.program_id(0) == 0)
    def _():
        stack_parts(parts, part_refs, 0, each, down_ref)

    for i, block_ref in enumerate((g0, g1, g2, g3)):
        grad_ref[i * rows : (i + 1) * rows, :] = block_ref[0]
    pull_ref[0] = dot(grad_ref[...], down_ref[...], 1, 1).astype(BF)


def feed_pull(grads, blocks):
    micro, rows, model = grads[0].shape
    group = 4 * rows
    each = sum(p.shape[0] for p in blocks[0]) // 2
    hidden = 8 * each
    parts, arrays = parts_between(blocks, 0, each)
    return pl.pallas_call(
        partial(pull_kernel, parts),
        grid=(micro,),
        in_specs=[per((rows, model))] * 4 + [whole(b) for b in arrays],
        out_specs=per((group, hidden)),
        out_shape=shape_of(BF, micro, group, hidden),
        scratch_shapes=[pltpu.VMEM((group, model), BF), pltpu.VMEM((hidden, model), BF)],
        compiler_params=params(56),
        cost_estimate=pl.CostEstimate(
            flops=2 * micro * group * model * hidden,
            bytes_accessed=8 * micro * group * model,
            transcendentals=0,
        ),
        name="feed_pull",
    )(*grads, *arrays)


def feed_kernel(parts, x0, x1, x2, x3, pull_ref, bias_ref, *rest):
    *part_refs, active_ref, grad_hidden_ref, keep_ref, other_ref, send_ref, sum_ref, x_ref, up_ref = rest
    rows = x0.shape[1]
    each = up_ref.shape[0] // 8

    @pl.when(pl.program_id(0) == 0)
    def _():
        stack_parts(parts, part_refs, each, 2 * each, up_ref)
        sum_ref[...] = jnp.zeros_like(sum_ref)

    for i, block_ref in enumerate((x0, x1, x2, x3)):
        x_ref[i * rows : (i + 1) * rows, :] = block_ref[0]
    active, slope = gelu_parts(dot(x_ref[...], up_ref[...], 1, 1) + bias_ref[...])
    active_ref[0] = active.astype(BF)
    grad_hidden = (pull_ref[0].astype(F32) * slope).astype(BF)
    grad_hidden_ref[0] = grad_hidden
    sum_ref[...] += jnp.sum(grad_hidden.astype(F32), axis=0, keepdims=True)
    write_halves(dot(grad_hidden, up_ref[...], 1, 0), rows, keep_ref, other_ref, send_ref)


def halves_of(micro, rows, model):
    specs = [per((rows, model)), per((rows, model)), per((2 * rows, model))]
    return specs, [
        shape_of(F32, micro, rows, model), shape_of(BF, micro, rows, model),
        shape_of(BF, micro, 2 * rows, model),
    ]


def feed_forward(x, pull, blocks, bias):
    micro, rows, model = x[0].shape
    group = 4 * rows
    hidden = pull.shape[2]
    specs, shapes = halves_of(micro, rows, model)
    parts, arrays = parts_between(blocks, hidden // 8, hidden // 4)
    return pl.pallas_call(
        partial(feed_kernel, parts),
        grid=(micro,),
        in_specs=[per((rows, model))] * 4 + [per((group, hidden)), whole(bias)]
        + [whole(b) for b in arrays],
        out_specs=[per((group, hidden))] * 2 + specs + [full((1, hidden))],
        out_shape=[shape_of(BF, micro, group, hidden)] * 2 + shapes + [shape_of(F32, 1, hidden)],
        scratch_shapes=[pltpu.VMEM((group, model), BF), pltpu.VMEM((hidden, model), BF)],
        compiler_params=params(56),
        cost_estimate=pl.CostEstimate(
            flops=4 * micro * group * model * hidden,
            bytes_accessed=12 * micro * group * model,
            transcendentals=micro * group * hidden,
        ),
        name="feed_forward",
    )(*x, pull, bias, *arrays)


def feed_out_kernel(parts, active_ref, *rest):
    *part_refs, keep_ref, other_ref, send_ref, down_ref = rest

    @pl.when(pl.program_id(0) == 0)
    def _():
        stack_parts(parts, part_refs, 0, down_ref.shape[0] // 8, down_ref)

    write_halves(
        dot(active_ref[0], down_ref[...], 1, 0), keep_ref.shape[1], keep_ref, other_ref, send_ref
    )


def feed_out(active, blocks):
    micro, group, hidden = active.shape
    parts, arrays = parts_between(blocks, 0, hidden // 8)
    model = arrays[0].shape[1]
    specs, shapes = halves_of(micro, group // 4, model)
    return pl.pallas_call(
        partial(feed_out_kernel, parts),
        grid=(micro,),
        in_specs=[per((group, hidden))] + [whole(b) for b in arrays],
        out_specs=specs,
        out_shape=shapes,
        scratch_shapes=[pltpu.VMEM((hidden, model), BF)],
        compiler_params=params(56),
        cost_estimate=pl.CostEstimate(
            flops=2 * micro * group * model * hidden,
            bytes_accessed=8 * micro * group * model,
            transcendentals=0,
        ),
        name="feed_out",
    )(active, *arrays)


def rows_from(refs, to_ref):
    micro, rows, _ = refs[0].shape
    for m in range(micro):
        for i, block_ref in enumerate(refs):
            at = (4 * m + i) * rows
            to_ref[at : at + rows, :] = block_ref[m]


def feed_grads_kernel(active_ref, grad_hidden_ref, g0, g1, g2, g3, x0, x1, x2, x3, *rest):
    *outs, total_ref, right_ref = rest
    each = outs[0].shape[0] // 2
    step = pl.program_id(0)
    hidden = active_ref.shape[1]
    cut = hidden // 256 * 128
    for left_ref, refs, part in (
        (active_ref, (g0, g1, g2, g3), 0), (grad_hidden_ref, (x0, x1, x2, x3), 1)
    ):

        @pl.when(step == part)
        def _():
            rows_from(refs, right_ref)
            total_ref[:cut, :] = dot(left_ref[:, :cut], right_ref[...], 0, 0)
            total_ref[cut:, :] = dot(left_ref[:, cut:], right_ref[...], 0, 0)
            for i, out_ref in enumerate(outs):
                rows = total_ref[(i + 1) * each : (i + 2) * each, :].astype(BF)
                out_ref[part * each : (part + 1) * each, :] = rows


def feed_grads(active, grad_hidden, grad, x):
    rows, hidden = active.shape
    model = grad[0].shape[2]
    block = (hidden // 4, model)
    arrays = [active, grad_hidden, *grad, *x]
    return pl.pallas_call(
        feed_grads_kernel,
        grid=(2,),
        in_specs=[whole(a) for a in arrays],
        out_specs=[full(block)] * 7,
        out_shape=[shape_of(BF, *block)] * 7,
        scratch_shapes=[pltpu.VMEM((hidden, model), F32), pltpu.VMEM((rows, model), BF)],
        compiler_params=params(56),
        cost_estimate=pl.CostEstimate(
            flops=4 * rows * model * hidden, bytes_accessed=12 * rows * model, transcendentals=0
        ),
        name="feed_grads",
    )(*arrays)


def feed_grads_first_kernel(
    active_ref, grad_hidden_ref, g0, g1, g2, g3, x0, x1, x2, x3, first_ref, second_ref,
    total_ref, right_ref,
):
    each = total_ref.shape[0] // 2
    cut = first_ref.shape[0]
    step = pl.program_id(0)
    for left_ref, refs, part in (
        (active_ref, (g0, g1, g2, g3), 0), (grad_hidden_ref, (x0, x1, x2, x3), 1)
    ):
        rows_from(refs, right_ref)
        rows = dot(left_ref[...], right_ref[...], 0, 0)[:each]
        at = slice(part * each, (part + 1) * each)

        @pl.when(step == 0)
        def _():
            total_ref[at, :] = rows

        @pl.when(step > 0)
        def _():
            total_ref[at, :] += rows

    @pl.when(step == pl.num_programs(0) - 1)
    def _():
        first_ref[...] = total_ref[:cut, :].astype(BF)
        second_ref[...] = total_ref[cut:, :].astype(BF)


def feed_grads_first(active, grad_hidden, grad, x):
    rows, hidden = active.shape
    micro, own, model = grad[0].shape
    group = 4 * own
    block = (hidden // 4, model)
    left = pl.BlockSpec((group, 256), lambda i: (i, 0))
    return pl.pallas_call(
        feed_grads_first_kernel,
        grid=(micro,),
        in_specs=[left] * 2 + [per((own, model))] * 8,
        out_specs=[full((BACK_CUT, model)), full((block[0] - BACK_CUT, model))],
        out_shape=[shape_of(BF, BACK_CUT, model), shape_of(BF, block[0] - BACK_CUT, model)],
        scratch_shapes=[pltpu.VMEM(block, F32), pltpu.VMEM((group, model), BF)],
        compiler_params=params(56),
        cost_estimate=pl.CostEstimate(
            flops=rows * model * hidden // 2, bytes_accessed=8 * rows * model, transcendentals=0
        ),
        name="feed_grads_first",
    )(active, grad_hidden, *grad, *x)


def middle_pull_kernel(
    out_ref, middle_ref, keep_ref, arrived_ref, across_ref, vec_ref, grad_ref, branch_ref, sum_ref
):
    rows = out_ref.shape[1]
    back = keep_ref[0] + arrived_ref[0, :rows, :].astype(F32) + across_ref[0].astype(F32)
    hat, scale = norm_stats(middle_ref[0])
    out = out_ref[0].astype(F32)
    grad = out + norm_pull(back, hat, scale, vec_ref[5:6, :])
    grad_ref[0] = grad
    branch = grad.astype(BF)
    branch_ref[0] = branch

    @pl.when(pl.program_id(0) == 0)
    def _():
        sum_ref[...] = jnp.zeros_like(sum_ref)

    for i, terms in enumerate((branch.astype(F32), back * hat, back, out)):
        sum_ref[i : i + 1, :] += jnp.sum(terms, axis=0, keepdims=True)


def middle_pull(out, middle, keep, arrived, across, vec):
    micro, rows, model = out.shape
    one = per((rows, model))
    return pl.pallas_call(
        middle_pull_kernel,
        grid=(micro,),
        in_specs=[one, one, one, per((2 * rows, model)), one, whole(vec)],
        out_specs=[one, one, full((4, model))],
        out_shape=[
            shape_of(F32, micro, rows, model), shape_of(BF, micro, rows, model),
            shape_of(F32, 4, model),
        ],
        name="middle_pull",
    )(out, middle, keep, arrived, across, vec)


def attend_pull_kernel(
    place_ref, g0, g1, g2, g3, n0, n1, n2, n3, m0, m1, m2, m3, row_ref,
    qkv_ref, log_ref, heads_ref, normed_ref,
    keep_ref, other_ref, send_ref, k0, k1, k2, k3, s0, s1, s2, s3, bias_ref,
    grad_ref, grad_qkv_ref, total_ref, sum_ref, weight_ref, mask_ref,
):
    width = heads_ref.shape[2]
    count = width // HEAD_DIM
    rows = g0.shape[1]
    model = g0.shape[2]
    scale = HEAD_DIM ** (-0.5)
    step = pl.program_id(0)

    @pl.when(step == 0)
    def _():
        assemble(place_ref, (n0, n1, n2, n3), (m0, m1, m2, m3), weight_ref)

    write_mask(row_ref, mask_ref)
    for i, block_ref in enumerate((g0, g1, g2, g3)):
        grad_ref[i * rows : (i + 1) * rows, :] = block_ref[0]
    grad_heads = dot(grad_ref[...], weight_ref[3 * width :, :], 1, 1).astype(BF)
    for head in range(count):
        lanes = [slice(i * width + head * HEAD_DIM, i * width + (head + 1) * HEAD_DIM) for i in range(3)]
        queries, keys, values = [qkv_ref[0, :, part] for part in lanes]
        scores = dot(keys, queries * jnp.asarray(scale, BF), 1, 1) + mask_ref[...]
        probs = jnp.exp(scores - log_ref[0, head : head + 1, :])
        grad = grad_heads[:, lanes[0]]
        product = grad.astype(F32) * heads_ref[0, :, lanes[0]].astype(F32)
        delta = jnp.sum(jnp.transpose(product), axis=0, keepdims=True)
        grad_scores = (probs * (dot(values, grad, 1, 1) - delta)).astype(BF)
        grad_qkv_ref[:, lanes[0]] = jnp.transpose(scale * dot(keys, grad_scores, 0, 0)).astype(BF)
        grad_qkv_ref[:, lanes[1]] = (scale * dot(grad_scores, queries, 1, 0)).astype(BF)
        grad_qkv_ref[:, lanes[2]] = dot(probs.astype(BF), grad, 1, 0).astype(BF)
    write_halves(dot(grad_qkv_ref[...], weight_ref[: 3 * width, :], 1, 0), rows, keep_ref, other_ref, send_ref)
    qkv_part = dot(grad_qkv_ref[...], normed_ref[0], 0, 0)
    out_part = dot(heads_ref[0], grad_ref[...], 0, 0)
    sums = jnp.sum(grad_qkv_ref[...].astype(F32), axis=0, keepdims=True)

    @pl.when(step == 0)
    def _():
        total_ref[: 3 * width, :] = qkv_part
        total_ref[3 * width :, :] = out_part
        sum_ref[...] = jnp.broadcast_to(sums, sum_ref.shape)

    @pl.when(step > 0)
    def _():
        total_ref[: 3 * width, :] += qkv_part
        total_ref[3 * width :, :] += out_part
        sum_ref[...] += sums

    @pl.when(step == pl.num_programs(0) - 1)
    def _():
        z, y, ctx = place_ref[0], place_ref[1], place_ref[2]
        for k, pair in zip(SHIFTS, ((k0, s0), (k1, s1), (k2, s2), (k3, s3))):
            region = lax.rem(z + 4 - k, 4) * width
            for out_ref, half in zip(pair, (y, 1 - y)):
                start = pl.multiple_of(region + BODY * half, HEAD_DIM)
                out_ref[:BODY, :] = total_ref[pl.ds(start, BODY), :].astype(BF)
                start = pl.multiple_of(region + 2 * BODY + HALO * half, HALO)
                out_ref[BODY:, :] = total_ref[pl.ds(start, HALO), :].astype(BF)
        own = head_places((width, model), 0, ctx)
        hot = (lax.broadcasted_iota(jnp.int32, (width, model), 1) == own).astype(F32)
        for i, part in enumerate((0, 2)):
            line = lax.dot_general(
                sum_ref[:, part * width : (part + 1) * width],
                hot,
                (((1,), (0,)), ((), ())),
                preferred_element_type=F32,
                precision=lax.Precision.HIGHEST,
            )
            bias_ref[i : i + 1, :] = line[0:1]


def attend_pull(place, grads, near, side, row, qkv, log_total, heads, normed):
    micro, rows, model = grads[0].shape
    group = 4 * rows
    width = heads.shape[2]
    count = width // HEAD_DIM
    block = (BODY + HALO, model)
    one = per((rows, model))
    return pl.pallas_call(
        attend_pull_kernel,
        grid=(micro,),
        in_specs=[SCALARS] + [one] * 4 + [whole(b) for b in near + side] + [
            per(row.shape[1:]), per((group, 3 * width)), per((8, group)),
            per((group, width)), per((group, model)),
        ],
        out_specs=[one, one, per((2 * rows, model))] + [full(block)] * 8 + [full((2, model))],
        out_shape=[
            shape_of(F32, micro, rows, model), shape_of(BF, micro, rows, model),
            shape_of(BF, micro, 2 * rows, model),
        ] + [shape_of(BF, *block)] * 8 + [shape_of(F32, 2, model)],
        scratch_shapes=[
            pltpu.VMEM((group, model), BF), pltpu.VMEM((group, 3 * width), BF),
            pltpu.VMEM((4 * width, model), F32), pltpu.VMEM((8, 3 * width), F32),
            pltpu.VMEM((4 * width, model), BF), pltpu.VMEM((group, group), F32),
        ],
        compiler_params=params(60),
        cost_estimate=pl.CostEstimate(
            flops=2 * micro * group * model * 10 * width,
            bytes_accessed=12 * micro * group * model,
            transcendentals=micro * count * group * group,
        ),
        name="attend_pull",
    )(place, *grads, *near, *side, row, qkv, log_total, heads, normed)


def input_pull_kernel(
    x_ref, grad_ref, keep_ref, arrived_ref, across_ref, vec_ref, out_ref, sum_ref
):
    rows = x_ref.shape[1]
    back = keep_ref[0] + arrived_ref[0, :rows, :].astype(F32) + across_ref[0].astype(F32)
    hat, scale = norm_stats(x_ref[0].astype(F32))
    out = grad_ref[0] + norm_pull(back, hat, scale, vec_ref[0:1, :])
    out_ref[0] = jnp.transpose(out).astype(BF)

    @pl.when(pl.program_id(0) == 0)
    def _():
        sum_ref[...] = jnp.zeros_like(sum_ref)

    for i, terms in enumerate((back * hat, back)):
        sum_ref[i : i + 1, :] += jnp.sum(terms, axis=0, keepdims=True)


def input_pull(x, grad, keep, arrived, across, vec):
    micro, rows, model = x.shape
    one = per((rows, model))
    out, sums = pl.pallas_call(
        input_pull_kernel,
        grid=(micro,),
        in_specs=[one, one, one, per((2 * rows, model)), one, whole(vec)],
        out_specs=[per((model, rows)), full((2, model))],
        out_shape=[shape_of(BF, micro, model, rows), shape_of(F32, 2, model)],
        name="input_pull",
    )(x, grad, keep, arrived, across, vec)
    return out.transpose(0, 2, 1), sums


def mixed_kernel(middle_ref, keep_ref, arrived_ref, across_ref, vec_ref, out_ref):
    rows = middle_ref.shape[1]
    feed = keep_ref[0] + arrived_ref[0, :rows, :].astype(F32) + across_ref[0].astype(F32)
    out_ref[0] = jnp.transpose(middle_ref[0] + feed + vec_ref[7:8, :]).astype(BF)


def mixed_rows(middle, keep, arrived, across, vec):
    micro, rows, model = middle.shape
    one = per((rows, model))
    return pl.pallas_call(
        mixed_kernel,
        grid=(micro,),
        in_specs=[one, one, per((2 * rows, model)), one, whole(vec)],
        out_specs=per((model, rows)),
        out_shape=shape_of(BF, micro, model, rows),
        name="mixed_rows",
    )(middle, keep, arrived, across, vec).transpose(0, 2, 1)


def row_places(segments, rows):
    ctx = lax.axis_index("ctx")
    ranks = [ctx ^ j for j in BLOCKS]
    starts = segments[:, 0].reshape(-1, 4, rows).transpose(1, 0, 2)
    starts = jnp.concatenate([pick(starts, r) for r in ranks], axis=1)
    places = jnp.concatenate([r * rows + jnp.arange(rows, dtype=jnp.int32) for r in ranks])
    places = jnp.broadcast_to(places[None], starts.shape)
    return jnp.stack([starts, places] + [places] * 6, axis=1)


def own_up_bias(lines, order, width):
    table = lines[16:].reshape(order.shape[0], 4, width).transpose(1, 0, 2)
    return reorder(pick(table, lax.axis_index("ctx")), order).reshape(1, -1)


def vector_parts(first_sums, bias_sums, sums, up_sum, order, width):
    up_rows = reorder_back(up_sum.reshape(order.shape[0], width), order)
    mine = (jnp.arange(4) == lax.axis_index("ctx")).astype(F32)
    table = jnp.concatenate([first_sums, bias_sums, sums], axis=0)
    up_part = (up_rows[:, None, :] * mine[None, :, None]).reshape(-1)
    return jnp.concatenate([table.reshape(-1), up_part])


def flat(values):
    return values.reshape(-1, values.shape[-1])


def halo_pairs(back):
    pairs = []
    for p in range(8):
        for c in range(4):
            to = (c - 1) % 4 if (p % 2 == 1) != back else (c + 1) % 4
            pairs.append((p * 4 + c, p * 4 + to))
    return pairs


def aligned_block(w_attn, vectors, odd, ctx):
    turned = row_major(w_attn.T)
    width, model = turned.shape
    table = ctx_table(vectors, ctx).astype(BF).reshape(3, model // 2)
    edge = jnp.where(odd, turned[:HALO], turned[width - HALO :])
    halo = lax.ppermute(edge, BOTH, halo_pairs(False))
    none = jnp.zeros_like(halo)
    wide = jnp.concatenate(
        [jnp.where(odd, none, halo), turned, jnp.where(odd, halo, none)], axis=0
    )
    shift = HALO * odd.astype(jnp.int32)
    body = lax.dynamic_slice_in_dim(wide, HALO - 8 * ctx + shift, BODY, axis=0)
    extra = lax.dynamic_slice_in_dim(wide, width + shift, HALO, axis=0)
    extra = jnp.where(ctx == 3, extra, jnp.zeros_like(extra))
    lines = jnp.pad(table, ((0, 13), (0, model // 2)))
    return jnp.concatenate([body, extra, lines], axis=0)


def aligned_owned(own, odd, ctx, width):
    last = ctx == 3
    body, extra = own[:BODY], own[BODY:]
    tail = jnp.where(last, extra, body[BODY - HALO :])
    halo = lax.ppermute(jnp.where(odd, tail, body[:HALO]), BOTH, halo_pairs(True))
    halo = jnp.where(last & jnp.logical_not(odd), extra, halo)
    wide = jnp.where(
        odd, jnp.concatenate([halo, body], axis=0), jnp.concatenate([body, halo], axis=0)
    )
    return lax.dynamic_slice_in_dim(wide, 8 * ctx, width, axis=0)


def vector_rows(part, ctx):
    table = part.reshape(8, 4, -1).transpose(1, 0, 2)
    mine = jnp.stack([pick(table, ctx ^ j) for j in (0, 1)])
    far = jnp.stack([pick(table, ctx ^ j) for j in (2, 3)])
    mine = mine + lax.ppermute(far, "ctx", CHIP_PAIRS)
    return mine[0] + lax.ppermute(mine[1], "ctx", CORE_PAIRS)


def vector_sides(mine, y):
    sides = mine.reshape(4, 2, -1).transpose(1, 0, 2)
    return pick(sides, y) + lax.ppermute(pick(sides, 1 - y), "dp", SIDE_PAIRS)


def vector_owned(mine, z):
    total = pick(mine, z)
    for k in (1, 2, 3):
        total = total + to_shift(pick(mine, (z - k) % 4)[None], k, True)[0]
    return total


def both(keep, arrived):
    return keep.astype(F32) + arrived.astype(F32)


def aligned(tokens, cotangent, w_attn, w_up, w_down, vectors, segments):
    rows = tokens.shape[1]
    width = w_attn.shape[1]
    ctx, dp = lax.axis_index("ctx"), lax.axis_index("dp")
    z, y = dp // 2, dp % 2
    odd = y == 1
    place = jnp.stack([z, y, ctx]).astype(jnp.int32)
    order = jnp.stack(dp_order(z, y))
    tokens, cotangent = row_major(tokens), row_major(cotangent)
    row_info = row_places(segments, rows)
    feed = jnp.concatenate([w_down, w_up.T], axis=0)

    n0 = aligned_block(w_attn, vectors, odd, ctx)
    n0, t0, place, row_info, b0 = hold([n0, tokens, place, row_info, feed])
    n1, n3, s0, t1, c0 = (
        to_shift(n0, 1), to_shift(n0, 3), to_side(n0), to_chip(t0), to_side(b0[:CUT])
    )
    n0, n1, n3, s0, t0, t1, g0, b0, c0 = hold([n0, n1, n3, s0, t0, t1, cotangent, b0, c0])
    n2, s1, s3, g1 = to_shift(n0, 2), to_side(n1), to_side(n3), to_chip(g0)
    n0, n1, n2, n3, s0, s1, s3, t0, t1, g0, g1, b0 = hold(
        [n0, n1, n2, n3, s0, s1, s3, t0, t1, g0, g1, b0]
    )
    s2, b1, t2, t3 = to_side(n2), to_shift(b0, 1), to_core(t0), to_core(t1)
    n0, n1, n2, n3, s0, s1, s2, s3, t0, t1, t2, t3, g0, g1, b0, b1 = hold(
        [n0, n1, n2, n3, s0, s1, s2, s3, t0, t1, t2, t3, g0, g1, b0, b1]
    )
    b3, b2, c1, d0 = (
        to_shift(b0, 3), to_shift(b0[: THIRDS[0]], 2), to_side(b1), to_side(b0[CUT:])
    )
    normed_one, qkv, log_total, heads, lines, rest, keep, other, away = attend(
        place, [t0, t1, t2, t3], [n0, n1, n3, n2], [s0, s1, s3, s2], row_info
    )
    away, keep, other, b0, b1, b2, b3, c1, d0, g0, g1 = hold(
        [away, keep, other, b0, b1, b2, b3, c1, d0, g0, g1]
    )
    arrived = to_core(away)
    away, arrived, keep, b0, b2, b3, g0, g1 = hold(
        [half_sum(other, arrived), arrived, keep, b0, b2, b3, g0, g1]
    )
    across, d2, c3 = to_chip(away), to_shift(b0[THIRDS[0] : THIRDS[1]], 2), to_side(b3)
    g2, g3 = to_core(g0), to_core(g1)
    across, arrived, keep, b0, d2, c3, b2, g2, g3 = hold(
        [across, arrived, keep, b0, d2, c3, b2, g2, g3]
    )
    middle, h0 = middle_rows(tokens, keep, arrived, across, lines)
    h0, middle, b0, d2, b2 = hold([h0, middle, b0, d2, b2])
    h1, e2, f2, c2 = to_chip(h0), to_shift(b0[THIRDS[1] :], 2), to_side(d2), to_side(b2)
    up_bias = own_up_bias(rest, order, width)
    h0, h1, e2, f2, c2, up_bias = hold([h0, h1, e2, f2, c2, up_bias])
    h2, h3, a2 = to_core(h0), to_core(h1), to_side(e2)
    blocks = [[c2, f2, a2], [b2, d2, e2], [b0], [c0, d0], [b1], [c1], [b3], [c3]]
    pull = feed_pull([g0, g1, g2, g3], blocks)
    h0, h1, h2, h3, pull = hold([h0, h1, h2, h3, pull], a2)
    active, grad_hidden, keep, other, away, up_sum = feed_forward(
        [h0, h1, h2, h3], pull, blocks, up_bias
    )
    x_all, grad_all = [h0, h1, h2, h3], [g0, g1, g2, g3]

    arrived = to_core(away)
    q2, v2 = feed_grads_first(flat(active), flat(grad_hidden), grad_all, x_all)
    away, arrived, keep, active, q2, v2 = hold(
        [half_sum(other, arrived), arrived, keep, active, q2, v2]
    )
    across, q2, v2 = to_chip(away), to_side(q2), to_side(v2)
    p2, p0, q0, p1, q1, p3, q3 = feed_grads(flat(active), flat(grad_hidden), grad_all, x_all)
    across, arrived, keep, p2, q2, v2 = hold([across, arrived, keep, p2, q2, v2])
    grad_middle, h0, sums = middle_pull(cotangent, middle, keep, arrived, across, lines)
    h0, q2, p2, v2, q3, grad_middle, active = hold(
        [h0, both(p2[:BACK_CUT], q2).astype(BF), p2, v2, q3, grad_middle, active]
    )
    h1, h2, r2, q3 = to_chip(h0), to_core(h0), to_shift(q2, 2, True), to_side(q3)
    p2 = both(p2[BACK_CUT:], v2).astype(BF)
    feed_keep, feed_other, feed_away = feed_out(active, blocks)
    h0, h1, h2, r2, q3, p2, feed_away = hold([h0, h1, h2, r2, q3, p2, feed_away])
    h3, feed_arrived = to_core(h1), to_core(feed_away)
    h0, h1, h2, h3, p2, p3, q1, q0, feed_arrived = hold(
        [h0, h1, h2, h3, p2, both(p3, q3).astype(BF), q1, q0, feed_arrived]
    )
    t2, r3 = to_shift(p2, 2, True), to_shift(p3, 3, True)
    q1, q0 = to_side(q1), to_side(q0)
    keep, other, away, *parts, bias_sums = attend_pull(
        place, [h0, h1, h2, h3], [n0, n1, n3, n2], [s0, s1, s3, s2], row_info,
        qkv, log_total, heads, normed_one,
    )
    away, t2, r3, q1, q0, p0, p1, *parts = hold([away, t2, r3, q1, q0, p0, p1] + parts)
    k0, k1, k3, k2, l0, l1, l3, l2 = parts
    arrived = to_core(away)
    away, arrived, keep, p1, l1, l2, l3 = hold(
        [half_sum(other, arrived), arrived, keep, both(p1, q1).astype(BF), l1, l2, l3]
    )
    r1, across, l2, l1 = to_shift(p1, 1, True), to_chip(away), to_side(l2), to_side(l1)
    across, arrived, keep, r1, k1, k2, l0, l3, feed_away = hold(
        [
            across, arrived, keep, r1, both(k1, l1).astype(BF), both(k2, l2).astype(BF),
            l0, l3, half_sum(feed_other, feed_arrived),
        ]
    )
    k2, k1, l3, l0, feed_across = (
        to_shift(k2, 2, True), to_shift(k1, 1, True), to_side(l3), to_side(l0),
        to_chip(feed_away),
    )
    input_grad, first_sums = input_pull(tokens, grad_middle, keep, arrived, across, lines)
    part = vector_parts(first_sums, bias_sums, sums, up_sum, order, width)
    k1, k2, k3, l0, part, feed_across, input_grad = hold(
        [k1, k2, both(k3, l3).astype(BF), l0, part, feed_across, input_grad]
    )
    k3, part = to_shift(k3, 3, True), vector_rows(part, ctx)
    k1, k2, k3, part = hold([k1, k2, k3, part])
    own = both(k0, l0) + k1.astype(F32) + k2.astype(F32) + k3.astype(F32)
    attn_owned = aligned_owned(own, odd, ctx, width).T
    part = vector_sides(part, y)
    mixed = mixed_rows(middle, feed_keep, feed_arrived, feed_across, lines)
    terms = [p0, q0, r1, jnp.concatenate([r2, t2], axis=0), r3]
    down_owned = sum(t[:width].astype(F32) for t in terms)
    up_owned = sum(t[width:].astype(F32) for t in terms).T
    part, mixed, down_owned, up_owned = hold([part, mixed, down_owned, up_owned])
    return mixed, input_grad, attn_owned, up_owned, down_owned, vector_owned(part, z)


def plain(tokens, cotangent, w_attn, w_up, w_down, vectors, segments):
    micro, rows, model = tokens.shape
    width = w_attn.shape[1]
    ctx = lax.axis_index("ctx")
    last = ctx == lax.axis_size("ctx") - 1
    place = jnp.stack([jnp.zeros((), ctx.dtype), jnp.zeros((), ctx.dtype), ctx])
    order = jnp.arange(lax.axis_size("dp"))
    table = lax.all_gather(w_attn.T, BOTH, axis=0, tiled=True)
    lines = lax.all_gather(vectors, BOTH, axis=0, tiled=True).reshape(24, model // 2)
    lines = jnp.pad(lines, ((0, 0), (0, model // 2)))
    near, side = [], []
    for region in (-k % 4 for k in SHIFTS):
        part = head_rows(table[region * model : (region + 1) * model], ctx, last)
        for blocks, half in ((near, 0), (side, 1)):
            line = 3 * (2 * region + half)
            blocks.append(
                jnp.concatenate(
                    [
                        part[BODY * half : BODY * (half + 1)],
                        part[2 * BODY + HALO * half : 2 * BODY + HALO * (half + 1)],
                        jnp.pad(lines[line : line + 3], ((0, 13), (0, 0))),
                    ],
                    axis=0,
                )
            )
    up = lax.all_gather(w_up.T, "dp", axis=0, tiled=True)
    down = lax.all_gather(w_down, "dp", axis=0, tiled=True)
    each = up.shape[0] // 8
    blocks = [
        jnp.concatenate([w[i * each : (i + 1) * each] for w in (down, up)], axis=0)
        for i in range(8)
    ]
    blocks = [[b] for b in blocks]
    row_info = row_places(segments, rows)

    normed_one, qkv, log_total, heads, lines, rest, *halves = attend(
        place, row_gather(tokens), near, side, row_info
    )
    middle, normed_two = middle_rows(tokens, *row_scatter(*halves), lines)
    x_all, grad_all = row_gather(normed_two), row_gather(cotangent)
    active, grad_hidden, *halves, up_sum = feed_forward(
        x_all, feed_pull(grad_all, blocks), blocks, own_up_bias(rest, order, width)
    )
    mixed = mixed_rows(middle, *row_scatter(*feed_out(active, blocks)), lines)
    grad_middle, branch, sums = middle_pull(cotangent, middle, *row_scatter(*halves), lines)
    arrays = flat(active), flat(grad_hidden), grad_all, x_all
    parts = [jnp.concatenate(feed_grads_first(*arrays), axis=0)] + list(feed_grads(*arrays))
    down_owned, up_owned = [
        lax.psum_scatter(
            jnp.concatenate([p[i * each : (i + 1) * each] for p in parts], axis=0),
            "dp", scatter_dimension=0, tiled=True,
        ).astype(F32)
        for i in range(2)
    ]
    *halves, k0, k1, k2, k3, s0, s1, s2, s3, bias_sums = attend_pull(
        place, row_gather(branch), near, side, row_info, qkv, log_total, heads, normed_one
    )
    input_grad, first_sums = input_pull(tokens, grad_middle, *row_scatter(*halves), lines)
    parts = []
    for region in range(4):
        at = SHIFTS.index(-region % 4)
        first, second = (k0, k1, k2, k3)[at], (s0, s1, s2, s3)[at]
        part = [first[:BODY], second[:BODY], first[BODY:], second[BODY:]]
        parts.append(head_rows_back(jnp.concatenate(part, axis=0), ctx, last))
    attn_owned = lax.psum_scatter(
        jnp.concatenate(parts, axis=0), BOTH, scatter_dimension=0, tiled=True
    ).astype(F32)
    part = vector_parts(first_sums, bias_sums, sums, up_sum, order, width)
    vector_grad = lax.psum_scatter(part, BOTH, scatter_dimension=0, tiled=True)
    return (mixed, input_grad, attn_owned.T, up_owned.T, down_owned, vector_grad)


def shards(*arrays):
    fits = lax.axis_size("dp") == 8 and lax.axis_size("ctx") == 4
    return (aligned if fits and arrays[2].shape == (1088, 136) else plain)(*arrays)


def solution(mesh):
    return jax.shard_map(
        shards,
        mesh=mesh,
        in_specs=(
            P(None, BOTH, None),
            P(None, BOTH, None),
            P(None, BOTH),
            P(None, BOTH),
            P(BOTH, None),
            P(BOTH),
            P(None, "dp", None),
        ),
        out_specs=(
            P(None, BOTH, None),
            P(None, BOTH, None),
            P(None, BOTH),
            P(None, BOTH),
            P(BOTH, None),
            P(BOTH),
        ),
        check_vma=False,
    )
```

```python
from functools import partial

import jax
import jax.numpy as jnp
from jax import lax
from jax.experimental import pallas as pl
from jax.experimental.layout import Layout, with_layout_constraint
from jax.experimental.pallas import tpu as pltpu
from jax.sharding import PartitionSpec as P

HEAD_DIM = 64
HALO = 32
BODY = 128
NEG_FILL = -1e30
EPSILON = 1e-05
BF = jnp.bfloat16
F32 = jnp.float32
BOTH = ("dp", "ctx")
CORE_PAIRS = [(0, 1), (1, 0), (2, 3), (3, 2)]
CHIP_PAIRS = [(0, 2), (2, 0), (1, 3), (3, 1)]
BLOCKS = (0, 2, 1, 3)
SHIFTS = (0, 1, 3, 2)
ORDER = ((2, 1), (2, 0), (0, 0), (0, 1), (1, 0), (1, 1), (3, 0), (3, 1))
THIRDS = (64, 160)
CUT = 144
BACK_CUT = 144
SIDE_PAIRS = [(p, p ^ 1) for p in range(8)]


def shift_pairs(step):
    return [(z * 2 + y, ((z + step) % 4) * 2 + y) for z in range(4) for y in range(2)]


def dot(left, right, left_dim, right_dim):
    return lax.dot_general(
        left, right, (((left_dim,), (right_dim,)), ((), ())), preferred_element_type=F32
    )


def norm_stats(values):
    centred = values - jnp.mean(values, axis=-1, keepdims=True)
    scale = lax.rsqrt(jnp.mean(centred * centred, axis=-1, keepdims=True) + EPSILON)
    return centred * scale, scale


def norm_pull(grad, hat, scale, gain):
    grad_hat = grad * gain
    along = jnp.mean(grad_hat * hat, axis=-1, keepdims=True)
    return scale * (grad_hat - jnp.mean(grad_hat, axis=-1, keepdims=True) - hat * along)


def row_major(value):
    return with_layout_constraint(value, Layout(tuple(range(value.ndim))))


def send(value, axes, pairs):
    rows = value.shape[-2]
    if rows % 16:
        return lax.ppermute(value, axes, pairs)
    cut = value.reshape(value.shape[:-2] + (rows // 16, 16, value.shape[-1]))
    return lax.ppermute(cut, axes, pairs).reshape(value.shape)


def hold(values, *others):
    return lax.optimization_barrier(tuple(values) + tuple(others))[: len(values)]


def to_core(value):
    return send(value, "ctx", CORE_PAIRS)


def to_chip(value):
    return send(value, "ctx", CHIP_PAIRS)


def to_side(value):
    return send(value, "dp", SIDE_PAIRS)


def to_shift(value, step, back=False):
    pairs = shift_pairs(step)
    return send(value, "dp", [(b, a) for a, b in pairs] if back else pairs)


def row_gather(mine):
    across = to_chip(mine)
    return [mine, across, to_core(mine), to_core(across)]


def half_sum(other, arrived):
    rows = other.shape[1]
    return (other.astype(F32) + arrived[:, rows:].astype(F32)).astype(BF)


def row_scatter(keep, other, away):
    arrived = to_core(away)
    return keep, arrived, to_chip(half_sum(other, arrived))


def dp_order(z, y):
    return [((z - k) % 4) * 2 + (y ^ s) for k, s in ORDER]


def pick(stacked, index):
    return lax.dynamic_index_in_dim(stacked, index, axis=0, keepdims=False)


def reorder(table, order):
    hot = (order[:, None] == jnp.arange(table.shape[0])[None, :]).astype(F32)
    return jnp.sum(hot[:, :, None] * table[None], axis=1)


def reorder_back(table, order):
    hot = (order[:, None] == jnp.arange(table.shape[0])[None, :]).astype(F32)
    return jnp.sum(hot[:, :, None] * table[:, None, :], axis=0)


def ctx_table(mine, ctx):
    across = lax.ppermute(mine[None], "ctx", CHIP_PAIRS)
    pair = jnp.concatenate([mine[None], across], axis=0)
    table = jnp.concatenate([pair, lax.ppermute(pair, "ctx", CORE_PAIRS)], axis=0)
    return reorder_back(table.astype(F32), jnp.stack([ctx ^ j for j in BLOCKS]))


def head_rows(table, ctx, last):
    middle = 8 * HEAD_DIM
    first = lax.dynamic_slice_in_dim(table, 128 * ctx, 128, axis=0)
    second = lax.dynamic_slice_in_dim(table, middle + HEAD_DIM + 128 * ctx, 128, axis=0)
    mid = table[middle : middle + HEAD_DIM]
    return jnp.concatenate([first, second, jnp.where(last, mid, jnp.zeros_like(mid))], axis=0)


def head_rows_back(mine, ctx, last):
    middle = 8 * HEAD_DIM
    table = jnp.zeros((2 * middle + HEAD_DIM,) + mine.shape[1:], mine.dtype)
    table = lax.dynamic_update_slice_in_dim(table, mine[:128], 128 * ctx, axis=0)
    table = lax.dynamic_update_slice_in_dim(
        table, mine[128:256], middle + HEAD_DIM + 128 * ctx, axis=0
    )
    mid = jnp.where(last, mine[256:], jnp.zeros_like(mine[256:]))
    return lax.dynamic_update_slice_in_dim(table, mid, middle, axis=0)


def gelu_parts(hidden):
    factor = 0.7978845608028654
    square = hidden * hidden
    bent = jnp.tanh(factor * hidden * (1.0 + 0.044715 * square))
    active = 0.5 * hidden * (1.0 + bent)
    slope = 0.5 * (1.0 + bent) + 0.5 * hidden * (1.0 - bent * bent) * factor * (
        1.0 + 3 * 0.044715 * square
    )
    return active, slope


def full(shape):
    return pl.BlockSpec(shape, lambda *_: (0,) * len(shape))


def per(shape, step=1):
    return pl.BlockSpec((1,) + shape, lambda i: (i // step,) + (0,) * len(shape))


def params(mib):
    return pltpu.CompilerParams(vmem_limit_bytes=mib * 1024 * 1024)


def whole(array):
    return full(array.shape)


SCALARS = pl.BlockSpec(memory_space=pltpu.SMEM)


def shape_of(dtype, *dims):
    return jax.ShapeDtypeStruct(dims, dtype)


def head_places(shape, axis, ctx):
    own = lax.broadcasted_iota(jnp.int32, shape, axis)
    middle = 8 * HEAD_DIM
    shift = jnp.where(own < BODY, BODY * ctx, middle + HEAD_DIM - BODY + BODY * ctx)
    shift = jnp.where(own < 2 * BODY, shift, middle - 2 * BODY)
    return jnp.where((own < 2 * BODY) | (ctx == 3), own + shift, -1)


def write_halves(values, rows, keep_ref, other_ref, send_ref):
    keep_ref[0] = values[:rows]
    other_ref[0] = values[rows : 2 * rows].astype(BF)
    send_ref[0] = values[2 * rows :].astype(BF)


def assemble(place_ref, near, side, weight_ref):
    width = weight_ref.shape[0] // 4
    z, y = place_ref[0], place_ref[1]
    for k, pair in zip(SHIFTS, zip(near, side)):
        region = lax.rem(z + 4 - k, 4) * width
        for block_ref, half in zip(pair, (y, 1 - y)):
            to = pl.multiple_of(region + BODY * half, HEAD_DIM)
            weight_ref[pl.ds(to, BODY), :] = block_ref[:BODY, :]
            to = pl.multiple_of(region + 2 * BODY + HALO * half, HALO)
            weight_ref[pl.ds(to, HALO), :] = block_ref[BODY : BODY + HALO, :]


def write_mask(row_ref, mask_ref):
    row = row_ref[0].astype(F32)
    first, own = row[0:1], row[1:2]
    square = (128, row.shape[1])
    first_col = jnp.transpose(jnp.broadcast_to(first, square))[:, :1]
    own_col = jnp.transpose(jnp.broadcast_to(own, square))[:, :1]
    allowed = (own_col <= own) & (first_col == first)
    mask_ref[...] = jnp.where(allowed, 0.0, NEG_FILL)


def attend_kernel(
    place_ref, x0, x1, x2, x3, n0, n1, n2, n3, s0, s1, s2, s3, row_ref,
    normed_ref, qkv_ref, log_ref, heads_ref, vec_ref, line_ref,
    keep_ref, other_ref, send_ref, weight_ref, mask_ref, bias_ref,
):
    width = heads_ref.shape[2]
    count = width // HEAD_DIM
    model = vec_ref.shape[1]
    part = model // 2
    rows = x0.shape[1]

    @pl.when(pl.program_id(0) == 0)
    def _():
        z, y, ctx = place_ref[0], place_ref[1], place_ref[2]
        assemble(place_ref, (n0, n1, n2, n3), (s0, s1, s2, s3), weight_ref)
        for k, pair in zip(SHIFTS, ((n0, s0), (n1, s1), (n2, s2), (n3, s3))):
            owner = lax.rem(z + 4 - k, 4)
            for block_ref, half in zip(pair, (y, 1 - y)):
                lines = block_ref[BODY + HALO :, :].astype(F32)
                for i in range(3):
                    line_ref[pl.ds(3 * (2 * owner + half) + i, 1), :] = lines[i : i + 1, :part]
        for i in range(8):
            vec_ref[i : i + 1, :part] = line_ref[2 * i : 2 * i + 1, :]
            vec_ref[i : i + 1, part:] = line_ref[2 * i + 1 : 2 * i + 2, :]
        own = head_places((model, width), 1, ctx)
        hot = (lax.broadcasted_iota(jnp.int32, (model, width), 0) == own).astype(F32).astype(BF)
        own_vec = dot(vec_ref[...].astype(BF), hot, 1, 0)
        bias_ref[:, :width] = own_vec[2:3]
        bias_ref[:, width : 2 * width] = jnp.zeros((1, width), F32)
        bias_ref[:, 2 * width :] = own_vec[3:4]

    gain, bias = vec_ref[0:1, :], vec_ref[1:2, :]
    for i, x_ref in enumerate((x0, x1, x2, x3)):
        hat, _ = norm_stats(x_ref[0].astype(F32))
        normed_ref[0, i * rows : (i + 1) * rows, :] = (hat * gain + bias).astype(BF)
    normed = normed_ref[0]
    qkv_ref[0] = (dot(normed, weight_ref[: 3 * width, :], 1, 1) + bias_ref[...]).astype(BF)
    write_mask(row_ref, mask_ref)
    for head in range(count):
        lanes = [slice(i * width + head * HEAD_DIM, i * width + (head + 1) * HEAD_DIM) for i in range(3)]
        queries, keys, values = [qkv_ref[0, :, part] for part in lanes]
        queries = queries * jnp.asarray(HEAD_DIM ** (-0.5), BF)
        scores = dot(keys, queries, 1, 1) + mask_ref[...]
        top = jnp.max(scores, axis=0, keepdims=True)
        weights = jnp.exp(scores - top)
        total = jnp.sum(weights, axis=0, keepdims=True)
        probs = (weights * (1.0 / total)).astype(BF)
        log_ref[0, head : head + 1, :] = top + jnp.log(total)
        heads_ref[0, :, lanes[0]] = jnp.transpose(dot(values, probs, 0, 0)).astype(BF)
    branch = dot(heads_ref[0], weight_ref[3 * width :, :], 1, 0)
    write_halves(branch, rows, keep_ref, other_ref, send_ref)


def attend(place, blocks, near, side, row):
    micro, rows, model = blocks[0].shape
    group = 4 * rows
    width = 2 * (BODY + HALO)
    count = width // HEAD_DIM
    return pl.pallas_call(
        attend_kernel,
        grid=(micro,),
        in_specs=[SCALARS] + [per((rows, model))] * 4
        + [whole(b) for b in near + side] + [per(row.shape[1:])],
        out_specs=[
            per((group, model)), per((group, 3 * width)), per((8, group)),
            per((group, width)), full((8, model)), full((24, model // 2)),
            per((rows, model)), per((rows, model)), per((2 * rows, model)),
        ],
        out_shape=[
            shape_of(BF, micro, group, model), shape_of(BF, micro, group, 3 * width),
            shape_of(F32, micro, 8, group), shape_of(BF, micro, group, width),
            shape_of(F32, 8, model),
            shape_of(F32, 24, model // 2), shape_of(F32, micro, rows, model),
            shape_of(BF, micro, rows, model), shape_of(BF, micro, 2 * rows, model),
        ],
        scratch_shapes=[
            pltpu.VMEM((4 * width, model), BF), pltpu.VMEM((group, group), F32),
            pltpu.VMEM((1, 3 * width), F32),
        ],
        compiler_params=params(56),
        cost_estimate=pl.CostEstimate(
            flops=2 * micro * group * model * 4 * width,
            bytes_accessed=12 * micro * group * model,
            transcendentals=micro * count * group * group,
        ),
        name="attend",
    )(place, *blocks, *near, *side, row)


def middle_kernel(x_ref, keep_ref, arrived_ref, across_ref, vec_ref, middle_ref, normed_ref):
    rows = x_ref.shape[1]
    branch = keep_ref[0] + arrived_ref[0, :rows, :].astype(F32) + across_ref[0].astype(F32)
    middle = x_ref[0].astype(F32) + branch + vec_ref[4:5, :]
    middle_ref[0] = middle
    hat, _ = norm_stats(middle)
    normed_ref[0] = (hat * vec_ref[5:6, :] + vec_ref[6:7, :]).astype(BF)


def middle_rows(x, keep, arrived, across, vec):
    micro, rows, model = x.shape
    one = per((rows, model))
    return pl.pallas_call(
        middle_kernel,
        grid=(micro,),
        in_specs=[one, one, per((2 * rows, model)), one, whole(vec)],
        out_specs=[one, one],
        out_shape=[shape_of(F32, micro, rows, model), shape_of(BF, micro, rows, model)],
        name="middle_rows",
    )(x, keep, arrived, across, vec)


def stack_parts(parts, refs, low, high, to_ref):
    for (block, start), part_ref in zip(parts, refs):
        first, last = max(start, low), min(start + part_ref.shape[0], high)
        to = block * (high - low) - low
        to_ref[to + first : to + last, :] = part_ref[first - start : last - start, :]


def parts_between(blocks, low, high):
    parts, arrays = [], []
    for block, pieces in enumerate(blocks):
        start = 0
        for piece in pieces:
            if start < high and start + piece.shape[0] > low:
                parts.append((block, start))
                arrays.append(piece)
            start += piece.shape[0]
    return parts, arrays


def pull_kernel(parts, g0, g1, g2, g3, *rest):
    *part_refs, pull_ref, grad_ref, down_ref = rest
    rows = g0.shape[1]
    each = down_ref.shape[0] // 8

    @pl.when(pl.program_id(0) == 0)
    def _():
        stack_parts(parts, part_refs, 0, each, down_ref)

    for i, block_ref in enumerate((g0, g1, g2, g3)):
        grad_ref[i * rows : (i + 1) * rows, :] = block_ref[0]
    pull_ref[0] = dot(grad_ref[...], down_ref[...], 1, 1).astype(BF)


def feed_pull(grads, blocks):
    micro, rows, model = grads[0].shape
    group = 4 * rows
    each = sum(p.shape[0] for p in blocks[0]) // 2
    hidden = 8 * each
    parts, arrays = parts_between(blocks, 0, each)
    return pl.pallas_call(
        partial(pull_kernel, parts),
        grid=(micro,),
        in_specs=[per((rows, model))] * 4 + [whole(b) for b in arrays],
        out_specs=per((group, hidden)),
        out_shape=shape_of(BF, micro, group, hidden),
        scratch_shapes=[pltpu.VMEM((group, model), BF), pltpu.VMEM((hidden, model), BF)],
        compiler_params=params(56),
        cost_estimate=pl.CostEstimate(
            flops=2 * micro * group * model * hidden,
            bytes_accessed=8 * micro * group * model,
            transcendentals=0,
        ),
        name="feed_pull",
    )(*grads, *arrays)


def feed_kernel(parts, x0, x1, x2, x3, pull_ref, bias_ref, *rest):
    *part_refs, active_ref, grad_hidden_ref, keep_ref, other_ref, send_ref, sum_ref, x_ref, up_ref = rest
    rows = x0.shape[1]
    each = up_ref.shape[0] // 8

    @pl.when(pl.program_id(0) == 0)
    def _():
        stack_parts(parts, part_refs, each, 2 * each, up_ref)
        sum_ref[...] = jnp.zeros_like(sum_ref)

    for i, block_ref in enumerate((x0, x1, x2, x3)):
        x_ref[i * rows : (i + 1) * rows, :] = block_ref[0]
    active, slope = gelu_parts(dot(x_ref[...], up_ref[...], 1, 1) + bias_ref[...])
    active_ref[0] = active.astype(BF)
    grad_hidden = (pull_ref[0].astype(F32) * slope).astype(BF)
    grad_hidden_ref[0] = grad_hidden
    sum_ref[...] += jnp.sum(grad_hidden.astype(F32), axis=0, keepdims=True)
    write_halves(dot(grad_hidden, up_ref[...], 1, 0), rows, keep_ref, other_ref, send_ref)


def halves_of(micro, rows, model):
    specs = [per((rows, model)), per((rows, model)), per((2 * rows, model))]
    return specs, [
        shape_of(F32, micro, rows, model), shape_of(BF, micro, rows, model),
        shape_of(BF, micro, 2 * rows, model),
    ]


def feed_forward(x, pull, blocks, bias):
    micro, rows, model = x[0].shape
    group = 4 * rows
    hidden = pull.shape[2]
    specs, shapes = halves_of(micro, rows, model)
    parts, arrays = parts_between(blocks, hidden // 8, hidden // 4)
    return pl.pallas_call(
        partial(feed_kernel, parts),
        grid=(micro,),
        in_specs=[per((rows, model))] * 4 + [per((group, hidden)), whole(bias)]
        + [whole(b) for b in arrays],
        out_specs=[per((group, hidden))] * 2 + specs + [full((1, hidden))],
        out_shape=[shape_of(BF, micro, group, hidden)] * 2 + shapes + [shape_of(F32, 1, hidden)],
        scratch_shapes=[pltpu.VMEM((group, model), BF), pltpu.VMEM((hidden, model), BF)],
        compiler_params=params(56),
        cost_estimate=pl.CostEstimate(
            flops=4 * micro * group * model * hidden,
            bytes_accessed=12 * micro * group * model,
            transcendentals=micro * group * hidden,
        ),
        name="feed_forward",
    )(*x, pull, bias, *arrays)


def feed_out_kernel(parts, active_ref, *rest):
    *part_refs, keep_ref, other_ref, send_ref, down_ref = rest

    @pl.when(pl.program_id(0) == 0)
    def _():
        stack_parts(parts, part_refs, 0, down_ref.shape[0] // 8, down_ref)

    write_halves(
        dot(active_ref[0], down_ref[...], 1, 0), keep_ref.shape[1], keep_ref, other_ref, send_ref
    )


def feed_out(active, blocks):
    micro, group, hidden = active.shape
    parts, arrays = parts_between(blocks, 0, hidden // 8)
    model = arrays[0].shape[1]
    specs, shapes = halves_of(micro, group // 4, model)
    return pl.pallas_call(
        partial(feed_out_kernel, parts),
        grid=(micro,),
        in_specs=[per((group, hidden))] + [whole(b) for b in arrays],
        out_specs=specs,
        out_shape=shapes,
        scratch_shapes=[pltpu.VMEM((hidden, model), BF)],
        compiler_params=params(56),
        cost_estimate=pl.CostEstimate(
            flops=2 * micro * group * model * hidden,
            bytes_accessed=8 * micro * group * model,
            transcendentals=0,
        ),
        name="feed_out",
    )(active, *arrays)


def rows_from(refs, to_ref):
    micro, rows, _ = refs[0].shape
    for m in range(micro):
        for i, block_ref in enumerate(refs):
            at = (4 * m + i) * rows
            to_ref[at : at + rows, :] = block_ref[m]


def feed_grads_kernel(active_ref, grad_hidden_ref, g0, g1, g2, g3, x0, x1, x2, x3, *rest):
    *outs, total_ref, right_ref = rest
    each = outs[0].shape[0] // 2
    step = pl.program_id(0)
    hidden = active_ref.shape[1]
    cut = hidden // 256 * 128
    for left_ref, refs, part in (
        (active_ref, (g0, g1, g2, g3), 0), (grad_hidden_ref, (x0, x1, x2, x3), 1)
    ):

        @pl.when(step == part)
        def _():
            rows_from(refs, right_ref)
            total_ref[:cut, :] = dot(left_ref[:, :cut], right_ref[...], 0, 0)
            total_ref[cut:, :] = dot(left_ref[:, cut:], right_ref[...], 0, 0)
            for i, out_ref in enumerate(outs):
                rows = total_ref[(i + 1) * each : (i + 2) * each, :].astype(BF)
                out_ref[part * each : (part + 1) * each, :] = rows


def feed_grads(active, grad_hidden, grad, x):
    rows, hidden = active.shape
    model = grad[0].shape[2]
    block = (hidden // 4, model)
    arrays = [active, grad_hidden, *grad, *x]
    return pl.pallas_call(
        feed_grads_kernel,
        grid=(2,),
        in_specs=[whole(a) for a in arrays],
        out_specs=[full(block)] * 7,
        out_shape=[shape_of(BF, *block)] * 7,
        scratch_shapes=[pltpu.VMEM((hidden, model), F32), pltpu.VMEM((rows, model), BF)],
        compiler_params=params(56),
        cost_estimate=pl.CostEstimate(
            flops=4 * rows * model * hidden, bytes_accessed=12 * rows * model, transcendentals=0
        ),
        name="feed_grads",
    )(*arrays)


def feed_grads_first_kernel(
    active_ref, grad_hidden_ref, g0, g1, g2, g3, x0, x1, x2, x3, first_ref, second_ref,
    total_ref, right_ref,
):
    each = total_ref.shape[0] // 2
    cut = first_ref.shape[0]
    step = pl.program_id(0)
    for left_ref, refs, part in (
        (active_ref, (g0, g1, g2, g3), 0), (grad_hidden_ref, (x0, x1, x2, x3), 1)
    ):
        rows_from(refs, right_ref)
        rows = dot(left_ref[...], right_ref[...], 0, 0)[:each]
        at = slice(part * each, (part + 1) * each)

        @pl.when(step == 0)
        def _():
            total_ref[at, :] = rows

        @pl.when(step > 0)
        def _():
            total_ref[at, :] += rows

    @pl.when(step == pl.num_programs(0) - 1)
    def _():
        first_ref[...] = total_ref[:cut, :].astype(BF)
        second_ref[...] = total_ref[cut:, :].astype(BF)


def feed_grads_first(active, grad_hidden, grad, x):
    rows, hidden = active.shape
    micro, own, model = grad[0].shape
    group = 4 * own
    block = (hidden // 4, model)
    left = pl.BlockSpec((group, 256), lambda i: (i, 0))
    return pl.pallas_call(
        feed_grads_first_kernel,
        grid=(micro,),
        in_specs=[left] * 2 + [per((own, model))] * 8,
        out_specs=[full((BACK_CUT, model)), full((block[0] - BACK_CUT, model))],
        out_shape=[shape_of(BF, BACK_CUT, model), shape_of(BF, block[0] - BACK_CUT, model)],
        scratch_shapes=[pltpu.VMEM(block, F32), pltpu.VMEM((group, model), BF)],
        compiler_params=params(56),
        cost_estimate=pl.CostEstimate(
            flops=rows * model * hidden // 2, bytes_accessed=8 * rows * model, transcendentals=0
        ),
        name="feed_grads_first",
    )(active, grad_hidden, *grad, *x)


def middle_pull_kernel(
    out_ref, middle_ref, keep_ref, arrived_ref, across_ref, vec_ref, grad_ref, branch_ref, sum_ref
):
    rows = out_ref.shape[1]
    back = keep_ref[0] + arrived_ref[0, :rows, :].astype(F32) + across_ref[0].astype(F32)
    hat, scale = norm_stats(middle_ref[0])
    out = out_ref[0].astype(F32)
    grad = out + norm_pull(back, hat, scale, vec_ref[5:6, :])
    grad_ref[0] = grad
    branch = grad.astype(BF)
    branch_ref[0] = branch

    @pl.when(pl.program_id(0) == 0)
    def _():
        sum_ref[...] = jnp.zeros_like(sum_ref)

    for i, terms in enumerate((branch.astype(F32), back * hat, back, out)):
        sum_ref[i : i + 1, :] += jnp.sum(terms, axis=0, keepdims=True)


def middle_pull(out, middle, keep, arrived, across, vec):
    micro, rows, model = out.shape
    one = per((rows, model))
    return pl.pallas_call(
        middle_pull_kernel,
        grid=(micro,),
        in_specs=[one, one, one, per((2 * rows, model)), one, whole(vec)],
        out_specs=[one, one, full((4, model))],
        out_shape=[
            shape_of(F32, micro, rows, model), shape_of(BF, micro, rows, model),
            shape_of(F32, 4, model),
        ],
        name="middle_pull",
    )(out, middle, keep, arrived, across, vec)


def attend_pull_kernel(
    place_ref, g0, g1, g2, g3, n0, n1, n2, n3, m0, m1, m2, m3, row_ref,
    qkv_ref, log_ref, heads_ref, normed_ref,
    keep_ref, other_ref, send_ref, k0, k1, k2, k3, s0, s1, s2, s3, bias_ref,
    grad_ref, grad_qkv_ref, total_ref, sum_ref, weight_ref, mask_ref,
):
    width = heads_ref.shape[2]
    count = width // HEAD_DIM
    rows = g0.shape[1]
    model = g0.shape[2]
    scale = HEAD_DIM ** (-0.5)
    step = pl.program_id(0)

    @pl.when(step == 0)
    def _():
        assemble(place_ref, (n0, n1, n2, n3), (m0, m1, m2, m3), weight_ref)

    write_mask(row_ref, mask_ref)
    for i, block_ref in enumerate((g0, g1, g2, g3)):
        grad_ref[i * rows : (i + 1) * rows, :] = block_ref[0]
    grad_heads = dot(grad_ref[...], weight_ref[3 * width :, :], 1, 1).astype(BF)
    for head in range(count):
        lanes = [slice(i * width + head * HEAD_DIM, i * width + (head + 1) * HEAD_DIM) for i in range(3)]
        queries, keys, values = [qkv_ref[0, :, part] for part in lanes]
        scores = dot(keys, queries * jnp.asarray(scale, BF), 1, 1) + mask_ref[...]
        probs = jnp.exp(scores - log_ref[0, head : head + 1, :])
        grad = grad_heads[:, lanes[0]]
        product = grad.astype(F32) * heads_ref[0, :, lanes[0]].astype(F32)
        delta = jnp.sum(jnp.transpose(product), axis=0, keepdims=True)
        grad_scores = (probs * (dot(values, grad, 1, 1) - delta)).astype(BF)
        grad_qkv_ref[:, lanes[0]] = jnp.transpose(scale * dot(keys, grad_scores, 0, 0)).astype(BF)
        grad_qkv_ref[:, lanes[1]] = (scale * dot(grad_scores, queries, 1, 0)).astype(BF)
        grad_qkv_ref[:, lanes[2]] = dot(probs.astype(BF), grad, 1, 0).astype(BF)
    write_halves(dot(grad_qkv_ref[...], weight_ref[: 3 * width, :], 1, 0), rows, keep_ref, other_ref, send_ref)
    qkv_part = dot(grad_qkv_ref[...], normed_ref[0], 0, 0)
    out_part = dot(heads_ref[0], grad_ref[...], 0, 0)
    sums = jnp.sum(grad_qkv_ref[...].astype(F32), axis=0, keepdims=True)

    @pl.when(step == 0)
    def _():
        total_ref[: 3 * width, :] = qkv_part
        total_ref[3 * width :, :] = out_part
        sum_ref[...] = jnp.broadcast_to(sums, sum_ref.shape)

    @pl.when(step > 0)
    def _():
        total_ref[: 3 * width, :] += qkv_part
        total_ref[3 * width :, :] += out_part
        sum_ref[...] += sums

    @pl.when(step == pl.num_programs(0) - 1)
    def _():
        z, y, ctx = place_ref[0], place_ref[1], place_ref[2]
        for k, pair in zip(SHIFTS, ((k0, s0), (k1, s1), (k2, s2), (k3, s3))):
            region = lax.rem(z + 4 - k, 4) * width
            for out_ref, half in zip(pair, (y, 1 - y)):
                start = pl.multiple_of(region + BODY * half, HEAD_DIM)
                out_ref[:BODY, :] = total_ref[pl.ds(start, BODY), :].astype(BF)
                start = pl.multiple_of(region + 2 * BODY + HALO * half, HALO)
                out_ref[BODY:, :] = total_ref[pl.ds(start, HALO), :].astype(BF)
        own = head_places((width, model), 0, ctx)
        hot = (lax.broadcasted_iota(jnp.int32, (width, model), 1) == own).astype(F32)
        for i, part in enumerate((0, 2)):
            line = lax.dot_general(
                sum_ref[:, part * width : (part + 1) * width],
                hot,
                (((1,), (0,)), ((), ())),
                preferred_element_type=F32,
                precision=lax.Precision.HIGHEST,
            )
            bias_ref[i : i + 1, :] = line[0:1]


def attend_pull(place, grads, near, side, row, qkv, log_total, heads, normed):
    micro, rows, model = grads[0].shape
    group = 4 * rows
    width = heads.shape[2]
    count = width // HEAD_DIM
    block = (BODY + HALO, model)
    one = per((rows, model))
    return pl.pallas_call(
        attend_pull_kernel,
        grid=(micro,),
        in_specs=[SCALARS] + [one] * 4 + [whole(b) for b in near + side] + [
            per(row.shape[1:]), per((group, 3 * width)), per((8, group)),
            per((group, width)), per((group, model)),
        ],
        out_specs=[one, one, per((2 * rows, model))] + [full(block)] * 8 + [full((2, model))],
        out_shape=[
            shape_of(F32, micro, rows, model), shape_of(BF, micro, rows, model),
            shape_of(BF, micro, 2 * rows, model),
        ] + [shape_of(BF, *block)] * 8 + [shape_of(F32, 2, model)],
        scratch_shapes=[
            pltpu.VMEM((group, model), BF), pltpu.VMEM((group, 3 * width), BF),
            pltpu.VMEM((4 * width, model), F32), pltpu.VMEM((8, 3 * width), F32),
            pltpu.VMEM((4 * width, model), BF), pltpu.VMEM((group, group), F32),
        ],
        compiler_params=params(60),
        cost_estimate=pl.CostEstimate(
            flops=2 * micro * group * model * 10 * width,
            bytes_accessed=12 * micro * group * model,
            transcendentals=micro * count * group * group,
        ),
        name="attend_pull",
    )(place, *grads, *near, *side, row, qkv, log_total, heads, normed)


def input_pull_kernel(
    x_ref, grad_ref, keep_ref, arrived_ref, across_ref, vec_ref, out_ref, sum_ref
):
    rows = x_ref.shape[1]
    back = keep_ref[0] + arrived_ref[0, :rows, :].astype(F32) + across_ref[0].astype(F32)
    hat, scale = norm_stats(x_ref[0].astype(F32))
    out = grad_ref[0] + norm_pull(back, hat, scale, vec_ref[0:1, :])
    out_ref[0] = jnp.transpose(out).astype(BF)

    @pl.when(pl.program_id(0) == 0)
    def _():
        sum_ref[...] = jnp.zeros_like(sum_ref)

    for i, terms in enumerate((back * hat, back)):
        sum_ref[i : i + 1, :] += jnp.sum(terms, axis=0, keepdims=True)


def input_pull(x, grad, keep, arrived, across, vec):
    micro, rows, model = x.shape
    one = per((rows, model))
    out, sums = pl.pallas_call(
        input_pull_kernel,
        grid=(micro,),
        in_specs=[one, one, one, per((2 * rows, model)), one, whole(vec)],
        out_specs=[per((model, rows)), full((2, model))],
        out_shape=[shape_of(BF, micro, model, rows), shape_of(F32, 2, model)],
        name="input_pull",
    )(x, grad, keep, arrived, across, vec)
    return out.transpose(0, 2, 1), sums


def mixed_kernel(middle_ref, keep_ref, arrived_ref, across_ref, vec_ref, out_ref):
    rows = middle_ref.shape[1]
    feed = keep_ref[0] + arrived_ref[0, :rows, :].astype(F32) + across_ref[0].astype(F32)
    out_ref[0] = jnp.transpose(middle_ref[0] + feed + vec_ref[7:8, :]).astype(BF)


def mixed_rows(middle, keep, arrived, across, vec):
    micro, rows, model = middle.shape
    one = per((rows, model))
    return pl.pallas_call(
        mixed_kernel,
        grid=(micro,),
        in_specs=[one, one, per((2 * rows, model)), one, whole(vec)],
        out_specs=per((model, rows)),
        out_shape=shape_of(BF, micro, model, rows),
        name="mixed_rows",
    )(middle, keep, arrived, across, vec).transpose(0, 2, 1)


def row_places(segments, rows):
    ctx = lax.axis_index("ctx")
    ranks = [ctx ^ j for j in BLOCKS]
    starts = segments[:, 0].reshape(-1, 4, rows).transpose(1, 0, 2)
    starts = jnp.concatenate([pick(starts, r) for r in ranks], axis=1)
    places = jnp.concatenate([r * rows + jnp.arange(rows, dtype=jnp.int32) for r in ranks])
    places = jnp.broadcast_to(places[None], starts.shape)
    return jnp.stack([starts, places] + [places] * 6, axis=1)


def own_up_bias(lines, order, width):
    table = lines[16:].reshape(order.shape[0], 4, width).transpose(1, 0, 2)
    return reorder(pick(table, lax.axis_index("ctx")), order).reshape(1, -1)


def vector_parts(first_sums, bias_sums, sums, up_sum, order, width):
    up_rows = reorder_back(up_sum.reshape(order.shape[0], width), order)
    mine = (jnp.arange(4) == lax.axis_index("ctx")).astype(F32)
    table = jnp.concatenate([first_sums, bias_sums, sums], axis=0)
    up_part = (up_rows[:, None, :] * mine[None, :, None]).reshape(-1)
    return jnp.concatenate([table.reshape(-1), up_part])


def flat(values):
    return values.reshape(-1, values.shape[-1])


def halo_pairs(back):
    pairs = []
    for p in range(8):
        for c in range(4):
            to = (c - 1) % 4 if (p % 2 == 1) != back else (c + 1) % 4
            pairs.append((p * 4 + c, p * 4 + to))
    return pairs


def aligned_block(w_attn, vectors, odd, ctx):
    turned = row_major(w_attn.T)
    width, model = turned.shape
    table = ctx_table(vectors, ctx).astype(BF).reshape(3, model // 2)
    edge = jnp.where(odd, turned[:HALO], turned[width - HALO :])
    halo = lax.ppermute(edge, BOTH, halo_pairs(False))
    none = jnp.zeros_like(halo)
    wide = jnp.concatenate(
        [jnp.where(odd, none, halo), turned, jnp.where(odd, halo, none)], axis=0
    )
    shift = HALO * odd.astype(jnp.int32)
    body = lax.dynamic_slice_in_dim(wide, HALO - 8 * ctx + shift, BODY, axis=0)
    extra = lax.dynamic_slice_in_dim(wide, width + shift, HALO, axis=0)
    extra = jnp.where(ctx == 3, extra, jnp.zeros_like(extra))
    lines = jnp.pad(table, ((0, 13), (0, model // 2)))
    return jnp.concatenate([body, extra, lines], axis=0)


def aligned_owned(own, odd, ctx, width):
    last = ctx == 3
    body, extra = own[:BODY], own[BODY:]
    tail = jnp.where(last, extra, body[BODY - HALO :])
    halo = lax.ppermute(jnp.where(odd, tail, body[:HALO]), BOTH, halo_pairs(True))
    halo = jnp.where(last & jnp.logical_not(odd), extra, halo)
    wide = jnp.where(
        odd, jnp.concatenate([halo, body], axis=0), jnp.concatenate([body, halo], axis=0)
    )
    return lax.dynamic_slice_in_dim(wide, 8 * ctx, width, axis=0)


def vector_rows(part, ctx):
    table = part.reshape(8, 4, -1).transpose(1, 0, 2)
    mine = jnp.stack([pick(table, ctx ^ j) for j in (0, 1)])
    far = jnp.stack([pick(table, ctx ^ j) for j in (2, 3)])
    mine = mine + lax.ppermute(far, "ctx", CHIP_PAIRS)
    return mine[0] + lax.ppermute(mine[1], "ctx", CORE_PAIRS)


def vector_sides(mine, y):
    sides = mine.reshape(4, 2, -1).transpose(1, 0, 2)
    return pick(sides, y) + lax.ppermute(pick(sides, 1 - y), "dp", SIDE_PAIRS)


def vector_owned(mine, z):
    total = pick(mine, z)
    for k in (1, 2, 3):
        total = total + to_shift(pick(mine, (z - k) % 4)[None], k, True)[0]
    return total


def both(keep, arrived):
    return keep.astype(F32) + arrived.astype(F32)


def aligned(tokens, cotangent, w_attn, w_up, w_down, vectors, segments):
    rows = tokens.shape[1]
    width = w_attn.shape[1]
    ctx, dp = lax.axis_index("ctx"), lax.axis_index("dp")
    z, y = dp // 2, dp % 2
    odd = y == 1
    place = jnp.stack([z, y, ctx]).astype(jnp.int32)
    order = jnp.stack(dp_order(z, y))
    tokens, cotangent = row_major(tokens), row_major(cotangent)
    row_info = row_places(segments, rows)
    feed = jnp.concatenate([w_down, w_up.T], axis=0)

    n0 = aligned_block(w_attn, vectors, odd, ctx)
    n0, t0, place, row_info, b0 = hold([n0, tokens, place, row_info, feed])
    n1, n3, s0, t1, c0 = (
        to_shift(n0, 1), to_shift(n0, 3), to_side(n0), to_chip(t0), to_side(b0[:CUT])
    )
    n0, n1, n3, s0, t0, t1, g0, b0, c0 = hold([n0, n1, n3, s0, t0, t1, cotangent, b0, c0])
    n2, s1, s3, g1 = to_shift(n0, 2), to_side(n1), to_side(n3), to_chip(g0)
    n0, n1, n2, n3, s0, s1, s3, t0, t1, g0, g1, b0 = hold(
        [n0, n1, n2, n3, s0, s1, s3, t0, t1, g0, g1, b0]
    )
    s2, b1, t2, t3 = to_side(n2), to_shift(b0, 1), to_core(t0), to_core(t1)
    n0, n1, n2, n3, s0, s1, s2, s3, t0, t1, t2, t3, g0, g1, b0, b1 = hold(
        [n0, n1, n2, n3, s0, s1, s2, s3, t0, t1, t2, t3, g0, g1, b0, b1]
    )
    b3, b2, c1, d0 = (
        to_shift(b0, 3), to_shift(b0[: THIRDS[0]], 2), to_side(b1), to_side(b0[CUT:])
    )
    normed_one, qkv, log_total, heads, lines, rest, keep, other, away = attend(
        place, [t0, t1, t2, t3], [n0, n1, n3, n2], [s0, s1, s3, s2], row_info
    )
    away, keep, other, b0, b1, b2, b3, c1, d0, g0, g1 = hold(
        [away, keep, other, b0, b1, b2, b3, c1, d0, g0, g1]
    )
    arrived = to_core(away)
    away, arrived, keep, b0, b2, b3, g0, g1 = hold(
        [half_sum(other, arrived), arrived, keep, b0, b2, b3, g0, g1]
    )
    across, d2, c3 = to_chip(away), to_shift(b0[THIRDS[0] : THIRDS[1]], 2), to_side(b3)
    g2, g3 = to_core(g0), to_core(g1)
    across, arrived, keep, b0, d2, c3, b2, g2, g3 = hold(
        [across, arrived, keep, b0, d2, c3, b2, g2, g3]
    )
    middle, h0 = middle_rows(tokens, keep, arrived, across, lines)
    h0, middle, b0, d2, b2 = hold([h0, middle, b0, d2, b2])
    h1, e2, f2, c2 = to_chip(h0), to_shift(b0[THIRDS[1] :], 2), to_side(d2), to_side(b2)
    up_bias = own_up_bias(rest, order, width)
    h0, h1, e2, f2, c2, up_bias = hold([h0, h1, e2, f2, c2, up_bias])
    h2, h3, a2 = to_core(h0), to_core(h1), to_side(e2)
    blocks = [[c2, f2, a2], [b2, d2, e2], [b0], [c0, d0], [b1], [c1], [b3], [c3]]
    pull = feed_pull([g0, g1, g2, g3], blocks)
    h0, h1, h2, h3, pull = hold([h0, h1, h2, h3, pull], a2)
    active, grad_hidden, keep, other, away, up_sum = feed_forward(
        [h0, h1, h2, h3], pull, blocks, up_bias
    )
    x_all, grad_all = [h0, h1, h2, h3], [g0, g1, g2, g3]

    arrived = to_core(away)
    q2, v2 = feed_grads_first(flat(active), flat(grad_hidden), grad_all, x_all)
    away, arrived, keep, active, q2, v2 = hold(
        [half_sum(other, arrived), arrived, keep, active, q2, v2]
    )
    across, q2, v2 = to_chip(away), to_side(q2), to_side(v2)
    p2, p0, q0, p1, q1, p3, q3 = feed_grads(flat(active), flat(grad_hidden), grad_all, x_all)
    across, arrived, keep, p2, q2, v2 = hold([across, arrived, keep, p2, q2, v2])
    grad_middle, h0, sums = middle_pull(cotangent, middle, keep, arrived, across, lines)
    h0, q2, p2, v2, q3, grad_middle, active = hold(
        [h0, both(p2[:BACK_CUT], q2).astype(BF), p2, v2, q3, grad_middle, active]
    )
    h1, h2, r2, q3 = to_chip(h0), to_core(h0), to_shift(q2, 2, True), to_side(q3)
    p2 = both(p2[BACK_CUT:], v2).astype(BF)
    feed_keep, feed_other, feed_away = feed_out(active, blocks)
    h0, h1, h2, r2, q3, p2, feed_away = hold([h0, h1, h2, r2, q3, p2, feed_away])
    h3, feed_arrived = to_core(h1), to_core(feed_away)
    h0, h1, h2, h3, p2, p3, q1, q0, feed_arrived = hold(
        [h0, h1, h2, h3, p2, both(p3, q3).astype(BF), q1, q0, feed_arrived]
    )
    t2, r3 = to_shift(p2, 2, True), to_shift(p3, 3, True)
    q1, q0 = to_side(q1), to_side(q0)
    keep, other, away, *parts, bias_sums = attend_pull(
        place, [h0, h1, h2, h3], [n0, n1, n3, n2], [s0, s1, s3, s2], row_info,
        qkv, log_total, heads, normed_one,
    )
    away, t2, r3, q1, q0, p0, p1, *parts = hold([away, t2, r3, q1, q0, p0, p1] + parts)
    k0, k1, k3, k2, l0, l1, l3, l2 = parts
    arrived = to_core(away)
    away, arrived, keep, p1, l1, l2, l3 = hold(
        [half_sum(other, arrived), arrived, keep, both(p1, q1).astype(BF), l1, l2, l3]
    )
    r1, across, l2, l1 = to_shift(p1, 1, True), to_chip(away), to_side(l2), to_side(l1)
    across, arrived, keep, r1, k1, k2, l0, l3, feed_away = hold(
        [
            across, arrived, keep, r1, both(k1, l1).astype(BF), both(k2, l2).astype(BF),
            l0, l3, half_sum(feed_other, feed_arrived),
        ]
    )
    k2, k1, l3, l0, feed_across = (
        to_shift(k2, 2, True), to_shift(k1, 1, True), to_side(l3), to_side(l0),
        to_chip(feed_away),
    )
    input_grad, first_sums = input_pull(tokens, grad_middle, keep, arrived, across, lines)
    part = vector_parts(first_sums, bias_sums, sums, up_sum, order, width)
    k1, k2, k3, l0, part, feed_across, input_grad = hold(
        [k1, k2, both(k3, l3).astype(BF), l0, part, feed_across, input_grad]
    )
    k3, part = to_shift(k3, 3, True), vector_rows(part, ctx)
    k1, k2, k3, part = hold([k1, k2, k3, part])
    own = both(k0, l0) + k1.astype(F32) + k2.astype(F32) + k3.astype(F32)
    attn_owned = aligned_owned(own, odd, ctx, width).T
    part = vector_sides(part, y)
    mixed = mixed_rows(middle, feed_keep, feed_arrived, feed_across, lines)
    terms = [p0, q0, r1, jnp.concatenate([r2, t2], axis=0), r3]
    down_owned = sum(t[:width].astype(F32) for t in terms)
    up_owned = sum(t[width:].astype(F32) for t in terms).T
    part, mixed, down_owned, up_owned = hold([part, mixed, down_owned, up_owned])
    return mixed, input_grad, attn_owned, up_owned, down_owned, vector_owned(part, z)


def plain(tokens, cotangent, w_attn, w_up, w_down, vectors, segments):
    micro, rows, model = tokens.shape
    width = w_attn.shape[1]
    ctx = lax.axis_index("ctx")
    last = ctx == lax.axis_size("ctx") - 1
    place = jnp.stack([jnp.zeros((), ctx.dtype), jnp.zeros((), ctx.dtype), ctx])
    order = jnp.arange(lax.axis_size("dp"))
    table = lax.all_gather(w_attn.T, BOTH, axis=0, tiled=True)
    lines = lax.all_gather(vectors, BOTH, axis=0, tiled=True).reshape(24, model // 2)
    lines = jnp.pad(lines, ((0, 0), (0, model // 2)))
    near, side = [], []
    for region in (-k % 4 for k in SHIFTS):
        part = head_rows(table[region * model : (region + 1) * model], ctx, last)
        for blocks, half in ((near, 0), (side, 1)):
            line = 3 * (2 * region + half)
            blocks.append(
                jnp.concatenate(
                    [
                        part[BODY * half : BODY * (half + 1)],
                        part[2 * BODY + HALO * half : 2 * BODY + HALO * (half + 1)],
                        jnp.pad(lines[line : line + 3], ((0, 13), (0, 0))),
                    ],
                    axis=0,
                )
            )
    up = lax.all_gather(w_up.T, "dp", axis=0, tiled=True)
    down = lax.all_gather(w_down, "dp", axis=0, tiled=True)
    each = up.shape[0] // 8
    blocks = [
        jnp.concatenate([w[i * each : (i + 1) * each] for w in (down, up)], axis=0)
        for i in range(8)
    ]
    blocks = [[b] for b in blocks]
    row_info = row_places(segments, rows)

    normed_one, qkv, log_total, heads, lines, rest, *halves = attend(
        place, row_gather(tokens), near, side, row_info
    )
    middle, normed_two = middle_rows(tokens, *row_scatter(*halves), lines)
    x_all, grad_all = row_gather(normed_two), row_gather(cotangent)
    active, grad_hidden, *halves, up_sum = feed_forward(
        x_all, feed_pull(grad_all, blocks), blocks, own_up_bias(rest, order, width)
    )
    mixed = mixed_rows(middle, *row_scatter(*feed_out(active, blocks)), lines)
    grad_middle, branch, sums = middle_pull(cotangent, middle, *row_scatter(*halves), lines)
    arrays = flat(active), flat(grad_hidden), grad_all, x_all
    parts = [jnp.concatenate(feed_grads_first(*arrays), axis=0)] + list(feed_grads(*arrays))
    down_owned, up_owned = [
        lax.psum_scatter(
            jnp.concatenate([p[i * each : (i + 1) * each] for p in parts], axis=0),
            "dp", scatter_dimension=0, tiled=True,
        ).astype(F32)
        for i in range(2)
    ]
    *halves, k0, k1, k2, k3, s0, s1, s2, s3, bias_sums = attend_pull(
        place, row_gather(branch), near, side, row_info, qkv, log_total, heads, normed_one
    )
    input_grad, first_sums = input_pull(tokens, grad_middle, *row_scatter(*halves), lines)
    parts = []
    for region in range(4):
        at = SHIFTS.index(-region % 4)
        first, second = (k0, k1, k2, k3)[at], (s0, s1, s2, s3)[at]
        part = [first[:BODY], second[:BODY], first[BODY:], second[BODY:]]
        parts.append(head_rows_back(jnp.concatenate(part, axis=0), ctx, last))
    attn_owned = lax.psum_scatter(
        jnp.concatenate(parts, axis=0), BOTH, scatter_dimension=0, tiled=True
    ).astype(F32)
    part = vector_parts(first_sums, bias_sums, sums, up_sum, order, width)
    vector_grad = lax.psum_scatter(part, BOTH, scatter_dimension=0, tiled=True)
    return (mixed, input_grad, attn_owned.T, up_owned.T, down_owned, vector_grad)


def shards(*arrays):
    fits = lax.axis_size("dp") == 8 and lax.axis_size("ctx") == 4
    return (aligned if fits and arrays[2].shape == (1088, 136) else plain)(*arrays)


def solution(mesh):
    return jax.shard_map(
        shards,
        mesh=mesh,
        in_specs=(
            P(None, BOTH, None),
            P(None, BOTH, None),
            P(None, BOTH),
            P(None, BOTH),
            P(BOTH, None),
            P(BOTH),
            P(None, "dp", None),
        ),
        out_specs=(
            P(None, BOTH, None),
            P(None, BOTH, None),
            P(None, BOTH),
            P(None, BOTH),
            P(BOTH, None),
            P(BOTH),
        ),
        check_vma=False,
    )
```
